32 devices in a mesh: ind: 8 (over y, x, core), bin: 4 (over z).
Axes of the slice: x: 2, y: 2, z: 4, core: 2. Of those that a mesh axis runs over, the one named last changes fastest.
Arguments:
- genotype: int32 [2048, 102400], P('ind', 'bin'), may hold values from 0 to 2
- snp_mean: float32 [102400], P('bin'), may hold values from 0.9 to 1.1
- snp_scale: float32 [102400], P('bin'), may hold values from 0.75 to 0.9
- snp_label: int32 [102400], P('bin'), may hold values from 0 to 23, as said below
- probe_bits: int32 [10, 2048], P(None, 'ind'), may hold values from 0 to 1
- phenotype: bfloat16 [2048], P('ind'), may hold values from -6 to 6
Outputs:
- field: bfloat16 [24, 10, 2048], P('bin', None, 'ind')
- pair: float32 [24, 24], P('bin')
- trace: float32 [24], P('bin')
- quadratic: float32 [24], P('bin')
The draws below stay inside these ranges and needn't reach their ends.
Inputs may be any that keep to these rules, and one draw needn't show every extreme that they name: `snp_label`: the label of SNP m lies from (m // 25600) * 6 to (m // 25600) * 6 + 5, and every bin holds at least one SNP.
All inputs are finite; a program needn't handle non-finite values.
Results may differ from the reference program's by a relative error of at most 0.0053.
Values may be sent and summed in bfloat16 or wider, within the bound.
No kernel may reach another device: no remote copies, remote signals or barrier semaphores. Data moves between devices by JAX's collectives and lax.ppermute only.
A program may use at most 128 MiB of HBM per device.

```python
import jax
import jax.numpy as jnp
from jax import lax

BINS = 24
PROBES = 10
SNP_DEV = 25600
BINS_DEV = 6
INDIVIDUALS = 2048
SNPS = 102400
N_BIN = 4


def draw_snp_label(key, part):
    key = jax.random.fold_in(key, 7)
    key_local, key_offset = jax.random.split(key)
    local = jax.random.randint(key_local, (N_BIN, SNP_DEV), 0, BINS_DEV).astype(jnp.int32)
    offset = jax.random.randint(key_offset, (N_BIN, 1), 0, SNP_DEV - BINS_DEV + 1).astype(jnp.int32)
    place = jnp.arange(SNP_DEV, dtype=jnp.int32)[None, :] - offset
    local = jnp.where((place >= 0) & (place < BINS_DEV), place, local)
    labels = local + jnp.arange(N_BIN, dtype=jnp.int32)[:, None] * BINS_DEV
    return labels.reshape(SNPS).astype(jnp.int32)


def set_ends(result, rng, low, largest):
    longest = result.shape.index(max(result.shape))
    spots = []
    for shift in (0, 1):
        where = [jax.random.randint(jax.random.fold_in(rng, axis), (), 0, length) for axis, length in enumerate(result.shape)]
        where[longest] = (where[longest] + shift) % result.shape[longest]
        spots.append(tuple(where))
    return result.at[spots[0]].set(low).at[spots[1]].set(largest)


def shard_levels(key, extent, cuts, smallest, top_value):
    factor_of = 1.0
    for axis_at, blocks in cuts:
        steps = jax.random.uniform(jax.random.fold_in(jax.random.fold_in(key, 6), axis_at), (blocks,), jnp.float32, smallest / len(cuts), top_value / len(cuts))
        factor_of = factor_of * jnp.repeat(jnp.exp(steps), extent[axis_at] // blocks).reshape((-1,) + (1,) * (len(extent) - 1 - axis_at))
    return factor_of


def centred(key, shape, width, most, pieces=(), kind=jnp.bfloat16):
    array = jax.random.normal(key, shape, jnp.float32) * width
    if len(pieces) > 0:
        array = shard_levels(key, shape, pieces, -0.22, 0.18) * array
    return jnp.clip(array, min=-most, max=most).astype(kind)


def setup_inputs(seed: int = 0) -> dict:
    seeds = jax.random.split(jax.random.key(seed), 7)
    genotype = set_ends(jax.random.randint(seeds[0], (INDIVIDUALS, SNPS), 0, 3), jax.random.fold_in(seeds[0], 1), 0, 2).astype(jnp.int32)
    snp_mean = jnp.clip(0.9 + 0.20000005 * jax.random.uniform(seeds[1], (SNPS,), jnp.float32) ** shard_levels(seeds[1], (SNPS,), ((0, 4),), -0.2, 0.2), 0.9, 1.1)
    snp_scale = jnp.clip(0.75 + 0.14999998 * jax.random.uniform(seeds[2], (SNPS,), jnp.float32) ** shard_levels(seeds[2], (SNPS,), ((0, 4),), -0.2, 0.2), 0.75, 0.9)
    snp_label = draw_snp_label(jax.random.fold_in(seeds[6], 71), 0)
    probe_bits = set_ends(jax.random.randint(seeds[4], (PROBES, INDIVIDUALS), 0, 2), jax.random.fold_in(seeds[4], 1), 0, 1).astype(jnp.int32)
    phenotype = centred(seeds[5], (INDIVIDUALS,), 1.0, 6.0, ((0, 8),))
    return dict(genotype=genotype, snp_mean=snp_mean, snp_scale=snp_scale, snp_label=snp_label, probe_bits=probe_bits, phenotype=phenotype)


def standardize(geno, mean, scale):
    return ((geno.astype(jnp.float32) - mean[None, :]) / scale[None, :]).astype(jnp.bfloat16)


def reference(genotype, snp_mean, snp_scale, snp_label, probe_bits, phenotype):
    probes = (2 * probe_bits - 1).astype(jnp.bfloat16)
    left = jnp.concatenate([probes, phenotype[None, :]], axis=0)
    left_wide = left.astype(jnp.float32)
    member = snp_label[None, :] == jnp.arange(BINS, dtype=jnp.int32)[:, None]
    count = jnp.sum(member.astype(jnp.float32), axis=1)

    def first_pass(block, carry):
        moments, squares = carry
        start = (block * SNP_DEV).astype(jnp.int32)
        geno = lax.dynamic_slice_in_dim(genotype, start, SNP_DEV, 1)
        mean = lax.dynamic_slice_in_dim(snp_mean, start, SNP_DEV, 0)
        scale = lax.dynamic_slice_in_dim(snp_scale, start, SNP_DEV, 0)
        stand = standardize(geno, mean, scale).astype(jnp.float32)
        part = jnp.dot(left_wide, stand, precision=lax.Precision.HIGHEST)
        moments = lax.dynamic_update_slice_in_dim(moments, part, start, 1)
        squares = lax.dynamic_update_slice_in_dim(squares, jnp.sum(stand * stand, axis=0), start, 0)
        return moments, squares

    moments0 = jnp.zeros((PROBES + 1, SNPS), jnp.float32)
    squares0 = jnp.zeros((SNPS,), jnp.float32)
    moments, squares = lax.fori_loop(0, N_BIN, first_pass, (moments0, squares0))
    weights = lax.optimization_barrier(moments[:PROBES].astype(jnp.bfloat16)).astype(jnp.float32)

    def second_pass(block, hidden):
        start = (block * SNP_DEV).astype(jnp.int32)
        geno = lax.dynamic_slice_in_dim(genotype, start, SNP_DEV, 1)
        mean = lax.dynamic_slice_in_dim(snp_mean, start, SNP_DEV, 0)
        scale = lax.dynamic_slice_in_dim(snp_scale, start, SNP_DEV, 0)
        stand = standardize(geno, mean, scale).astype(jnp.float32)
        mask = lax.dynamic_slice_in_dim(member, start, SNP_DEV, 1)
        wblock = lax.dynamic_slice_in_dim(weights, start, SNP_DEV, 1)
        expanded = jnp.where(mask[:, None, :], wblock[None, :, :], jnp.zeros((), jnp.float32))
        expanded = expanded.reshape(BINS * PROBES, SNP_DEV)
        return hidden + jnp.dot(expanded, stand.T, precision=lax.Precision.HIGHEST)

    hidden0 = jnp.zeros((BINS * PROBES, INDIVIDUALS), jnp.float32)
    hidden = lax.fori_loop(0, N_BIN, second_pass, hidden0)
    field = (hidden.reshape(BINS, PROBES, INDIVIDUALS) / count[:, None, None]).astype(jnp.bfloat16)
    flat = lax.optimization_barrier(field).astype(jnp.float32).reshape(BINS, PROBES * INDIVIDUALS)
    pair = jnp.dot(flat, flat.T, precision=lax.Precision.HIGHEST) / (PROBES * INDIVIDUALS)
    trace = jnp.sum(jnp.where(member, squares[None, :], jnp.zeros((), jnp.float32)), axis=1) / (count * INDIVIDUALS)
    trait = moments[PROBES]
    quadratic = jnp.sum(jnp.where(member, (trait * trait)[None, :], jnp.zeros((), jnp.float32)), axis=1) / (count * INDIVIDUALS)
    return field, pair, trace, quadratic
```

```python
import functools

import jax
import jax.numpy as jnp
from jax import lax
from jax.experimental import pallas as pl
from jax.experimental.pallas import tpu as pltpu
from jax.sharding import PartitionSpec as P

BINS = 24
PROBES = 10
LANES = 128
SUBLANES = 8
ROWS = 16
TRAIT, ONES = PROBES, PROBES + 1
TRACE_LANE, QUAD_LANE = LANES - 2, LANES - 1
PIECE = 640
DOT_PIECE = 768
F32 = jnp.float32
BF16 = jnp.bfloat16
VMEM = pltpu.VMEM
MIB = 1 << 20


def core():
    return lax.rem(lax.axis_index("ind"), 2)


def fold_lanes(value):
    return tree_sum([value[:, at : at + LANES] for at in range(0, value.shape[1], LANES)])


def rows_iota(count, width=1):
    return lax.broadcasted_iota(jnp.int32, (count, width), 0)


def tree_sum(terms):
    terms = list(terms)
    while len(terms) > 1:
        pairs = [a + b for a, b in zip(terms[::2], terms[1::2])]
        terms = pairs + terms[len(pairs) * 2 :]
    return terms[0]


def pack_sums(value):
    half = value.shape[1] // 2
    low = value[SUBLANES:]
    turned = pltpu.roll(low[:, half:], 4, 0)
    low = jnp.where(rows_iota(SUBLANES) < 4, low[:, :half], turned)
    return value[:SUBLANES], low


def unpack_sums(value):
    span = value.shape[1] * 2 // 3
    low = value[:, span:]
    return value[:, :span], jnp.concatenate([low, pltpu.roll(low, 4, 0)], axis=1)


def moments_kernel(snps, distances, opening, taken, given, geno_ref, *rest):
    rest = list(rest)
    if opening:
        bits_ref, trait_ref, kept_ref, sums_ref, local_ref, left_ref = rest[:6]
        rest = rest[6:]
    else:
        raw_in = rest.pop(0) if taken else None
        left_ref, kept_ref, sums_ref, local_ref = rest[:4]
        rest = rest[4:]
    raw_out = rest.pop(0) if given is not None else None
    slots, rows, block = kept_ref.shape
    fetched = slots - taken
    devices = -(-snps // block)
    tail = snps - (devices - 1) * block
    span = sums_ref.shape[2] * 2 // 3

    def copy(distance, target, semaphore, width):
        start = pl.multiple_of((lax.axis_index("ind") ^ distance) * block, LANES)
        return pltpu.make_async_copy(
            geno_ref.at[:, pl.ds(start, width)], target.at[:, pl.ds(0, width)], semaphore
        )

    def whole_or_tail(distance, target, semaphore, act):
        if tail == block:
            act(copy(distance, target, semaphore, block))
        else:
            last = (lax.axis_index("ind") ^ distance) == devices - 1
            pl.when(last)(lambda: act(copy(distance, target, semaphore, tail)))
            pl.when(jnp.logical_not(last))(lambda: act(copy(distance, target, semaphore, block)))

    if fetched:
        buffer, arrived = rest[:2]
        rest = rest[2:]

        def fetch(index, act):
            distance = distances[0] - 2 * (index + taken)
            whole_or_tail(distance, buffer.at[index], arrived.at[index], act)

    if raw_out is not None:
        raw_arrived = rest.pop(0)

    if opening:
        bits, trait, small = rest[:3]
        bits_copy = pltpu.make_async_copy(bits_ref, bits, small.at[0])
        trait_copy = pltpu.make_async_copy(trait_ref, trait, small.at[1])
        bits_copy.start()
        trait_copy.start()
    if fetched:
        pl.loop(0, fetched)(lambda index: fetch(index, lambda c: c.start()))
    if raw_out is not None:
        whole_or_tail(given, raw_out, raw_arrived, lambda c: c.start())
    if opening:
        bits_copy.wait()
        trait_copy.wait()
        left_ref[...] = jnp.zeros_like(left_ref)
        left_ref[0:PROBES] = (2 * bits[...] - 1).astype(F32)
        left_ref[TRAIT : TRAIT + 1] = trait[...].astype(F32).reshape(1, rows)
        left_ref[ONES : ONES + 1] = jnp.ones((1, rows), F32)
    left = left_ref[...]
    base = jnp.sum(left, axis=1, keepdims=True)
    left = left.astype(BF16)
    row = rows_iota(ROWS)

    def with_low(value):
        high = value[TRAIT : TRAIT + 1]
        return jnp.where(row == TRAIT + 1, high - high.astype(BF16).astype(F32), value)

    ends = jnp.broadcast_to(with_low(base), (ROWS, span - block))

    def work(slot, source):
        squares = []
        for at in range(0, block, PIECE):
            lanes = slice(at, min(at + PIECE, block))
            square = 0.0
            for r in range(0, rows, 16):
                dose = source[r : r + 16, lanes].astype(F32)
                kept_ref[slot, r : r + 16, lanes] = dose.astype(BF16)
                dose = dose * dose
                square = square + (dose[:8] + dose[8:])
            squares.append(jnp.sum(square, axis=0, keepdims=True))
        total = jnp.dot(left, kept_ref[slot], preferred_element_type=F32) - base
        ones = total[ONES : ONES + 1]
        local_ref[slot, 0:1] = ones
        local_ref[slot, 1:2] = jnp.concatenate(squares, axis=1) - 2.0 * ones - rows
        high, low = pack_sums(jnp.concatenate([with_low(total), ends], axis=1))
        sums_ref[slot, :, :span] = high.astype(BF16)
        sums_ref[slot, :, span:] = low.astype(BF16)

    if taken:
        work(0, raw_in)
    if fetched:

        @pl.loop(0, fetched)
        def _(index):
            fetch(index, lambda c: c.wait())
            work(index + taken, buffer.at[index])

    if raw_out is not None:
        whole_or_tail(given, raw_out, raw_arrived, lambda c: c.wait())


def cores_kernel(left_ref, here_ref, away_ref, *outs):
    outs, left_out = outs[:-1], outs[-1]
    left_out[...] = left_ref[...]
    for index, out in enumerate(outs):
        out[...] = (here_ref[index].astype(F32) + away_ref[index].astype(F32)).astype(BF16)


def relay_kernel(token_ref, value_ref, out_ref):
    out_ref[...] = value_ref[...]


def weights_kernel(mean_ref, scale_ref, own_ref, near_ref, *refs):
    parts, (u_ref, trait_ref) = refs[:-2], refs[-2:]
    block = trait_ref.shape[1]
    width = u_ref.shape[1] - block
    here = pl.ds(pl.multiple_of(lax.axis_index("ind") * block, LANES), block)
    parts = [own_ref[0], near_ref[0]] + [part[...] for part in parts]
    total = tree_sum([part.astype(F32) for part in parts])
    shift = mean_ref[:, here] - 1.0
    inverse = 1.0 / scale_ref[:, here]
    high, low = [
        (part[:, :block] - part[:, block : block + 1] * shift) * inverse
        for part in unpack_sums(total)
    ]
    trait_ref[...] = low[2:3] + low[3:4]
    high, low = [part.astype(BF16).astype(F32) * inverse for part in (high, low)]
    low = jnp.concatenate([low, jnp.zeros((SUBLANES, 4 * width - block), F32)], axis=1)
    folded = low[:, :width]
    for j in range(1, 4):
        turned = pltpu.roll(low[:, j * width : (j + 1) * width], 2 * j, 0)
        folded = jnp.where(rows_iota(SUBLANES) < 2 * j, folded, turned)
    u_ref[:, :block] = high.astype(BF16)
    u_ref[:, block:] = folded.astype(BF16)


def stats_kernel(own_bins, order, flat_ref, mean_ref, scale_ref, label_ref, trait_ref, *rest):
    locals_, (out_ref, field_ref) = rest[:-2], rest[-2:]
    block = trait_ref.shape[1]
    rows = order[0]
    bins = rows_iota(SUBLANES)

    def member_of(owner):
        here = pl.ds(pl.multiple_of(owner * block, LANES), block)
        member = label_ref[:, here] - lax.axis_index("bin") * own_bins == bins
        return here, member & (bins < own_bins)

    trace = jnp.zeros((SUBLANES, 1), F32)
    for ref, distances in zip(locals_, order[1]):
        for slot, distance in enumerate(distances):
            here, member = member_of(lax.axis_index("ind") ^ distance)
            shift = mean_ref[:, here] - 1.0
            inverse = 1.0 / scale_ref[:, here]
            square = ref[slot, 1:2] - 2.0 * shift * ref[slot, 0:1] + rows * shift * shift
            square = square * (inverse * inverse)
            trace += jnp.sum(jnp.where(member, square, 0.0), axis=1, keepdims=True)
    _, member = member_of(lax.axis_index("ind"))
    trait = trait_ref[...]
    quad = jnp.sum(jnp.where(member, trait * trait, 0.0), axis=1, keepdims=True)
    lane = lax.broadcasted_iota(jnp.int32, (SUBLANES, LANES), 1)
    out_ref[...] = jnp.where(lane == TRACE_LANE, trace, jnp.where(lane == QUAD_LANE, quad, 0.0))
    flat = flat_ref[...].astype(F32)
    for b in range(PROBES):
        field_ref[b] = flat[:own_bins, b * rows : (b + 1) * rows].astype(BF16)


def field_kernel(own_bins, blocks, sources, started, last, *refs):
    refs = list(refs)
    mean_ref, label_ref = refs[:2]
    kept_refs, refs = refs[2 : 2 + sources], refs[2 + sources :]
    u_refs, refs = refs[: len(blocks)], refs[len(blocks) :]
    rows, block = kept_refs[0].shape[1:]
    bins = rows_iota(SUBLANES)
    if started:
        acc, offset, number = [ref[...] for ref in refs[:3]]
        refs = refs[3:]
    else:
        acc = jnp.zeros((rows, PROBES * SUBLANES), F32)
        offset = jnp.zeros((PROBES * SUBLANES, LANES), F32)
        number = jnp.zeros((SUBLANES, LANES), F32)
    for index, (slot, distance) in enumerate(blocks):
        start = (lax.axis_index("ind") ^ distance) * block
        u = u_refs[index][...].astype(F32)
        lines = [u[b : b + 1, :block] for b in range(SUBLANES)]
        for b in range(PROBES - SUBLANES):
            line = [u[2 * j + b : 2 * j + b + 1, block:] for j in range(4)]
            lines.append(jnp.concatenate(line, axis=1)[:, :block])
        for at in range(0, block, DOT_PIECE):
            width = min(DOT_PIECE, block - at)
            here = pl.ds(pl.multiple_of(start + at, LANES), width)
            member = label_ref[:, here] - lax.axis_index("bin") * own_bins == bins
            member = member & (bins < own_bins)
            mean = mean_ref[:, here]
            spread = [jnp.where(member, line[:, at : at + width], 0.0) for line in lines]
            offset += jnp.concatenate([fold_lanes(value * mean) for value in spread], axis=0)
            number += fold_lanes(jnp.where(member, 1.0, 0.0))
            acc += lax.dot_general(
                kept_refs[index if sources > 1 else 0][slot, :, at : at + width],
                jnp.concatenate(spread, axis=0).astype(BF16),
                (((1,), (1,)), ((), ())),
                preferred_element_type=F32,
            )
    if not last:
        for ref, value in zip(refs, (acc, offset, number)):
            ref[...] = value
        return
    flat_ref, count_ref = refs
    acc = jnp.concatenate([acc, jnp.zeros((rows, LANES - acc.shape[1]), F32)], axis=1)
    acc = jnp.transpose(acc)[: PROBES * SUBLANES] - jnp.sum(offset, axis=1, keepdims=True)
    number = jnp.sum(number, axis=1, keepdims=True)
    count_ref[...] = jnp.broadcast_to(number, count_ref.shape)
    inverse = 1.0 / jnp.maximum(number, 1.0)
    flat = [acc[b * SUBLANES : (b + 1) * SUBLANES] * inverse for b in range(PROBES)]
    flat_ref[...] = jnp.concatenate(flat, axis=1).astype(BF16)


def pair_kernel(stats_ref, *rest):
    flats, out_ref = rest[:-1], rest[-1]
    everyone = [flat[...].astype(F32) for flat in flats]
    everyone += [jnp.zeros_like(everyone[0])] * (LANES // SUBLANES - len(flats))
    out_ref[...] = stats_ref[...] + lax.dot_general(
        flats[0][...],
        jnp.concatenate(everyone, axis=0).astype(BF16),
        (((1,), (1,)), ((), ())),
        preferred_element_type=F32,
    )


def final_kernel(own_bins, n_bin, pairs, total_rows, count_ref, own_ref, common_ref, *rest):
    mine, theirs, outs = rest[:pairs], rest[pairs : 2 * pairs + 1], rest[2 * pairs + 1 :]
    pair_ref, trace_ref, quad_ref = outs
    terms = [own_ref[...]]
    even = core() == 0
    for ref, other in zip(mine, theirs):
        terms.append(jnp.where(even, ref[...], other[...]))
        terms.append(jnp.where(even, other[...], ref[...]))
    terms.append(common_ref[...] + theirs[pairs][...])
    total = tree_sum(terms)
    row = lax.broadcasted_iota(jnp.int32, (SUBLANES, LANES), 0)
    lane = lax.broadcasted_iota(jnp.int32, (SUBLANES, LANES), 1)
    pair = jnp.zeros_like(total)
    for slot in range(n_bin):
        start = slot * SUBLANES
        part = jnp.where((lane >= start) & (lane < start + own_bins), total, 0.0)
        shift = (lax.axis_index("bin") ^ slot) * own_bins - start + LANES
        pair = pair + pltpu.roll(part, lax.rem(shift, LANES), 1)
    pair_ref[...] = pair[:own_bins, :BINS] / (PROBES * total_rows)
    scaled = total / (count_ref[...] * total_rows)
    for ref, column in ((trace_ref, TRACE_LANE), (quad_ref, QUAD_LANE)):
        turned = jnp.where(row == lane, scaled[:, column : column + 1], 0.0)
        ref[...] = jnp.sum(turned, axis=0, keepdims=True)[:, :own_bins]


def swap(value, axis, size, distance):
    return lax.ppermute(value, axis, [(i, i ^ distance) for i in range(size)])


def swap_mixed(value, size, pair):
    return lax.ppermute(value, "ind", [(i, i ^ pair[i % 2]) for i in range(size)])


def chosen_pairs(distances):
    return list(zip(distances[:-1:2], distances[1:-1:2])), distances[-1]


def in_vmem():
    return pl.BlockSpec(memory_space=VMEM)


def in_hbm():
    return pl.BlockSpec(memory_space=pltpu.HBM)


def params(mib):
    return pltpu.CompilerParams(vmem_limit_bytes=mib * MIB)


def cost(flops, moved):
    return pl.CostEstimate(flops=flops, bytes_accessed=moved, transcendentals=0)


def shards(genotype, snp_mean, snp_scale, snp_label, probe_bits, phenotype):
    n = lax.axis_size("ind")
    n_bin = lax.axis_size("bin")
    chips = n // 2
    own_bins = BINS // n_bin
    rows, snps = genotype.shape
    tiles = -(-snps // LANES)
    block_tiles = -(-tiles // n)
    block = block_tiles * LANES
    span = block + LANES * (2 - block_tiles % 2)
    folded = block + -(-block_tiles // 4) * LANES
    whole = n * block
    mean, scale, label = snp_mean, snp_scale, snp_label
    if whole != snps:
        mean = jnp.pad(mean, (0, whole - snps), constant_values=1.0)
        scale = jnp.pad(scale, (0, whole - snps), constant_values=1.0)
        label = jnp.pad(label, (0, whole - snps), constant_values=-1)
    mean, scale, label = mean[None, :], scale[None, :], label[None, :]
    genotype, probe_bits, phenotype = [
        pltpu.with_memory_space_constraint(value, pltpu.HBM)
        for value in (genotype, probe_bits, phenotype)
    ]

    def moments(distances, given, extra, name):
        slots = len(distances)
        opening = extra[0] is probe_bits
        taken = int(not opening and extra[0] is not None)
        extra = [value for value in extra if value is not None]
        fetched = slots - taken
        out_shape = [
            jax.ShapeDtypeStruct((slots, rows, block), BF16),
            jax.ShapeDtypeStruct((slots, SUBLANES, span * 3 // 2), BF16),
            jax.ShapeDtypeStruct((slots, 2, block), F32),
        ]
        if opening:
            out_shape.append(jax.ShapeDtypeStruct((ROWS, rows), F32))
        if given is not None:
            out_shape.append(jax.ShapeDtypeStruct((rows, block), jnp.int32))
        scratch = []
        if fetched:
            scratch += [VMEM((fetched, rows, block), jnp.int32), pltpu.SemaphoreType.DMA((fetched,))]
        if given is not None:
            scratch.append(pltpu.SemaphoreType.DMA)
        if opening:
            scratch += [
                VMEM(probe_bits.shape, jnp.int32),
                VMEM((rows,), BF16),
                pltpu.SemaphoreType.DMA((2,)),
            ]
        return pl.pallas_call(
            functools.partial(moments_kernel, snps, distances, opening, taken, given),
            in_specs=[in_hbm()] + [in_hbm() if opening else in_vmem()] * len(extra),
            out_specs=[in_vmem()] * len(out_shape),
            scratch_shapes=scratch,
            out_shape=out_shape,
            cost_estimate=cost(1, 4 * rows * block * slots if slots > 1 else 1),
            compiler_params=params(20),
            name=name,
        )(genotype, *extra)

    here_order = list(range(n - 2, 0, -2))
    away_order = [d + 1 for d in here_order]

    def plain(kernel, operands, out_shape, name, **options):
        return pl.pallas_call(
            kernel,
            in_specs=[in_vmem()] * len(operands),
            out_specs=[in_vmem()] * len(out_shape),
            out_shape=out_shape,
            compiler_params=params(20),
            name=name,
            **options,
        )(*operands)

    kept_away, away, local_away, left, raw = moments(
        away_order, here_order[0], (probe_bits, phenotype), "moments_away"
    )
    away = swap(away, "ind", n, 1)
    kept_here, here, local_here = moments(here_order, None, (raw, left), "moments_here")
    packed = jax.ShapeDtypeStruct((SUBLANES, span * 3 // 2), BF16)
    *sums, left = plain(
        cores_kernel,
        (left, here, away),
        [packed] * (chips - 1) + [jax.ShapeDtypeStruct(left.shape, F32)],
        "cores",
    )
    sums = [swap(value, "ind", n, d) for value, d in zip(sums, here_order)]
    kept_near, near, local_near, raw = moments([1], 0, (None, left), "moments_near")
    near = swap(near, "ind", n, 1)
    kept_own, own, local_own = moments([0], None, (raw, left), "moments_own")

    u, trait = plain(
        weights_kernel,
        (mean, scale, own, near, *sums),
        [
            jax.ShapeDtypeStruct((SUBLANES, folded), BF16),
            jax.ShapeDtypeStruct((1, block), F32),
        ],
        "weights",
    )

    number_shape = jax.ShapeDtypeStruct((SUBLANES, LANES), F32)
    term_shape = [
        jax.ShapeDtypeStruct((rows, PROBES * SUBLANES), F32),
        jax.ShapeDtypeStruct((PROBES * SUBLANES, LANES), F32),
        number_shape,
    ]
    end_shape = [jax.ShapeDtypeStruct((SUBLANES, PROBES * rows), BF16), number_shape]

    def fields(kept, blocks, us, terms, last=False):
        return plain(
            functools.partial(field_kernel, own_bins, blocks, len(kept), bool(terms), last),
            (mean, label, *kept, *us, *terms),
            end_shape if last else term_shape,
            "field",
            cost_estimate=cost(1, 1),
        )

    u_near = swap(u, "ind", n, 1)
    u_here = [swap(u, "ind", n, d) for d in here_order]
    terms = fields([kept_own, kept_near], [(0, 0), (0, 1)], [u, u_near], [])
    u_away = []
    for slot, (distance, value) in enumerate(zip(here_order, u_here)):
        shape = [jax.ShapeDtypeStruct(value.shape, value.dtype)]
        (value,) = plain(relay_kernel, (terms[2], value), shape, "relay")
        u_away.append(swap(value, "ind", n, 1))
        terms = fields([kept_here], [(slot, distance)], [value], terms)
    blocks = list(enumerate(away_order))
    middle = (chips - 1) // 2
    terms = fields([kept_away], blocks[:middle], u_away[:middle], terms)
    flat, number = fields([kept_away], blocks[middle:], u_away[middle:], terms, last=True)

    flats = [flat] + [swap(flat, "bin", n_bin, d) for d in range(1, n_bin)]
    order = (rows, (away_order, here_order, [1], [0]))
    stats, field = plain(
        functools.partial(stats_kernel, own_bins, order),
        (flat, mean, scale, label, trait, local_away, local_here, local_near, local_own),
        [number_shape, jax.ShapeDtypeStruct((PROBES, own_bins, rows), BF16)],
        "stats",
    )
    (part,) = plain(pair_kernel, (stats, *flats), [number_shape], "pair")
    pairs, common = chosen_pairs(list(range(2, n, 2)))
    part_common = swap(part, "ind", n, common)
    part = part + swap(part, "ind", n, 1)
    mine = [swap_mixed(part, n, pair) for pair in pairs]
    theirs = [swap(value, "ind", n, 1) for value in mine + [part_common]]
    pair, trace, quad = plain(
        functools.partial(final_kernel, own_bins, n_bin, len(pairs), rows * n),
        (number, part, part_common, *mine, *theirs),
        [
            jax.ShapeDtypeStruct((own_bins, BINS), F32),
            jax.ShapeDtypeStruct((1, own_bins), F32),
            jax.ShapeDtypeStruct((1, own_bins), F32),
        ],
        "final",
    )
    return jnp.transpose(field, (1, 0, 2)), pair, trace[0], quad[0]


def solution(mesh):
    placed = (P("ind", "bin"), P("bin"), P("bin"), P("bin"), P(None, "ind"), P("ind"))
    return jax.shard_map(
        shards,
        mesh=mesh,
        in_specs=placed,
        out_specs=(P("bin", None, "ind"), P("bin", None), P("bin"), P("bin")),
        check_vma=False,
    )
```

```python
import functools

import jax
import jax.numpy as jnp
from jax import lax
from jax.experimental import pallas as pl
from jax.experimental.pallas import tpu as pltpu
from jax.sharding import PartitionSpec as P

BINS = 24
PROBES = 10
LANES = 128
SUBLANES = 8
ROWS = 16
TRAIT, ONES = PROBES, PROBES + 1
TRACE_LANE, QUAD_LANE = LANES - 2, LANES - 1
PIECE = 640
DOT_PIECE = 768
F32 = jnp.float32
BF16 = jnp.bfloat16
VMEM = pltpu.VMEM
MIB = 1 << 20


def core():
    return lax.rem(lax.axis_index("ind"), 2)


def fold_lanes(value):
    return tree_sum([value[:, at : at + LANES] for at in range(0, value.shape[1], LANES)])


def rows_iota(count, width=1):
    return lax.broadcasted_iota(jnp.int32, (count, width), 0)


def tree_sum(terms):
    terms = list(terms)
    while len(terms) > 1:
        pairs = [a + b for a, b in zip(terms[::2], terms[1::2])]
        terms = pairs + terms[len(pairs) * 2 :]
    return terms[0]


def pack_sums(value):
    half = value.shape[1] // 2
    low = value[SUBLANES:]
    turned = pltpu.roll(low[:, half:], 4, 0)
    low = jnp.where(rows_iota(SUBLANES) < 4, low[:, :half], turned)
    return value[:SUBLANES], low


def halves_of(block):
    first = -(-block // (2 * LANES)) * LANES
    return (0, first), (first, block - first)


def unpack_sums(value):
    span = value.shape[1] * 2 // 3
    low = value[:, span:]
    return value[:, :span], jnp.concatenate([low, pltpu.roll(low, 4, 0)], axis=1)


def moments_kernel(snps, distances, opening, taken, given, geno_ref, *rest):
    rest = list(rest)
    if opening:
        bits_ref, trait_ref, kept_ref, sums_ref, local_ref, left_ref = rest[:6]
        rest = rest[6:]
    else:
        raw_in = rest.pop(0) if taken else None
        left_ref, kept_ref, sums_ref, local_ref = rest[:4]
        rest = rest[4:]
    raw_out = rest.pop(0) if given else None
    buffer, arrived, total_ref = rest[:3]
    rest = rest[3:]
    raw_arrived = rest.pop(0) if given else None
    slots, rows, block = kept_ref.shape
    devices = -(-snps // block)
    tail = snps - (devices - 1) * block
    span = total_ref.shape[1]
    halves = halves_of(block)

    def move(distance, target, semaphore, half, act):
        first, width = halves[half]
        owner = lax.axis_index("ind") ^ distance

        def copy(size):
            start = pl.multiple_of(owner * block + first, LANES)
            act(
                pltpu.make_async_copy(
                    geno_ref.at[:, pl.ds(start, size)],
                    target.at[:, pl.ds(first, size)],
                    semaphore.at[half],
                )
            )

        if tail == block:
            copy(width)
        else:
            last = owner == devices - 1
            short = min(max(tail - first, 0), width)
            pl.when(jnp.logical_not(last))(lambda: copy(width))
            if short:
                pl.when(last)(lambda: copy(short))

    def fetch(slot, half, act):
        move(distances[0] - 2 * slot, buffer.at[slot], arrived.at[slot], half, act)

    def start(copy):
        copy.start()

    def wait(copy):
        copy.wait()

    if opening:
        bits, trait, small = rest[:3]
        bits_copy = pltpu.make_async_copy(bits_ref, bits, small.at[0])
        trait_copy = pltpu.make_async_copy(trait_ref, trait, small.at[1])
        bits_copy.start()
        trait_copy.start()
    for half in range(taken, 2):
        fetch(0, half, start)
    for slot in range(1, slots):
        fetch(slot, 0, start)
        fetch(slot, 1, start)
    if given:
        for half in range(given[1]):
            move(given[0], raw_out, raw_arrived, half, start)
    if opening:
        bits_copy.wait()
        trait_copy.wait()
        left_ref[...] = jnp.zeros_like(left_ref)
        left_ref[0:PROBES] = (2 * bits[...] - 1).astype(F32)
        left_ref[TRAIT : TRAIT + 1] = trait[...].astype(F32).reshape(1, rows)
        left_ref[ONES : ONES + 1] = jnp.ones((1, rows), F32)
    left = left_ref[...]
    base = jnp.sum(left, axis=1, keepdims=True)
    left = left.astype(BF16)
    row = rows_iota(ROWS)

    def with_low(value):
        high = value[TRAIT : TRAIT + 1]
        return jnp.where(row == TRAIT + 1, high - high.astype(BF16).astype(F32), value)

    total_ref[:, block:] = jnp.broadcast_to(with_low(base), (ROWS, span - block))

    def work(slot, half, source):
        first, width = halves[half]
        lanes = slice(first, first + width)
        squares = []
        for at in range(first, first + width, PIECE):
            piece = slice(at, min(at + PIECE, first + width))
            square = 0.0
            for r in range(0, rows, 16):
                dose = source[r : r + 16, piece].astype(F32)
                kept_ref[slot, r : r + 16, piece] = dose.astype(BF16)
                dose = dose * dose
                square = square + (dose[:8] + dose[8:])
            squares.append(jnp.sum(square, axis=0, keepdims=True))
        total = jnp.dot(left, kept_ref[slot, :, lanes], preferred_element_type=F32) - base
        ones = total[ONES : ONES + 1]
        local_ref[slot, 0:1, lanes] = ones
        local_ref[slot, 1:2, lanes] = jnp.concatenate(squares, axis=1) - 2.0 * ones - rows
        total_ref[:, lanes] = with_low(total)

    def close(slot):
        high, low = pack_sums(total_ref[...])
        sums_ref[slot, :, :span] = high.astype(BF16)
        sums_ref[slot, :, span:] = low.astype(BF16)

    for half in range(2):
        if half >= taken:
            fetch(0, half, wait)
        work(0, half, raw_in if half < taken else buffer.at[0])
    close(0)
    if slots > 1:

        @pl.loop(1, slots)
        def _(slot):
            for half in range(2):
                fetch(slot, half, wait)
                work(slot, half, buffer.at[slot])
            close(slot)

    if given:
        for half in range(given[1]):
            move(given[0], raw_out, raw_arrived, half, wait)


def cores_kernel(left_ref, here_ref, away_ref, *outs):
    outs, left_out = outs[:-1], outs[-1]
    left_out[...] = left_ref[...]
    for index, out in enumerate(outs):
        out[...] = (here_ref[index].astype(F32) + away_ref[index].astype(F32)).astype(BF16)


def relay_kernel(token_ref, value_ref, out_ref):
    out_ref[...] = value_ref[...]


def weights_kernel(mean_ref, scale_ref, own_ref, *refs):
    parts, (near_ref, u_ref, trait_ref) = refs[:-3], refs[-3:]
    block = trait_ref.shape[1]
    width = u_ref.shape[1] - block
    here = pl.ds(pl.multiple_of(lax.axis_index("ind") * block, LANES), block)
    parts = [own_ref[0], near_ref[0]] + [part[...] for part in parts]
    total = tree_sum([part.astype(F32) for part in parts])
    shift = mean_ref[:, here] - 1.0
    inverse = 1.0 / scale_ref[:, here]
    high, low = [
        (part[:, :block] - part[:, block : block + 1] * shift) * inverse
        for part in unpack_sums(total)
    ]
    trait_ref[...] = low[2:3] + low[3:4]
    high, low = [part.astype(BF16).astype(F32) * inverse for part in (high, low)]
    low = jnp.concatenate([low, jnp.zeros((SUBLANES, 4 * width - block), F32)], axis=1)
    folded = low[:, :width]
    for j in range(1, 4):
        turned = pltpu.roll(low[:, j * width : (j + 1) * width], 2 * j, 0)
        folded = jnp.where(rows_iota(SUBLANES) < 2 * j, folded, turned)
    u_ref[:, :block] = high.astype(BF16)
    u_ref[:, block:] = folded.astype(BF16)


def stats_kernel(own_bins, order, flat_ref, mean_ref, scale_ref, label_ref, trait_ref, *rest):
    locals_, (out_ref, field_ref) = rest[:-2], rest[-2:]
    block = trait_ref.shape[1]
    rows = order[0]
    bins = rows_iota(SUBLANES)

    def member_of(owner):
        here = pl.ds(pl.multiple_of(owner * block, LANES), block)
        member = label_ref[:, here] - lax.axis_index("bin") * own_bins == bins
        return here, member & (bins < own_bins)

    trace = jnp.zeros((SUBLANES, 1), F32)
    for ref, distances in zip(locals_, order[1]):
        for slot, distance in enumerate(distances):
            here, member = member_of(lax.axis_index("ind") ^ distance)
            shift = mean_ref[:, here] - 1.0
            inverse = 1.0 / scale_ref[:, here]
            square = ref[slot, 1:2] - 2.0 * shift * ref[slot, 0:1] + rows * shift * shift
            square = square * (inverse * inverse)
            trace += jnp.sum(jnp.where(member, square, 0.0), axis=1, keepdims=True)
    _, member = member_of(lax.axis_index("ind"))
    trait = trait_ref[...]
    quad = jnp.sum(jnp.where(member, trait * trait, 0.0), axis=1, keepdims=True)
    lane = lax.broadcasted_iota(jnp.int32, (SUBLANES, LANES), 1)
    out_ref[...] = jnp.where(lane == TRACE_LANE, trace, jnp.where(lane == QUAD_LANE, quad, 0.0))
    flat = flat_ref[...].astype(F32)
    for b in range(PROBES):
        field_ref[b] = flat[:own_bins, b * rows : (b + 1) * rows].astype(BF16)


def labels_kernel(own_bins, token_ref, mean_ref, label_ref, split_ref, count_ref):
    mean = mean_ref[...]
    high = mean.astype(BF16).astype(F32)
    middle = (mean - high).astype(BF16).astype(F32)
    row = rows_iota(ROWS)
    split = jnp.where(row == 0, high, jnp.where(row == 1, middle, mean - high - middle))
    split_ref[...] = jnp.where(row < 3, split, 0.0).astype(BF16)
    member = label_ref[...] - lax.axis_index("bin") * own_bins == rows_iota(SUBLANES)
    number = jnp.sum(jnp.where(member, 1.0, 0.0), axis=1, keepdims=True)
    count_ref[...] = jnp.broadcast_to(number, count_ref.shape)


def field_kernel(own_bins, blocks, sources, started, last, *refs):
    refs = list(refs)
    split_ref, label_ref = refs[:2]
    kept_refs, refs = refs[2 : 2 + sources], refs[2 + sources :]
    u_refs, refs = refs[: len(blocks)], refs[len(blocks) :]
    rows, block = kept_refs[0].shape[1:]
    bins = rows_iota(SUBLANES)
    if started:
        acc, refs = refs[0][...], refs[1:]
    else:
        acc = jnp.zeros((rows + ROWS, PROBES * SUBLANES), F32)
    for index, (slot, distance) in enumerate(blocks):
        start = (lax.axis_index("ind") ^ distance) * block
        u = u_refs[index][...].astype(F32)
        lines = [u[b : b + 1, :block] for b in range(SUBLANES)]
        for b in range(PROBES - SUBLANES):
            line = [u[2 * j + b : 2 * j + b + 1, block:] for j in range(4)]
            lines.append(jnp.concatenate(line, axis=1)[:, :block])
        for at in range(0, block, DOT_PIECE):
            width = min(DOT_PIECE, block - at)
            here = pl.ds(pl.multiple_of(start + at, LANES), width)
            member = label_ref[:, here] - lax.axis_index("bin") * own_bins == bins
            member = member & (bins < own_bins)
            spread = [jnp.where(member, line[:, at : at + width], 0.0) for line in lines]
            kept = kept_refs[index if sources > 1 else 0][slot, :, at : at + width]
            acc += lax.dot_general(
                jnp.concatenate([kept, split_ref[:, here]], axis=0),
                jnp.concatenate(spread, axis=0).astype(BF16),
                (((1,), (1,)), ((), ())),
                preferred_element_type=F32,
            )
    if not last:
        refs[0][...] = acc
        return
    count_ref, flat_ref = refs
    acc = acc[:rows] - jnp.sum(acc[rows:], axis=0, keepdims=True)
    acc = jnp.concatenate([acc, jnp.zeros((rows, LANES - acc.shape[1]), F32)], axis=1)
    acc = jnp.transpose(acc)
    inverse = 1.0 / jnp.maximum(count_ref[:, :1], 1.0)
    flat = [acc[b * SUBLANES : (b + 1) * SUBLANES] * inverse for b in range(PROBES)]
    flat_ref[...] = jnp.concatenate(flat, axis=1).astype(BF16)


def pair_kernel(stats_ref, *rest):
    flats, out_ref = rest[-2::-1], rest[-1]
    everyone = [flat[...].astype(F32) for flat in flats]
    everyone += [jnp.zeros_like(everyone[0])] * (LANES // SUBLANES - len(flats))
    out_ref[...] = stats_ref[...] + lax.dot_general(
        flats[0][...],
        jnp.concatenate(everyone, axis=0).astype(BF16),
        (((1,), (1,)), ((), ())),
        preferred_element_type=F32,
    )


def final_kernel(own_bins, n_bin, pairs, total_rows, count_ref, own_ref, common_ref, *rest):
    mine, theirs, outs = rest[:pairs], rest[pairs : 2 * pairs + 1], rest[2 * pairs + 1 :]
    pair_ref, trace_ref, quad_ref = outs
    terms = [own_ref[...]]
    even = core() == 0
    for ref, other in zip(mine, theirs):
        terms.append(jnp.where(even, ref[...], other[...]))
        terms.append(jnp.where(even, other[...], ref[...]))
    terms.append(common_ref[...] + theirs[pairs][...])
    total = tree_sum(terms)
    row = lax.broadcasted_iota(jnp.int32, (SUBLANES, LANES), 0)
    lane = lax.broadcasted_iota(jnp.int32, (SUBLANES, LANES), 1)
    pair = jnp.zeros_like(total)
    for slot in range(n_bin):
        start = slot * SUBLANES
        part = jnp.where((lane >= start) & (lane < start + own_bins), total, 0.0)
        shift = (lax.axis_index("bin") ^ slot) * own_bins - start + LANES
        pair = pair + pltpu.roll(part, lax.rem(shift, LANES), 1)
    pair_ref[...] = pair[:own_bins, :BINS] / (PROBES * total_rows)
    scaled = total / (count_ref[...] * total_rows)
    for ref, column in ((trace_ref, TRACE_LANE), (quad_ref, QUAD_LANE)):
        turned = jnp.where(row == lane, scaled[:, column : column + 1], 0.0)
        ref[...] = jnp.sum(turned, axis=0, keepdims=True)[:, :own_bins]


def swap(value, axis, size, distance):
    return lax.ppermute(value, axis, [(i, i ^ distance) for i in range(size)])


def swap_mixed(value, size, pair):
    return lax.ppermute(value, "ind", [(i, i ^ pair[i % 2]) for i in range(size)])


def chosen_pairs(distances):
    return list(zip(distances[:-1:2], distances[1:-1:2])), distances[-1]


def in_vmem():
    return pl.BlockSpec(memory_space=VMEM)


def in_hbm():
    return pl.BlockSpec(memory_space=pltpu.HBM)


def params(mib):
    return pltpu.CompilerParams(vmem_limit_bytes=mib * MIB)


def cost(flops, moved):
    return pl.CostEstimate(flops=flops, bytes_accessed=moved, transcendentals=0)


def shards(genotype, snp_mean, snp_scale, snp_label, probe_bits, phenotype):
    n = lax.axis_size("ind")
    n_bin = lax.axis_size("bin")
    chips = n // 2
    own_bins = BINS // n_bin
    rows, snps = genotype.shape
    tiles = -(-snps // LANES)
    block_tiles = -(-tiles // n)
    block = block_tiles * LANES
    span = block + LANES * (2 - block_tiles % 2)
    folded = block + -(-block_tiles // 4) * LANES
    whole = n * block
    mean, scale, label = snp_mean, snp_scale, snp_label
    if whole != snps:
        mean = jnp.pad(mean, (0, whole - snps), constant_values=1.0)
        scale = jnp.pad(scale, (0, whole - snps), constant_values=1.0)
        label = jnp.pad(label, (0, whole - snps), constant_values=-1)
    mean, scale, label = mean[None, :], scale[None, :], label[None, :]
    genotype, probe_bits, phenotype = [
        pltpu.with_memory_space_constraint(value, pltpu.HBM)
        for value in (genotype, probe_bits, phenotype)
    ]

    def moments(distances, taken, given, extra, name):
        slots = len(distances)
        opening = extra[0] is probe_bits
        extra = [value for value in extra if value is not None]
        out_shape = [
            jax.ShapeDtypeStruct((slots, rows, block), BF16),
            jax.ShapeDtypeStruct((slots, SUBLANES, span * 3 // 2), BF16),
            jax.ShapeDtypeStruct((slots, 2, block), F32),
        ]
        if opening:
            out_shape.append(jax.ShapeDtypeStruct((ROWS, rows), F32))
        if given:
            out_shape.append(jax.ShapeDtypeStruct((rows, block), jnp.int32))
        scratch = [
            VMEM((slots, rows, block), jnp.int32),
            pltpu.SemaphoreType.DMA((slots, 2)),
            VMEM((ROWS, span), F32),
        ]
        if given:
            scratch.append(pltpu.SemaphoreType.DMA((2,)))
        if opening:
            scratch += [
                VMEM(probe_bits.shape, jnp.int32),
                VMEM((rows,), BF16),
                pltpu.SemaphoreType.DMA((2,)),
            ]
        return pl.pallas_call(
            functools.partial(moments_kernel, snps, distances, opening, taken, given),
            in_specs=[in_hbm()] + [in_hbm() if opening else in_vmem()] * len(extra),
            out_specs=[in_vmem()] * len(out_shape),
            scratch_shapes=scratch,
            out_shape=out_shape,
            cost_estimate=cost(1, 4 * rows * block * slots if slots > 1 else 1),
            compiler_params=params(20),
            name=name,
        )(genotype, *extra)

    here_order = list(range(n - 2, 0, -2))
    away_order = [d + 1 for d in here_order]

    def plain(kernel, operands, out_shape, name, **options):
        return pl.pallas_call(
            kernel,
            in_specs=[in_vmem()] * len(operands),
            out_specs=[in_vmem()] * len(out_shape),
            out_shape=out_shape,
            compiler_params=params(20),
            name=name,
            **options,
        )(*operands)

    kept_away, away, local_away, left, raw = moments(
        away_order, 0, (here_order[0], 2), (probe_bits, phenotype), "moments_away"
    )
    away = swap(away, "ind", n, 1)
    kept_here, here, local_here = moments(here_order, 2, None, (raw, left), "moments_here")
    packed = jax.ShapeDtypeStruct((SUBLANES, span * 3 // 2), BF16)
    *sums, left = plain(
        cores_kernel,
        (left, here, away),
        [packed] * (chips - 1) + [jax.ShapeDtypeStruct(left.shape, F32)],
        "cores",
    )
    sums = [swap(value, "ind", n, d) for value, d in zip(sums, here_order)]
    kept_near, near, local_near, raw = moments([1], 0, (0, 1), (None, left), "moments_near")
    near = swap(near, "ind", n, 1)
    kept_own, own, local_own = moments([0], 1, None, (raw, left), "moments_own")

    u, trait = plain(
        weights_kernel,
        (mean, scale, own, *sums, near),
        [
            jax.ShapeDtypeStruct((SUBLANES, folded), BF16),
            jax.ShapeDtypeStruct((1, block), F32),
        ],
        "weights",
    )

    number_shape = jax.ShapeDtypeStruct((SUBLANES, LANES), F32)
    term_shape = jax.ShapeDtypeStruct((rows + ROWS, PROBES * SUBLANES), F32)
    flat_shape = jax.ShapeDtypeStruct((SUBLANES, PROBES * rows), BF16)
    split, number = plain(
        functools.partial(labels_kernel, own_bins),
        (trait, mean, label),
        [jax.ShapeDtypeStruct((ROWS, whole), BF16), number_shape],
        "labels",
    )

    def fields(kept, blocks, us, terms, last=False):
        terms = ([terms] if terms is not None else []) + ([number] if last else [])
        started = len(terms) > last
        return plain(
            functools.partial(field_kernel, own_bins, blocks, len(kept), started, last),
            (split, label, *kept, *us, *terms),
            [flat_shape if last else term_shape],
            "field",
            cost_estimate=cost(1, 2 * MIB),
        )[0]

    u_near = swap(u, "ind", n, 1)
    u_here = [swap(u, "ind", n, d) for d in here_order]
    terms = fields([kept_own, kept_near], [(0, 0), (0, 1)], [u, u_near], None)
    u_away = []
    for slot, (distance, value) in enumerate(zip(here_order, u_here)):
        shape = [jax.ShapeDtypeStruct(value.shape, value.dtype)]
        (value,) = plain(relay_kernel, (terms, value), shape, "relay")
        u_away.append(swap(value, "ind", n, 1))
        terms = fields([kept_here], [(slot, distance)], [value], terms)
    blocks = list(enumerate(away_order))
    middle = (chips - 1) // 2
    terms = fields([kept_away], blocks[:middle], u_away[:middle], terms)
    flat = fields([kept_away], blocks[middle:], u_away[middle:], terms, last=True)

    flats = [swap(flat, "bin", n_bin, d) for d in range(n_bin - 1, 0, -1)]
    flats = [flat] + flats[::-1]
    order = (rows, (away_order, here_order, [1], [0]))
    stats, field = plain(
        functools.partial(stats_kernel, own_bins, order),
        (flat, mean, scale, label, trait, local_away, local_here, local_near, local_own),
        [number_shape, jax.ShapeDtypeStruct((PROBES, own_bins, rows), BF16)],
        "stats",
    )
    (part,) = plain(pair_kernel, (stats, *flats[::-1]), [number_shape], "pair")
    pairs, common = chosen_pairs(list(range(2, n, 2)))
    part_common = swap(part, "ind", n, common)
    part = part + swap(part, "ind", n, 1)
    mine = [swap_mixed(part, n, pair) for pair in pairs]
    theirs = [swap(value, "ind", n, 1) for value in mine + [part_common]]
    pair, trace, quad = plain(
        functools.partial(final_kernel, own_bins, n_bin, len(pairs), rows * n),
        (number, part, part_common, *mine, *theirs),
        [
            jax.ShapeDtypeStruct((own_bins, BINS), F32),
            jax.ShapeDtypeStruct((1, own_bins), F32),
            jax.ShapeDtypeStruct((1, own_bins), F32),
        ],
        "final",
    )
    return jnp.transpose(field, (1, 0, 2)), pair, trace[0], quad[0]


def solution(mesh):
    placed = (P("ind", "bin"), P("bin"), P("bin"), P("bin"), P(None, "ind"), P("ind"))
    return jax.shard_map(
        shards,
        mesh=mesh,
        in_specs=placed,
        out_specs=(P("bin", None, "ind"), P("bin", None), P("bin"), P("bin")),
        check_vma=False,
    )
```

```python
import functools

import jax
import jax.numpy as jnp
from jax import lax
from jax.experimental import pallas as pl
from jax.experimental.pallas import tpu as pltpu
from jax.sharding import PartitionSpec as P

BINS = 24
PROBES = 10
LANES = 128
SUBLANES = 8
ROWS = 16
TRAIT, ONES = PROBES, PROBES + 1
TRACE_LANE, QUAD_LANE = LANES - 2, LANES - 1
PIECE = 640
DOT_PIECE = 768
F32 = jnp.float32
BF16 = jnp.bfloat16
VMEM = pltpu.VMEM
MIB = 1 << 20


def core():
    return lax.rem(lax.axis_index("ind"), 2)


def pick(pair):
    return pair[0] if pair[0] == pair[1] else jnp.where(core() == 0, pair[0], pair[1])


def turns(distances):
    pairs = [(distances[0], distances[0])]
    for a, b in zip(distances[1::2], distances[2::2]):
        pairs += [(a, b), (b, a)]
    return pairs


def fold_lanes(value):
    return tree_sum([value[:, at : at + LANES] for at in range(0, value.shape[1], LANES)])


def rows_iota(count, width=1):
    return lax.broadcasted_iota(jnp.int32, (count, width), 0)


def tree_sum(terms):
    terms = list(terms)
    while len(terms) > 1:
        pairs = [a + b for a, b in zip(terms[::2], terms[1::2])]
        terms = pairs + terms[len(pairs) * 2 :]
    return terms[0]


def pack_sums(value):
    half = value.shape[1] // 2
    low = value[SUBLANES:]
    turned = pltpu.roll(low[:, half:], 4, 0)
    low = jnp.where(rows_iota(SUBLANES) < 4, low[:, :half], turned)
    return value[:SUBLANES], low


def unpack_sums(value):
    span = value.shape[1] * 2 // 3
    low = value[:, span:]
    return value[:, :span], jnp.concatenate([low, pltpu.roll(low, 4, 0)], axis=1)


def moments_kernel(snps, distances, opening, taken, given, geno_ref, *rest):
    rest = list(rest)
    raw_ins = []
    if opening:
        bits_ref, trait_ref, kept_ref, sums_ref, local_ref, left_ref = rest[:6]
        rest = rest[6:]
    else:
        raw_ins, rest = rest[:taken], rest[taken:]
        left_ref, kept_ref, sums_ref, local_ref = rest[:4]
        rest = rest[4:]
    raw_outs, rest = rest[: len(given)], rest[len(given) :]
    slots, rows, block = kept_ref.shape
    fetched = slots - taken
    devices = -(-snps // block)
    tail = snps - (devices - 1) * block
    span = sums_ref.shape[2] * 2 // 3

    def copy(distance, target, semaphore, width):
        start = pl.multiple_of((lax.axis_index("ind") ^ distance) * block, LANES)
        return pltpu.make_async_copy(
            geno_ref.at[:, pl.ds(start, width)], target.at[:, pl.ds(0, width)], semaphore
        )

    def whole_or_tail(distance, target, semaphore, act):
        if tail == block:
            act(copy(distance, target, semaphore, block))
        else:
            last = (lax.axis_index("ind") ^ distance) == devices - 1
            pl.when(last)(lambda: act(copy(distance, target, semaphore, tail)))
            pl.when(jnp.logical_not(last))(lambda: act(copy(distance, target, semaphore, block)))

    if fetched:
        buffer, arrived = rest[:2]
        rest = rest[2:]

        def fetch(index, act):
            distance = pick(distances[taken])
            for slot in range(taken + 1, slots):
                distance = jnp.where(index + taken == slot, pick(distances[slot]), distance)
            whole_or_tail(distance, buffer.at[index], arrived.at[index], act)

    if given:
        raw_arrived = rest.pop(0)

    def hand_over(act):
        for index, (distance, out) in enumerate(zip(given, raw_outs)):
            whole_or_tail(pick(distance), out, raw_arrived.at[index], act)

    if opening:
        bits, trait, small = rest[:3]
        bits_copy = pltpu.make_async_copy(bits_ref, bits, small.at[0])
        trait_copy = pltpu.make_async_copy(trait_ref, trait, small.at[1])
        bits_copy.start()
        trait_copy.start()
    if fetched:
        pl.loop(0, fetched)(lambda index: fetch(index, lambda c: c.start()))
    hand_over(lambda c: c.start())
    if opening:
        bits_copy.wait()
        trait_copy.wait()
        left_ref[...] = jnp.zeros_like(left_ref)
        left_ref[0:PROBES] = (2 * bits[...] - 1).astype(F32)
        left_ref[TRAIT : TRAIT + 1] = trait[...].astype(F32).reshape(1, rows)
        left_ref[ONES : ONES + 1] = jnp.ones((1, rows), F32)
    left = left_ref[...]
    base = jnp.sum(left, axis=1, keepdims=True)
    left = left.astype(BF16)
    row = rows_iota(ROWS)

    def with_low(value):
        high = value[TRAIT : TRAIT + 1]
        return jnp.where(row == TRAIT + 1, high - high.astype(BF16).astype(F32), value)

    ends = jnp.broadcast_to(with_low(base), (ROWS, span - block))

    def work(slot, source):
        squares = []
        for at in range(0, block, PIECE):
            lanes = slice(at, min(at + PIECE, block))
            square = 0.0
            for r in range(0, rows, 16):
                dose = source[r : r + 16, lanes].astype(F32)
                kept_ref[slot, r : r + 16, lanes] = dose.astype(BF16)
                dose = dose * dose
                square = square + (dose[:8] + dose[8:])
            squares.append(jnp.sum(square, axis=0, keepdims=True))
        total = jnp.dot(left, kept_ref[slot], preferred_element_type=F32) - base
        ones = total[ONES : ONES + 1]
        local_ref[slot, 0:1] = ones
        local_ref[slot, 1:2] = jnp.concatenate(squares, axis=1) - 2.0 * ones - rows
        high, low = pack_sums(jnp.concatenate([with_low(total), ends], axis=1))
        sums_ref[slot, :, :span] = high.astype(BF16)
        sums_ref[slot, :, span:] = low.astype(BF16)

    for slot, raw_in in enumerate(raw_ins):
        work(slot, raw_in)
    if fetched:

        @pl.loop(0, fetched)
        def _(index):
            fetch(index, lambda c: c.wait())
            work(index + taken, buffer.at[index])

    hand_over(lambda c: c.wait())


def cores_kernel(left_ref, here_ref, away_ref, *outs):
    outs, left_out = outs[:-1], outs[-1]
    left_out[...] = left_ref[...]
    for index, out in enumerate(outs):
        out[...] = (here_ref[index].astype(F32) + away_ref[index].astype(F32)).astype(BF16)


def relay_kernel(token_ref, value_ref, out_ref):
    out_ref[...] = value_ref[...]


def weights_kernel(mean_ref, scale_ref, own_ref, near_ref, *refs):
    parts, (u_ref, trait_ref) = refs[:-2], refs[-2:]
    block = trait_ref.shape[1]
    width = u_ref.shape[1] - block
    here = pl.ds(pl.multiple_of(lax.axis_index("ind") * block, LANES), block)
    parts = [own_ref[0], near_ref[0]] + [part[...] for part in parts]
    total = tree_sum([part.astype(F32) for part in parts])
    shift = mean_ref[:, here] - 1.0
    inverse = 1.0 / scale_ref[:, here]
    high, low = [
        (part[:, :block] - part[:, block : block + 1] * shift) * inverse
        for part in unpack_sums(total)
    ]
    trait_ref[...] = low[2:3] + low[3:4]
    high, low = [part.astype(BF16).astype(F32) * inverse for part in (high, low)]
    low = jnp.concatenate([low, jnp.zeros((SUBLANES, 4 * width - block), F32)], axis=1)
    folded = low[:, :width]
    for j in range(1, 4):
        turned = pltpu.roll(low[:, j * width : (j + 1) * width], 2 * j, 0)
        folded = jnp.where(rows_iota(SUBLANES) < 2 * j, folded, turned)
    u_ref[:, :block] = high.astype(BF16)
    u_ref[:, block:] = folded.astype(BF16)


def stats_kernel(own_bins, order, flat_ref, mean_ref, scale_ref, label_ref, trait_ref, *rest):
    locals_, (out_ref, field_ref) = rest[:-2], rest[-2:]
    block = trait_ref.shape[1]
    rows = order[0]
    bins = rows_iota(SUBLANES)

    def member_of(owner):
        here = pl.ds(pl.multiple_of(owner * block, LANES), block)
        member = label_ref[:, here] - lax.axis_index("bin") * own_bins == bins
        return here, member & (bins < own_bins)

    trace = jnp.zeros((SUBLANES, 1), F32)
    for ref, distances in zip(locals_, order[1]):
        for slot, distance in enumerate(distances):
            here, member = member_of(lax.axis_index("ind") ^ pick(distance))
            shift = mean_ref[:, here] - 1.0
            inverse = 1.0 / scale_ref[:, here]
            square = ref[slot, 1:2] - 2.0 * shift * ref[slot, 0:1] + rows * shift * shift
            square = square * (inverse * inverse)
            trace += jnp.sum(jnp.where(member, square, 0.0), axis=1, keepdims=True)
    _, member = member_of(lax.axis_index("ind"))
    trait = trait_ref[...]
    quad = jnp.sum(jnp.where(member, trait * trait, 0.0), axis=1, keepdims=True)
    lane = lax.broadcasted_iota(jnp.int32, (SUBLANES, LANES), 1)
    out_ref[...] = jnp.where(lane == TRACE_LANE, trace, jnp.where(lane == QUAD_LANE, quad, 0.0))
    flat = flat_ref[...].astype(F32)
    for b in range(PROBES):
        field_ref[b] = flat[:own_bins, b * rows : (b + 1) * rows].astype(BF16)


def field_kernel(own_bins, blocks, sources, started, last, *refs):
    refs = list(refs)
    mean_ref, label_ref = refs[:2]
    kept_refs, refs = refs[2 : 2 + sources], refs[2 + sources :]
    u_refs, refs = refs[: len(blocks)], refs[len(blocks) :]
    rows, block = kept_refs[0].shape[1:]
    bins = rows_iota(SUBLANES)
    if started:
        acc, offset, number = [ref[...] for ref in refs[:3]]
        refs = refs[3:]
    else:
        acc = jnp.zeros((rows, PROBES * SUBLANES), F32)
        offset = jnp.zeros((PROBES * SUBLANES, LANES), F32)
        number = jnp.zeros((SUBLANES, LANES), F32)
    for index, (slot, distance) in enumerate(blocks):
        start = (lax.axis_index("ind") ^ pick(distance)) * block
        u = u_refs[index][...].astype(F32)
        lines = [u[b : b + 1, :block] for b in range(SUBLANES)]
        for b in range(PROBES - SUBLANES):
            line = [u[2 * j + b : 2 * j + b + 1, block:] for j in range(4)]
            lines.append(jnp.concatenate(line, axis=1)[:, :block])
        for at in range(0, block, DOT_PIECE):
            width = min(DOT_PIECE, block - at)
            here = pl.ds(pl.multiple_of(start + at, LANES), width)
            member = label_ref[:, here] - lax.axis_index("bin") * own_bins == bins
            member = member & (bins < own_bins)
            mean = mean_ref[:, here]
            spread = [jnp.where(member, line[:, at : at + width], 0.0) for line in lines]
            offset += jnp.concatenate([fold_lanes(value * mean) for value in spread], axis=0)
            number += fold_lanes(jnp.where(member, 1.0, 0.0))
            acc += lax.dot_general(
                kept_refs[index if sources > 1 else 0][slot, :, at : at + width],
                jnp.concatenate(spread, axis=0).astype(BF16),
                (((1,), (1,)), ((), ())),
                preferred_element_type=F32,
            )
    if not last:
        for ref, value in zip(refs, (acc, offset, number)):
            ref[...] = value
        return
    flat_ref, count_ref = refs
    acc = jnp.concatenate([acc, jnp.zeros((rows, LANES - acc.shape[1]), F32)], axis=1)
    acc = jnp.transpose(acc)[: PROBES * SUBLANES] - jnp.sum(offset, axis=1, keepdims=True)
    number = jnp.sum(number, axis=1, keepdims=True)
    count_ref[...] = jnp.broadcast_to(number, count_ref.shape)
    inverse = 1.0 / jnp.maximum(number, 1.0)
    flat = [acc[b * SUBLANES : (b + 1) * SUBLANES] * inverse for b in range(PROBES)]
    flat_ref[...] = jnp.concatenate(flat, axis=1).astype(BF16)


def pair_kernel(stats_ref, *rest):
    flats, out_ref = rest[:-1], rest[-1]
    slots = [flat[...].astype(F32) for flat in flats]
    everyone = slots[:1]
    for low, high in zip(slots[1:-1:2], slots[2:-1:2]):
        everyone.append(jnp.where(core() == 0, low, high))
        everyone.append(jnp.where(core() == 0, high, low))
    everyone.append(slots[-1])
    everyone += [jnp.zeros_like(everyone[0])] * (LANES // SUBLANES - len(flats))
    out_ref[...] = stats_ref[...] + lax.dot_general(
        flats[0][...],
        jnp.concatenate(everyone, axis=0).astype(BF16),
        (((1,), (1,)), ((), ())),
        preferred_element_type=F32,
    )


def final_kernel(own_bins, n_bin, pairs, total_rows, count_ref, own_ref, common_ref, *rest):
    mine, theirs, outs = rest[:pairs], rest[pairs : 2 * pairs + 1], rest[2 * pairs + 1 :]
    pair_ref, trace_ref, quad_ref = outs
    terms = [own_ref[...]]
    even = core() == 0
    for ref, other in zip(mine, theirs):
        terms.append(jnp.where(even, ref[...], other[...]))
        terms.append(jnp.where(even, other[...], ref[...]))
    terms.append(common_ref[...] + theirs[pairs][...])
    total = tree_sum(terms)
    row = lax.broadcasted_iota(jnp.int32, (SUBLANES, LANES), 0)
    lane = lax.broadcasted_iota(jnp.int32, (SUBLANES, LANES), 1)
    pair = jnp.zeros_like(total)
    for slot in range(n_bin):
        start = slot * SUBLANES
        part = jnp.where((lane >= start) & (lane < start + own_bins), total, 0.0)
        shift = (lax.axis_index("bin") ^ slot) * own_bins - start + LANES
        pair = pair + pltpu.roll(part, lax.rem(shift, LANES), 1)
    pair_ref[...] = pair[:own_bins, :BINS] / (PROBES * total_rows)
    scaled = total / (count_ref[...] * total_rows)
    for ref, column in ((trace_ref, TRACE_LANE), (quad_ref, QUAD_LANE)):
        turned = jnp.where(row == lane, scaled[:, column : column + 1], 0.0)
        ref[...] = jnp.sum(turned, axis=0, keepdims=True)[:, :own_bins]


def swap(value, axis, size, distance):
    return lax.ppermute(value, axis, [(i, i ^ distance) for i in range(size)])


def swap_mixed(value, axis, sizes, pair):
    moves = []
    for i in range(sizes[0]):
        for j in range(sizes[1]):
            k, m = (i ^ pair[i % 2], j) if axis == "ind" else (i, j ^ pair[i % 2])
            moves.append((i * sizes[1] + j, k * sizes[1] + m))
    return lax.ppermute(value, ("ind", "bin"), moves)


def chosen_pairs(distances):
    return list(zip(distances[:-1:2], distances[1:-1:2])), distances[-1]


def in_vmem():
    return pl.BlockSpec(memory_space=VMEM)


def in_hbm():
    return pl.BlockSpec(memory_space=pltpu.HBM)


def params(mib):
    return pltpu.CompilerParams(vmem_limit_bytes=mib * MIB)


def cost(flops, moved):
    return pl.CostEstimate(flops=flops, bytes_accessed=moved, transcendentals=0)


def shards(genotype, snp_mean, snp_scale, snp_label, probe_bits, phenotype):
    n = lax.axis_size("ind")
    n_bin = lax.axis_size("bin")
    chips = n // 2
    own_bins = BINS // n_bin
    rows, snps = genotype.shape
    tiles = -(-snps // LANES)
    block_tiles = -(-tiles // n)
    block = block_tiles * LANES
    span = block + LANES * (2 - block_tiles % 2)
    folded = block + -(-block_tiles // 4) * LANES
    whole = n * block
    mean, scale, label = snp_mean, snp_scale, snp_label
    if whole != snps:
        mean = jnp.pad(mean, (0, whole - snps), constant_values=1.0)
        scale = jnp.pad(scale, (0, whole - snps), constant_values=1.0)
        label = jnp.pad(label, (0, whole - snps), constant_values=-1)
    mean, scale, label = mean[None, :], scale[None, :], label[None, :]
    genotype, probe_bits, phenotype = [
        pltpu.with_memory_space_constraint(value, pltpu.HBM)
        for value in (genotype, probe_bits, phenotype)
    ]

    def moments(distances, given, extra, name):
        slots = len(distances)
        opening = extra[0] is probe_bits
        taken = 0 if opening else len(extra) - 1
        fetched = slots - taken
        out_shape = [
            jax.ShapeDtypeStruct((slots, rows, block), BF16),
            jax.ShapeDtypeStruct((slots, SUBLANES, span * 3 // 2), BF16),
            jax.ShapeDtypeStruct((slots, 2, block), F32),
        ]
        if opening:
            out_shape.append(jax.ShapeDtypeStruct((ROWS, rows), F32))
        out_shape += [jax.ShapeDtypeStruct((rows, block), jnp.int32)] * len(given)
        scratch = []
        if fetched:
            scratch += [VMEM((fetched, rows, block), jnp.int32), pltpu.SemaphoreType.DMA((fetched,))]
        if given:
            scratch.append(pltpu.SemaphoreType.DMA((len(given),)))
        if opening:
            scratch += [
                VMEM(probe_bits.shape, jnp.int32),
                VMEM((rows,), BF16),
                pltpu.SemaphoreType.DMA((2,)),
            ]
        return pl.pallas_call(
            functools.partial(moments_kernel, snps, distances, opening, taken, given),
            in_specs=[in_hbm()] + [in_hbm() if opening else in_vmem()] * len(extra),
            out_specs=[in_vmem()] * len(out_shape),
            scratch_shapes=scratch,
            out_shape=out_shape,
            cost_estimate=cost(1, 4 * rows * block * slots if slots > 1 else 1),
            compiler_params=params(20),
            name=name,
        )(genotype, *extra)

    sizes = (n, n_bin)
    here_order = turns(list(range(n - 2, 0, -2)))
    away_order = [(b + 1, a + 1) for a, b in here_order]

    def plain(kernel, operands, out_shape, name, **options):
        return pl.pallas_call(
            kernel,
            in_specs=[in_vmem()] * len(operands),
            out_specs=[in_vmem()] * len(out_shape),
            out_shape=out_shape,
            compiler_params=params(20),
            name=name,
            **options,
        )(*operands)

    kept_away, away, local_away, left, *raws = moments(
        away_order, here_order[:2], (probe_bits, phenotype), "moments_away"
    )
    away = swap(away, "ind", n, 1)
    kept_here, here, local_here = moments(here_order, [], (*raws, left), "moments_here")
    packed = jax.ShapeDtypeStruct((SUBLANES, span * 3 // 2), BF16)
    *sums, left = plain(
        cores_kernel,
        (left, here, away),
        [packed] * (chips - 1) + [jax.ShapeDtypeStruct(left.shape, F32)],
        "cores",
    )
    sums = [swap_mixed(value, "ind", sizes, d) for value, d in zip(sums, here_order)]
    kept_near, near, local_near, raw = moments([(1, 1)], [(0, 0)], (left,), "moments_near")
    near = swap(near, "ind", n, 1)
    kept_own, own, local_own = moments([(0, 0)], [], (raw, left), "moments_own")

    u, trait = plain(
        weights_kernel,
        (mean, scale, own, near, *sums),
        [
            jax.ShapeDtypeStruct((SUBLANES, folded), BF16),
            jax.ShapeDtypeStruct((1, block), F32),
        ],
        "weights",
    )

    number_shape = jax.ShapeDtypeStruct((SUBLANES, LANES), F32)
    term_shape = [
        jax.ShapeDtypeStruct((rows, PROBES * SUBLANES), F32),
        jax.ShapeDtypeStruct((PROBES * SUBLANES, LANES), F32),
        number_shape,
    ]
    end_shape = [jax.ShapeDtypeStruct((SUBLANES, PROBES * rows), BF16), number_shape]

    def fields(kept, blocks, us, terms, last=False):
        return plain(
            functools.partial(field_kernel, own_bins, blocks, len(kept), bool(terms), last),
            (mean, label, *kept, *us, *terms),
            end_shape if last else term_shape,
            "field",
            cost_estimate=cost(1, 1),
        )

    u_near = swap(u, "ind", n, 1)
    u_here = [swap_mixed(u, "ind", sizes, d) for d in here_order]
    terms = fields([kept_own, kept_near], [(0, (0, 0)), (0, (1, 1))], [u, u_near], [])
    u_away = []
    for slot, (distance, value) in enumerate(zip(here_order, u_here)):
        shape = [jax.ShapeDtypeStruct(value.shape, value.dtype)]
        (value,) = plain(relay_kernel, (terms[2], value), shape, "relay")
        u_away.append(swap(value, "ind", n, 1))
        terms = fields([kept_here], [(slot, distance)], [value], terms)
    blocks = list(enumerate(away_order))
    middle = (chips - 1) // 2
    terms = fields([kept_away], blocks[:middle], u_away[:middle], terms)
    flat, number = fields([kept_away], blocks[middle:], u_away[middle:], terms, last=True)

    bin_order = turns(list(range(n_bin - 1, 0, -1)))
    flats = [flat] + [swap_mixed(flat, "bin", sizes, d) for d in bin_order[::-1]]
    order = (rows, (away_order, here_order, [(1, 1)], [(0, 0)]))
    stats, field = plain(
        functools.partial(stats_kernel, own_bins, order),
        (flat, mean, scale, label, trait, local_away, local_here, local_near, local_own),
        [number_shape, jax.ShapeDtypeStruct((PROBES, own_bins, rows), BF16)],
        "stats",
    )
    (part,) = plain(pair_kernel, (stats, *flats), [number_shape], "pair")
    pairs, common = chosen_pairs(list(range(2, n, 2)))
    part_common = swap(part, "ind", n, common)
    part = part + swap(part, "ind", n, 1)
    mine = [swap_mixed(part, "ind", sizes, pair) for pair in pairs]
    theirs = [swap(value, "ind", n, 1) for value in mine + [part_common]]
    pair, trace, quad = plain(
        functools.partial(final_kernel, own_bins, n_bin, len(pairs), rows * n),
        (number, part, part_common, *mine, *theirs),
        [
            jax.ShapeDtypeStruct((own_bins, BINS), F32),
            jax.ShapeDtypeStruct((1, own_bins), F32),
            jax.ShapeDtypeStruct((1, own_bins), F32),
        ],
        "final",
    )
    return jnp.transpose(field, (1, 0, 2)), pair, trace[0], quad[0]


def solution(mesh):
    placed = (P("ind", "bin"), P("bin"), P("bin"), P("bin"), P(None, "ind"), P("ind"))
    return jax.shard_map(
        shards,
        mesh=mesh,
        in_specs=placed,
        out_specs=(P("bin", None, "ind"), P("bin", None), P("bin"), P("bin")),
        check_vma=False,
    )
```

```python
import functools

import jax
import jax.numpy as jnp
from jax import lax
from jax.experimental import pallas as pl
from jax.experimental.pallas import tpu as pltpu
from jax.sharding import PartitionSpec as P

BINS = 24
PROBES = 10
LANES = 128
SUBLANES = 8
ROWS = 16
TRAIT, ONES = PROBES, PROBES + 1
TRACE_LANE, QUAD_LANE = LANES - 2, LANES - 1
PIECE = 640
DOT_PIECE = 768
F32 = jnp.float32
BF16 = jnp.bfloat16
VMEM = pltpu.VMEM
MIB = 1 << 20


def core():
    return lax.rem(lax.axis_index("ind"), 2)


def fold_lanes(value):
    return tree_sum([value[:, at : at + LANES] for at in range(0, value.shape[1], LANES)])


def rows_iota(count, width=1):
    return lax.broadcasted_iota(jnp.int32, (count, width), 0)


def tree_sum(terms):
    terms = list(terms)
    while len(terms) > 1:
        pairs = [a + b for a, b in zip(terms[::2], terms[1::2])]
        terms = pairs + terms[len(pairs) * 2 :]
    return terms[0]


def pack_sums(value):
    half = value.shape[1] // 2
    low = value[SUBLANES:]
    turned = pltpu.roll(low[:, half:], 4, 0)
    low = jnp.where(rows_iota(SUBLANES) < 4, low[:, :half], turned)
    return value[:SUBLANES], low


def unpack_sums(value):
    span = value.shape[1] * 2 // 3
    low = value[:, span:]
    return value[:, :span], jnp.concatenate([low, pltpu.roll(low, 4, 0)], axis=1)


def owner_of(chip, keep):
    return 2 * chip + (core() if keep else 1 - core())


def moments_kernel(snps, chip, keep, opening, taken, given, geno_ref, *rest):
    rest = list(rest)
    if opening:
        bits_ref, trait_ref, kept_ref, sums_ref, local_ref, left_ref = rest[:6]
        rest = rest[6:]
    else:
        raw_in = rest.pop(0) if taken else None
        left_ref, kept_ref, sums_ref, local_ref = rest[:4]
        rest = rest[4:]
    raw_out = rest.pop(0) if given is not None else None
    slots, rows, block = kept_ref.shape
    fetched = slots - taken
    devices = -(-snps // block)
    tail = snps - (devices - 1) * block
    span = sums_ref.shape[2] * 2 // 3

    def copy(owner, target, semaphore, width):
        start = pl.multiple_of(owner * block, LANES)
        return pltpu.make_async_copy(
            geno_ref.at[:, pl.ds(start, width)], target.at[:, pl.ds(0, width)], semaphore
        )

    def whole_or_tail(owner, target, semaphore, act):
        if tail == block:
            act(copy(owner, target, semaphore, block))
        else:
            last = owner == devices - 1
            pl.when(last)(lambda: act(copy(owner, target, semaphore, tail)))
            pl.when(jnp.logical_not(last))(lambda: act(copy(owner, target, semaphore, block)))

    if fetched:
        buffer, arrived = rest[:2]
        rest = rest[2:]

        def fetch(index, act):
            owner = owner_of(chip + index + taken, keep)
            whole_or_tail(owner, buffer.at[index], arrived.at[index], act)

    if raw_out is not None:
        raw_arrived = rest.pop(0)

    if opening:
        bits, trait, small = rest[:3]
        bits_copy = pltpu.make_async_copy(bits_ref, bits, small.at[0])
        trait_copy = pltpu.make_async_copy(trait_ref, trait, small.at[1])
        bits_copy.start()
        trait_copy.start()
    if fetched:
        pl.loop(0, fetched)(lambda index: fetch(index, lambda c: c.start()))
    if raw_out is not None:
        whole_or_tail(owner_of(*given), raw_out, raw_arrived, lambda c: c.start())
    if opening:
        bits_copy.wait()
        trait_copy.wait()
        left_ref[...] = jnp.zeros_like(left_ref)
        left_ref[0:PROBES] = (2 * bits[...] - 1).astype(F32)
        left_ref[TRAIT : TRAIT + 1] = trait[...].astype(F32).reshape(1, rows)
        left_ref[ONES : ONES + 1] = jnp.ones((1, rows), F32)
    left = left_ref[...]
    base = jnp.sum(left, axis=1, keepdims=True)
    left = left.astype(BF16)
    row = rows_iota(ROWS)

    def with_low(value):
        high = value[TRAIT : TRAIT + 1]
        return jnp.where(row == TRAIT + 1, high - high.astype(BF16).astype(F32), value)

    ends = jnp.broadcast_to(with_low(base), (ROWS, span - block))

    def work(slot, source):
        squares = []
        for at in range(0, block, PIECE):
            lanes = slice(at, min(at + PIECE, block))
            square = 0.0
            for r in range(0, rows, 16):
                dose = source[r : r + 16, lanes].astype(F32)
                kept_ref[slot, r : r + 16, lanes] = dose.astype(BF16)
                dose = dose * dose
                square = square + (dose[:8] + dose[8:])
            squares.append(jnp.sum(square, axis=0, keepdims=True))
        total = jnp.dot(left, kept_ref[slot], preferred_element_type=F32) - base
        ones = total[ONES : ONES + 1]
        local_ref[slot, 0:1] = ones
        local_ref[slot, 1:2] = jnp.concatenate(squares, axis=1) - 2.0 * ones - rows
        high, low = pack_sums(jnp.concatenate([with_low(total), ends], axis=1))
        sums_ref[slot, :, :span] = high.astype(BF16)
        sums_ref[slot, :, span:] = low.astype(BF16)

    if taken:
        work(0, raw_in)
    if fetched:

        @pl.loop(0, fetched)
        def _(index):
            fetch(index, lambda c: c.wait())
            work(index + taken, buffer.at[index])

    if raw_out is not None:
        whole_or_tail(owner_of(*given), raw_out, raw_arrived, lambda c: c.wait())


def cores_kernel(left_ref, here_ref, away_ref, out_ref, left_out):
    left_out[...] = left_ref[...]
    for slot in range(out_ref.shape[0]):
        total = here_ref[slot].astype(F32) + away_ref[slot].astype(F32)
        out_ref[slot] = total.astype(BF16)


def weights_kernel(chip, token_ref, mean_ref, scale_ref, *refs):
    parts, (u_ref, trait_ref) = refs[:-2], refs[-2:]
    slots, _, block = trait_ref.shape
    width = u_ref.shape[2] - block
    for slot in range(slots):
        here = pl.ds(pl.multiple_of(owner_of(chip + slot, True) * block, LANES), block)
        total = [part[slot].astype(F32) for part in parts]
        total = tree_sum(total[:1] + total[:0:-1])
        shift = mean_ref[:, here] - 1.0
        inverse = 1.0 / scale_ref[:, here]
        high, low = [
            (part[:, :block] - part[:, block : block + 1] * shift) * inverse
            for part in unpack_sums(total)
        ]
        trait_ref[slot] = low[2:3] + low[3:4]
        high, low = [part.astype(BF16).astype(F32) * inverse for part in (high, low)]
        low = jnp.concatenate([low, jnp.zeros((SUBLANES, 4 * width - block), F32)], axis=1)
        folded = low[:, :width]
        for j in range(1, 4):
            turned = pltpu.roll(low[:, j * width : (j + 1) * width], 2 * j, 0)
            folded = jnp.where(rows_iota(SUBLANES) < 2 * j, folded, turned)
        u_ref[slot, :, :block] = high.astype(BF16)
        u_ref[slot, :, block:] = folded.astype(BF16)


def stats_kernel(own_bins, groups, flat_ref, mean_ref, scale_ref, label_ref, *rest):
    rest, (out_ref, field_ref) = list(rest[:-2]), rest[-2:]
    rows = flat_ref.shape[1] // PROBES
    bins = rows_iota(SUBLANES)
    trace = jnp.zeros((SUBLANES, 1), F32)
    quad = jnp.zeros((SUBLANES, 1), F32)
    for chip, keep in groups:
        local_ref = rest.pop(0)
        trait_ref = rest.pop(0) if keep else None
        slots, _, block = local_ref.shape
        for slot in range(slots):
            owner = owner_of(chip + slot, keep)
            here = pl.ds(pl.multiple_of(owner * block, LANES), block)
            member = label_ref[:, here] - lax.axis_index("bin") * own_bins == bins
            member = member & (bins < own_bins)
            shift = mean_ref[:, here] - 1.0
            inverse = 1.0 / scale_ref[:, here]
            square = local_ref[slot, 1:2] - 2.0 * shift * local_ref[slot, 0:1] + rows * shift * shift
            square = square * (inverse * inverse)
            trace += jnp.sum(jnp.where(member, square, 0.0), axis=1, keepdims=True)
            if keep:
                mine = member & (owner == lax.axis_index("ind"))
                trait = trait_ref[slot]
                quad += jnp.sum(jnp.where(mine, trait * trait, 0.0), axis=1, keepdims=True)
    lane = lax.broadcasted_iota(jnp.int32, (SUBLANES, LANES), 1)
    out_ref[...] = jnp.where(lane == TRACE_LANE, trace, jnp.where(lane == QUAD_LANE, quad, 0.0))
    flat = flat_ref[...].astype(F32)
    for b in range(PROBES):
        field_ref[b] = flat[:own_bins, b * rows : (b + 1) * rows].astype(BF16)


def field_kernel(own_bins, blocks, sources, started, last, *refs):
    refs = list(refs)
    mean_ref, label_ref = refs[:2]
    kept_refs, refs = refs[2 : 2 + sources], refs[2 + sources :]
    u_refs, refs = refs[:sources], refs[sources:]
    rows, block = kept_refs[0].shape[1:]
    bins = rows_iota(SUBLANES)
    if started:
        acc, offset, number = [ref[...] for ref in refs[:3]]
        refs = refs[3:]
    else:
        acc = jnp.zeros((rows, PROBES * SUBLANES), F32)
        offset = jnp.zeros((PROBES * SUBLANES, LANES), F32)
        number = jnp.zeros((SUBLANES, LANES), F32)
    for chip, keep, source, slot in blocks:
        start = owner_of(chip, keep) * block
        u = u_refs[source][slot].astype(F32)
        lines = [u[b : b + 1, :block] for b in range(SUBLANES)]
        for b in range(PROBES - SUBLANES):
            line = [u[2 * j + b : 2 * j + b + 1, block:] for j in range(4)]
            lines.append(jnp.concatenate(line, axis=1)[:, :block])
        for at in range(0, block, DOT_PIECE):
            width = min(DOT_PIECE, block - at)
            here = pl.ds(pl.multiple_of(start + at, LANES), width)
            member = label_ref[:, here] - lax.axis_index("bin") * own_bins == bins
            member = member & (bins < own_bins)
            mean = mean_ref[:, here]
            spread = [jnp.where(member, line[:, at : at + width], 0.0) for line in lines]
            offset += jnp.concatenate([fold_lanes(value * mean) for value in spread], axis=0)
            number += fold_lanes(jnp.where(member, 1.0, 0.0))
            acc += lax.dot_general(
                kept_refs[source][slot, :, at : at + width],
                jnp.concatenate(spread, axis=0).astype(BF16),
                (((1,), (1,)), ((), ())),
                preferred_element_type=F32,
            )
    if not last:
        for ref, value in zip(refs, (acc, offset, number)):
            ref[...] = value
        return
    flat_ref, count_ref = refs
    acc = jnp.concatenate([acc, jnp.zeros((rows, LANES - acc.shape[1]), F32)], axis=1)
    acc = jnp.transpose(acc)[: PROBES * SUBLANES] - jnp.sum(offset, axis=1, keepdims=True)
    number = jnp.sum(number, axis=1, keepdims=True)
    count_ref[...] = jnp.broadcast_to(number, count_ref.shape)
    inverse = 1.0 / jnp.maximum(number, 1.0)
    flat = [acc[b * SUBLANES : (b + 1) * SUBLANES] * inverse for b in range(PROBES)]
    flat_ref[...] = jnp.concatenate(flat, axis=1).astype(BF16)


def relay_kernel(token_ref, value_ref, out_ref):
    out_ref[...] = value_ref[...]


def weights_field_kernel(own_bins, chip, count, token_ref, mean_ref, scale_ref, label_ref, kept_ref, *refs):
    parts, (u_ref, trait_ref), terms = refs[:-5], refs[-5:-3], refs[-3:]
    weights_kernel(chip, token_ref, mean_ref, scale_ref, *parts, u_ref, trait_ref)
    blocks = [(chip + slot, True, 0, slot) for slot in range(count)]
    field_kernel(own_bins, blocks, 1, False, False, mean_ref, label_ref, kept_ref, u_ref, *terms)


def pair_kernel(stats_ref, *rest):
    flats, out_ref = rest[-2::-1], rest[-1]
    everyone = [flat[...].astype(F32) for flat in flats]
    everyone += [jnp.zeros_like(everyone[0])] * (LANES // SUBLANES - len(flats))
    out_ref[...] = stats_ref[...] + lax.dot_general(
        flats[0][...],
        jnp.concatenate(everyone, axis=0).astype(BF16),
        (((1,), (1,)), ((), ())),
        preferred_element_type=F32,
    )


def final_kernel(own_bins, n_bin, pairs, total_rows, count_ref, own_ref, common_ref, *rest):
    mine, theirs, outs = rest[:pairs], rest[pairs : 2 * pairs + 1], rest[2 * pairs + 1 :]
    pair_ref, trace_ref, quad_ref = outs
    terms = [own_ref[...]]
    even = core() == 0
    for ref, other in zip(mine, theirs):
        terms.append(jnp.where(even, ref[...], other[...]))
        terms.append(jnp.where(even, other[...], ref[...]))
    terms.append(common_ref[...] + theirs[pairs][...])
    total = tree_sum(terms)
    row = lax.broadcasted_iota(jnp.int32, (SUBLANES, LANES), 0)
    lane = lax.broadcasted_iota(jnp.int32, (SUBLANES, LANES), 1)
    pair = jnp.zeros_like(total)
    for slot in range(n_bin):
        start = slot * SUBLANES
        part = jnp.where((lane >= start) & (lane < start + own_bins), total, 0.0)
        shift = (lax.axis_index("bin") ^ slot) * own_bins - start + LANES
        pair = pair + pltpu.roll(part, lax.rem(shift, LANES), 1)
    pair_ref[...] = pair[:own_bins, :BINS] / (PROBES * total_rows)
    scaled = total / (count_ref[...] * total_rows)
    for ref, column in ((trace_ref, TRACE_LANE), (quad_ref, QUAD_LANE)):
        turned = jnp.where(row == lane, scaled[:, column : column + 1], 0.0)
        ref[...] = jnp.sum(turned, axis=0, keepdims=True)[:, :own_bins]


def swap(value, axis, size, distance):
    return lax.ppermute(value, axis, [(i, i ^ distance) for i in range(size)])


def swap_mixed(value, size, pair):
    return lax.ppermute(value, "ind", [(i, i ^ pair[i % 2]) for i in range(size)])


def chosen_pairs(distances):
    return list(zip(distances[:-1:2], distances[1:-1:2])), distances[-1]


def in_vmem():
    return pl.BlockSpec(memory_space=VMEM)


def in_hbm():
    return pl.BlockSpec(memory_space=pltpu.HBM)


def params(mib):
    return pltpu.CompilerParams(vmem_limit_bytes=mib * MIB)


def cost(flops, moved):
    return pl.CostEstimate(flops=flops, bytes_accessed=moved, transcendentals=0)


def shards(genotype, snp_mean, snp_scale, snp_label, probe_bits, phenotype):
    n = lax.axis_size("ind")
    n_bin = lax.axis_size("bin")
    chips = n // 2
    own_bins = BINS // n_bin
    rows, snps = genotype.shape
    tiles = -(-snps // LANES)
    block_tiles = -(-tiles // n)
    block = block_tiles * LANES
    span = block + LANES * (2 - block_tiles % 2)
    folded = block + -(-block_tiles // 4) * LANES
    whole = n * block
    mean, scale, label = snp_mean, snp_scale, snp_label
    if whole != snps:
        mean = jnp.pad(mean, (0, whole - snps), constant_values=1.0)
        scale = jnp.pad(scale, (0, whole - snps), constant_values=1.0)
        label = jnp.pad(label, (0, whole - snps), constant_values=-1)
    mean, scale, label = mean[None, :], scale[None, :], label[None, :]
    genotype, probe_bits, phenotype = [
        pltpu.with_memory_space_constraint(value, pltpu.HBM)
        for value in (genotype, probe_bits, phenotype)
    ]

    def moments(chip, slots, keep, given, extra, name):
        opening = extra[0] is probe_bits
        taken = int(not opening and extra[0] is not None)
        extra = [value for value in extra if value is not None]
        fetched = slots - taken
        out_shape = [
            jax.ShapeDtypeStruct((slots, rows, block), BF16),
            jax.ShapeDtypeStruct((slots, SUBLANES, span * 3 // 2), BF16),
            jax.ShapeDtypeStruct((slots, 2, block), F32),
        ]
        if opening:
            out_shape.append(jax.ShapeDtypeStruct((ROWS, rows), F32))
        if given is not None:
            out_shape.append(jax.ShapeDtypeStruct((rows, block), jnp.int32))
        scratch = []
        if fetched:
            scratch += [VMEM((fetched, rows, block), jnp.int32), pltpu.SemaphoreType.DMA((fetched,))]
        if given is not None:
            scratch.append(pltpu.SemaphoreType.DMA)
        if opening:
            scratch += [
                VMEM(probe_bits.shape, jnp.int32),
                VMEM((rows,), BF16),
                pltpu.SemaphoreType.DMA((2,)),
            ]
        return pl.pallas_call(
            functools.partial(moments_kernel, snps, chip, keep, opening, taken, given),
            in_specs=[in_hbm()] + [in_hbm() if opening else in_vmem()] * len(extra),
            out_specs=[in_vmem()] * len(out_shape),
            scratch_shapes=scratch,
            out_shape=out_shape,
            cost_estimate=cost(1, 4 * rows * block * slots if slots > 1 else 1),
            compiler_params=params(20),
            name=name,
        )(genotype, *extra)

    others = list(range(n - 2, 0, -2))
    split = max(chips * 3 // 4, 1)

    def plain(kernel, operands, out_shape, name, **options):
        return pl.pallas_call(
            kernel,
            in_specs=[in_vmem()] * len(operands),
            out_specs=[in_vmem()] * len(out_shape),
            out_shape=out_shape,
            compiler_params=params(20),
            name=name,
            **options,
        )(*operands)

    def cores(left, here, away):
        return plain(
            cores_kernel,
            (left, here, away),
            [jax.ShapeDtypeStruct(here.shape, BF16), jax.ShapeDtypeStruct(left.shape, F32)],
            "cores",
        )

    def spread(value):
        return [value] + [swap(value, "ind", n, d) for d in others]

    late = chips - split
    kept_a_give, give, local_a_give, left, raw = moments(
        0, split, False, (0, True), (probe_bits, phenotype), "moments_a_give"
    )
    give = swap(give, "ind", n, 1)
    kept_a_keep, keep, local_a_keep, raw = moments(
        0, split, True, (split, False), (raw, left), "moments_a_keep"
    )
    sum_a, left = cores(left, keep, give)
    parts_a = spread(sum_a)
    kept_b_give, give, local_b_give, raw = moments(
        split, late, False, (split, True), (raw, left), "moments_b_give"
    )
    give = swap(give, "ind", n, 1)
    kept_b_keep, keep, local_b_keep = moments(
        split, late, True, None, (raw, left), "moments_b_keep"
    )
    sum_b, token = cores(left, keep, give)
    parts_b = spread(sum_b)
    number_shape = jax.ShapeDtypeStruct((SUBLANES, LANES), F32)
    term_shape = [
        jax.ShapeDtypeStruct((rows, PROBES * SUBLANES), F32),
        jax.ShapeDtypeStruct((PROBES * SUBLANES, LANES), F32),
        number_shape,
    ]
    end_shape = [jax.ShapeDtypeStruct((SUBLANES, PROBES * rows), BF16), number_shape]

    def fields(kept, blocks, us, terms, last=False):
        return plain(
            functools.partial(field_kernel, own_bins, blocks, len(kept), bool(terms), last),
            (mean, label, *kept, *us, *terms),
            end_shape if last else term_shape,
            "field",
            cost_estimate=cost(0, 0),
        )

    def listed(chip, slots, keep, source):
        return [(chip + slot, keep, source, slot) for slot in range(slots)]

    def weights_shape(slots):
        return [
            jax.ShapeDtypeStruct((slots, SUBLANES, folded), BF16),
            jax.ShapeDtypeStruct((slots, 1, block), F32),
        ]

    u_a, trait_a, *terms = plain(
        functools.partial(weights_field_kernel, own_bins, 0, split - 1),
        (token, mean, scale, label, kept_a_keep, *parts_a),
        weights_shape(split) + term_shape,
        "weights_field",
    )
    u_b, trait_b = plain(
        functools.partial(weights_kernel, split),
        (terms[2], mean, scale, *parts_b),
        weights_shape(late),
        "weights",
    )
    u_b_other = swap(u_b, "ind", n, 1)
    (u_a,) = plain(
        relay_kernel, (trait_b, u_a), [jax.ShapeDtypeStruct(u_a.shape, u_a.dtype)], "relay"
    )
    u_a_other = swap(u_a, "ind", n, 1)
    blocks = [(split - 1, True, 0, split - 1)] + listed(split, late, True, 1)
    terms = fields([kept_a_keep, kept_b_keep], blocks, [u_a, u_b], terms)
    terms = fields([kept_a_give], listed(0, split, False, 0), [u_a_other], terms)
    flat, number = fields(
        [kept_b_give], listed(split, late, False, 0), [u_b_other], terms, last=True
    )

    flats = [flat] + [swap(flat, "bin", n_bin, d) for d in range(1, n_bin)]
    groups = [(0, False), (0, True), (split, False), (split, True)]
    stats, field = plain(
        functools.partial(stats_kernel, own_bins, groups),
        (
            flat, mean, scale, label,
            local_a_give, local_a_keep, trait_a, local_b_give, local_b_keep, trait_b,
        ),
        [number_shape, jax.ShapeDtypeStruct((PROBES, own_bins, rows), BF16)],
        "stats",
    )
    (part,) = plain(pair_kernel, (stats, *flats[::-1]), [number_shape], "pair")
    pairs, common = chosen_pairs(list(range(2, n, 2)))
    part_common = swap(part, "ind", n, common)
    part = part + swap(part, "ind", n, 1)
    mine = [swap_mixed(part, n, pair) for pair in pairs]
    theirs = [swap(value, "ind", n, 1) for value in mine + [part_common]]
    pair, trace, quad = plain(
        functools.partial(final_kernel, own_bins, n_bin, len(pairs), rows * n),
        (number, part, part_common, *mine, *theirs),
        [
            jax.ShapeDtypeStruct((own_bins, BINS), F32),
            jax.ShapeDtypeStruct((1, own_bins), F32),
            jax.ShapeDtypeStruct((1, own_bins), F32),
        ],
        "final",
    )
    return jnp.transpose(field, (1, 0, 2)), pair, trace[0], quad[0]


def solution(mesh):
    placed = (P("ind", "bin"), P("bin"), P("bin"), P("bin"), P(None, "ind"), P("ind"))
    return jax.shard_map(
        shards,
        mesh=mesh,
        in_specs=placed,
        out_specs=(P("bin", None, "ind"), P("bin", None), P("bin"), P("bin")),
        check_vma=False,
    )
```

```python
import functools

import jax
import jax.numpy as jnp
from jax import lax
from jax.experimental import pallas as pl
from jax.experimental.pallas import tpu as pltpu
from jax.sharding import PartitionSpec as P

BINS = 24
PROBES = 10
LANES = 128
SUBLANES = 8
ROWS = 16
TRAIT, ONES = PROBES, PROBES + 1
TRACE_LANE, QUAD_LANE = LANES - 2, LANES - 1
PIECE = 640
DOT_PIECE = 768
F32 = jnp.float32
BF16 = jnp.bfloat16
VMEM = pltpu.VMEM
MIB = 1 << 20


def core():
    return lax.rem(lax.axis_index("ind"), 2)


def fold_lanes(value):
    return tree_sum([value[:, at : at + LANES] for at in range(0, value.shape[1], LANES)])


def rows_iota(count, width=1):
    return lax.broadcasted_iota(jnp.int32, (count, width), 0)


def tree_sum(terms):
    terms = list(terms)
    while len(terms) > 1:
        pairs = [a + b for a, b in zip(terms[::2], terms[1::2])]
        terms = pairs + terms[len(pairs) * 2 :]
    return terms[0]


def pack_sums(value):
    half = value.shape[1] // 2
    low = value[SUBLANES:]
    turned = pltpu.roll(low[:, half:], 4, 0)
    low = jnp.where(rows_iota(SUBLANES) < 4, low[:, :half], turned)
    return value[:SUBLANES], low


def unpack_sums(value):
    span = value.shape[1] * 2 // 3
    low = value[:, span:]
    return value[:, :span], jnp.concatenate([low, pltpu.roll(low, 4, 0)], axis=1)


def moments_kernel(snps, distances, opening, taken, given, geno_ref, *rest):
    rest = list(rest)
    if opening:
        bits_ref, trait_ref, kept_ref, sums_ref, local_ref, left_ref = rest[:6]
        rest = rest[6:]
    else:
        raw_in = rest.pop(0) if taken else None
        left_ref, kept_ref, sums_ref, local_ref = rest[:4]
        rest = rest[4:]
    raw_out = rest.pop(0) if given is not None else None
    slots, rows, block = kept_ref.shape
    fetched = slots - taken
    devices = -(-snps // block)
    tail = snps - (devices - 1) * block
    span = sums_ref.shape[2] * 2 // 3

    def copy(distance, target, semaphore, width):
        start = pl.multiple_of((lax.axis_index("ind") ^ distance) * block, LANES)
        return pltpu.make_async_copy(
            geno_ref.at[:, pl.ds(start, width)], target.at[:, pl.ds(0, width)], semaphore
        )

    def whole_or_tail(distance, target, semaphore, act):
        if tail == block:
            act(copy(distance, target, semaphore, block))
        else:
            last = (lax.axis_index("ind") ^ distance) == devices - 1
            pl.when(last)(lambda: act(copy(distance, target, semaphore, tail)))
            pl.when(jnp.logical_not(last))(lambda: act(copy(distance, target, semaphore, block)))

    square_ref = rest.pop(0)
    if fetched:
        buffer, arrived = rest[:2]
        rest = rest[2:]

        def fetch(index, act):
            distance = distances[0] - 2 * (index + taken)
            whole_or_tail(distance, buffer.at[index], arrived.at[index], act)

    if raw_out is not None:
        raw_arrived = rest.pop(0)

    if opening:
        bits, trait, small = rest[:3]
        bits_copy = pltpu.make_async_copy(bits_ref, bits, small.at[0])
        trait_copy = pltpu.make_async_copy(trait_ref, trait, small.at[1])
        bits_copy.start()
        trait_copy.start()
    if fetched:
        pl.loop(0, fetched)(lambda index: fetch(index, lambda c: c.start()))
    if raw_out is not None:
        whole_or_tail(given, raw_out, raw_arrived, lambda c: c.start())
    if opening:
        bits_copy.wait()
        trait_copy.wait()
        left_ref[...] = jnp.zeros_like(left_ref)
        left_ref[0:PROBES] = (2 * bits[...] - 1).astype(F32)
        left_ref[TRAIT : TRAIT + 1] = trait[...].astype(F32).reshape(1, rows)
        left_ref[ONES : ONES + 1] = jnp.ones((1, rows), F32)
    left = left_ref[...]
    base = jnp.sum(left, axis=1, keepdims=True)
    left = left.astype(BF16)
    row = rows_iota(ROWS)

    def with_low(value):
        high = value[TRAIT : TRAIT + 1]
        return jnp.where(row == TRAIT + 1, high - high.astype(BF16).astype(F32), value)

    ends = jnp.broadcast_to(with_low(base), (ROWS, span - block))

    def work(slot, source):
        def piece(at, width):
            lanes = pl.ds(at, width)
            square = 0.0
            for r in range(0, rows, 16):
                dose = source[r : r + 16, lanes].astype(F32)
                kept_ref[slot, r : r + 16, lanes] = dose.astype(BF16)
                dose = dose * dose
                square = square + (dose[:8] + dose[8:])
            square_ref[:, lanes] = jnp.sum(square, axis=0, keepdims=True)

        @pl.loop(0, block // PIECE)
        def _(index):
            piece(pl.multiple_of(index * PIECE, LANES), PIECE)

        if block % PIECE:
            piece(block - block % PIECE, block % PIECE)
        total = jnp.dot(left, kept_ref[slot], preferred_element_type=F32) - base
        ones = total[ONES : ONES + 1]
        local_ref[slot, 0:1] = ones
        local_ref[slot, 1:2] = square_ref[...] - 2.0 * ones - rows
        high, low = pack_sums(jnp.concatenate([with_low(total), ends], axis=1))
        sums_ref[slot, :, :span] = high.astype(BF16)
        sums_ref[slot, :, span:] = low.astype(BF16)

    if taken:
        work(0, raw_in)
    if fetched:

        @pl.loop(0, fetched)
        def _(index):
            fetch(index, lambda c: c.wait())
            work(index + taken, buffer.at[index])

    if raw_out is not None:
        whole_or_tail(given, raw_out, raw_arrived, lambda c: c.wait())


def cores_kernel(left_ref, here_ref, away_ref, *outs):
    outs, left_out = outs[:-1], outs[-1]
    left_out[...] = left_ref[...]
    for index, out in enumerate(outs):
        out[...] = (here_ref[index].astype(F32) + away_ref[index].astype(F32)).astype(BF16)


def relay_kernel(token_ref, value_ref, out_ref):
    out_ref[...] = value_ref[...]


def weights_kernel(mean_ref, scale_ref, own_ref, near_ref, *refs):
    parts, (u_ref, trait_ref) = refs[:-2], refs[-2:]
    block = trait_ref.shape[1]
    width = u_ref.shape[1] - block
    here = pl.ds(pl.multiple_of(lax.axis_index("ind") * block, LANES), block)
    parts = [own_ref[0], near_ref[0]] + [part[...] for part in parts]
    total = tree_sum([part.astype(F32) for part in parts])
    shift = mean_ref[:, here] - 1.0
    inverse = 1.0 / scale_ref[:, here]
    high, low = [
        (part[:, :block] - part[:, block : block + 1] * shift) * inverse
        for part in unpack_sums(total)
    ]
    trait_ref[...] = low[2:3] + low[3:4]
    high, low = [part.astype(BF16).astype(F32) * inverse for part in (high, low)]
    low = jnp.concatenate([low, jnp.zeros((SUBLANES, 4 * width - block), F32)], axis=1)
    folded = low[:, :width]
    for j in range(1, 4):
        turned = pltpu.roll(low[:, j * width : (j + 1) * width], 2 * j, 0)
        folded = jnp.where(rows_iota(SUBLANES) < 2 * j, folded, turned)
    u_ref[:, :block] = high.astype(BF16)
    u_ref[:, block:] = folded.astype(BF16)


def stats_kernel(own_bins, order, flat_ref, mean_ref, scale_ref, label_ref, trait_ref, *rest):
    locals_, (out_ref, field_ref) = rest[:-2], rest[-2:]
    block = trait_ref.shape[1]
    rows = order[0]
    bins = rows_iota(SUBLANES)

    def member_of(owner):
        here = pl.ds(pl.multiple_of(owner * block, LANES), block)
        member = label_ref[:, here] - lax.axis_index("bin") * own_bins == bins
        return here, member & (bins < own_bins)

    trace = jnp.zeros((SUBLANES, 1), F32)
    for ref, distances in zip(locals_, order[1]):
        for slot, distance in enumerate(distances):
            here, member = member_of(lax.axis_index("ind") ^ distance)
            shift = mean_ref[:, here] - 1.0
            inverse = 1.0 / scale_ref[:, here]
            square = ref[slot, 1:2] - 2.0 * shift * ref[slot, 0:1] + rows * shift * shift
            square = square * (inverse * inverse)
            trace += jnp.sum(jnp.where(member, square, 0.0), axis=1, keepdims=True)
    _, member = member_of(lax.axis_index("ind"))
    trait = trait_ref[...]
    quad = jnp.sum(jnp.where(member, trait * trait, 0.0), axis=1, keepdims=True)
    lane = lax.broadcasted_iota(jnp.int32, (SUBLANES, LANES), 1)
    out_ref[...] = jnp.where(lane == TRACE_LANE, trace, jnp.where(lane == QUAD_LANE, quad, 0.0))
    flat = flat_ref[...].astype(F32)
    for b in range(PROBES):
        field_ref[b] = flat[:own_bins, b * rows : (b + 1) * rows].astype(BF16)


def field_kernel(own_bins, blocks, sources, started, last, *refs):
    refs = list(refs)
    mean_ref, label_ref = refs[:2]
    kept_refs, refs = refs[2 : 2 + sources], refs[2 + sources :]
    u_refs, refs = refs[: len(blocks)], refs[len(blocks) :]
    rows, block = kept_refs[0].shape[1:]
    bins = rows_iota(SUBLANES)
    if started:
        acc, offset, number = [ref[...] for ref in refs[:3]]
        refs = refs[3:]
    else:
        acc = jnp.zeros((rows, PROBES * SUBLANES), F32)
        offset = jnp.zeros((PROBES * SUBLANES, LANES), F32)
        number = jnp.zeros((SUBLANES, LANES), F32)
    for index, (slot, distance) in enumerate(blocks):
        start = (lax.axis_index("ind") ^ distance) * block
        u = u_refs[index][...].astype(F32)
        lines = [u[b : b + 1, :block] for b in range(SUBLANES)]
        for b in range(PROBES - SUBLANES):
            line = [u[2 * j + b : 2 * j + b + 1, block:] for j in range(4)]
            lines.append(jnp.concatenate(line, axis=1)[:, :block])
        for at in range(0, block, DOT_PIECE):
            width = min(DOT_PIECE, block - at)
            here = pl.ds(pl.multiple_of(start + at, LANES), width)
            member = label_ref[:, here] - lax.axis_index("bin") * own_bins == bins
            member = member & (bins < own_bins)
            mean = mean_ref[:, here]
            spread = [jnp.where(member, line[:, at : at + width], 0.0) for line in lines]
            offset += jnp.concatenate([fold_lanes(value * mean) for value in spread], axis=0)
            number += fold_lanes(jnp.where(member, 1.0, 0.0))
            acc += lax.dot_general(
                kept_refs[index if sources > 1 else 0][slot, :, at : at + width],
                jnp.concatenate(spread, axis=0).astype(BF16),
                (((1,), (1,)), ((), ())),
                preferred_element_type=F32,
            )
    if not last:
        for ref, value in zip(refs, (acc, offset, number)):
            ref[...] = value
        return
    flat_ref, count_ref = refs
    acc = jnp.concatenate([acc, jnp.zeros((rows, LANES - acc.shape[1]), F32)], axis=1)
    acc = jnp.transpose(acc)[: PROBES * SUBLANES] - jnp.sum(offset, axis=1, keepdims=True)
    number = jnp.sum(number, axis=1, keepdims=True)
    count_ref[...] = jnp.broadcast_to(number, count_ref.shape)
    inverse = 1.0 / jnp.maximum(number, 1.0)
    flat = [acc[b * SUBLANES : (b + 1) * SUBLANES] * inverse for b in range(PROBES)]
    flat_ref[...] = jnp.concatenate(flat, axis=1).astype(BF16)


def pair_kernel(stats_ref, *rest):
    flats, out_ref = rest[:-1], rest[-1]
    everyone = [flat[...].astype(F32) for flat in flats]
    everyone += [jnp.zeros_like(everyone[0])] * (LANES // SUBLANES - len(flats))
    out_ref[...] = stats_ref[...] + lax.dot_general(
        flats[0][...],
        jnp.concatenate(everyone, axis=0).astype(BF16),
        (((1,), (1,)), ((), ())),
        preferred_element_type=F32,
    )


def final_kernel(own_bins, n_bin, pairs, total_rows, count_ref, own_ref, common_ref, *rest):
    mine, theirs, outs = rest[:pairs], rest[pairs : 2 * pairs + 1], rest[2 * pairs + 1 :]
    pair_ref, trace_ref, quad_ref = outs
    terms = [own_ref[...]]
    even = core() == 0
    for ref, other in zip(mine, theirs):
        terms.append(jnp.where(even, ref[...], other[...]))
        terms.append(jnp.where(even, other[...], ref[...]))
    terms.append(common_ref[...] + theirs[pairs][...])
    total = tree_sum(terms)
    row = lax.broadcasted_iota(jnp.int32, (SUBLANES, LANES), 0)
    lane = lax.broadcasted_iota(jnp.int32, (SUBLANES, LANES), 1)
    pair = jnp.zeros_like(total)
    for slot in range(n_bin):
        start = slot * SUBLANES
        part = jnp.where((lane >= start) & (lane < start + own_bins), total, 0.0)
        shift = (lax.axis_index("bin") ^ slot) * own_bins - start + LANES
        pair = pair + pltpu.roll(part, lax.rem(shift, LANES), 1)
    pair_ref[...] = pair[:own_bins, :BINS] / (PROBES * total_rows)
    scaled = total / (count_ref[...] * total_rows)
    for ref, column in ((trace_ref, TRACE_LANE), (quad_ref, QUAD_LANE)):
        turned = jnp.where(row == lane, scaled[:, column : column + 1], 0.0)
        ref[...] = jnp.sum(turned, axis=0, keepdims=True)[:, :own_bins]


def swap(value, axis, size, distance):
    return lax.ppermute(value, axis, [(i, i ^ distance) for i in range(size)])


def swap_mixed(value, size, pair):
    return lax.ppermute(value, "ind", [(i, i ^ pair[i % 2]) for i in range(size)])


def chosen_pairs(distances):
    return list(zip(distances[:-1:2], distances[1:-1:2])), distances[-1]


def in_vmem():
    return pl.BlockSpec(memory_space=VMEM)


def in_hbm():
    return pl.BlockSpec(memory_space=pltpu.HBM)


def params(mib):
    return pltpu.CompilerParams(vmem_limit_bytes=mib * MIB)


def cost(flops, moved):
    return pl.CostEstimate(flops=flops, bytes_accessed=moved, transcendentals=0)


def shards(genotype, snp_mean, snp_scale, snp_label, probe_bits, phenotype):
    n = lax.axis_size("ind")
    n_bin = lax.axis_size("bin")
    chips = n // 2
    own_bins = BINS // n_bin
    rows, snps = genotype.shape
    tiles = -(-snps // LANES)
    block_tiles = -(-tiles // n)
    block = block_tiles * LANES
    span = block + LANES * (2 - block_tiles % 2)
    folded = block + -(-block_tiles // 4) * LANES
    whole = n * block
    mean, scale, label = snp_mean, snp_scale, snp_label
    if whole != snps:
        mean = jnp.pad(mean, (0, whole - snps), constant_values=1.0)
        scale = jnp.pad(scale, (0, whole - snps), constant_values=1.0)
        label = jnp.pad(label, (0, whole - snps), constant_values=-1)
    mean, scale, label = mean[None, :], scale[None, :], label[None, :]
    genotype, probe_bits, phenotype = [
        pltpu.with_memory_space_constraint(value, pltpu.HBM)
        for value in (genotype, probe_bits, phenotype)
    ]

    def moments(distances, given, extra, name):
        slots = len(distances)
        opening = extra[0] is probe_bits
        taken = int(not opening and extra[0] is not None)
        extra = [value for value in extra if value is not None]
        fetched = slots - taken
        out_shape = [
            jax.ShapeDtypeStruct((slots, rows, block), BF16),
            jax.ShapeDtypeStruct((slots, SUBLANES, span * 3 // 2), BF16),
            jax.ShapeDtypeStruct((slots, 2, block), F32),
        ]
        if opening:
            out_shape.append(jax.ShapeDtypeStruct((ROWS, rows), F32))
        if given is not None:
            out_shape.append(jax.ShapeDtypeStruct((rows, block), jnp.int32))
        scratch = [VMEM((1, block), F32)]
        if fetched:
            scratch += [VMEM((fetched, rows, block), jnp.int32), pltpu.SemaphoreType.DMA((fetched,))]
        if given is not None:
            scratch.append(pltpu.SemaphoreType.DMA)
        if opening:
            scratch += [
                VMEM(probe_bits.shape, jnp.int32),
                VMEM((rows,), BF16),
                pltpu.SemaphoreType.DMA((2,)),
            ]
        return pl.pallas_call(
            functools.partial(moments_kernel, snps, distances, opening, taken, given),
            in_specs=[in_hbm()] + [in_hbm() if opening else in_vmem()] * len(extra),
            out_specs=[in_vmem()] * len(out_shape),
            scratch_shapes=scratch,
            out_shape=out_shape,
            cost_estimate=cost(1, 4 * rows * block * slots if slots > 1 else 1),
            compiler_params=params(20),
            name=name,
        )(genotype, *extra)

    here_order = list(range(n - 2, 0, -2))
    away_order = [d + 1 for d in here_order]

    def plain(kernel, operands, out_shape, name, **options):
        return pl.pallas_call(
            kernel,
            in_specs=[in_vmem()] * len(operands),
            out_specs=[in_vmem()] * len(out_shape),
            out_shape=out_shape,
            compiler_params=params(20),
            name=name,
            **options,
        )(*operands)

    kept_away, away, local_away, left, raw = moments(
        away_order, here_order[0], (probe_bits, phenotype), "moments_away"
    )
    away = swap(away, "ind", n, 1)
    kept_here, here, local_here = moments(here_order, None, (raw, left), "moments_here")
    packed = jax.ShapeDtypeStruct((SUBLANES, span * 3 // 2), BF16)
    *sums, left = plain(
        cores_kernel,
        (left, here, away),
        [packed] * (chips - 1) + [jax.ShapeDtypeStruct(left.shape, F32)],
        "cores",
    )
    sums = [swap(value, "ind", n, d) for value, d in zip(sums, here_order)]
    kept_near, near, local_near, raw = moments([1], 0, (None, left), "moments_near")
    near = swap(near, "ind", n, 1)
    kept_own, own, local_own = moments([0], None, (raw, left), "moments_own")

    u, trait = plain(
        weights_kernel,
        (mean, scale, own, near, *sums),
        [
            jax.ShapeDtypeStruct((SUBLANES, folded), BF16),
            jax.ShapeDtypeStruct((1, block), F32),
        ],
        "weights",
    )

    number_shape = jax.ShapeDtypeStruct((SUBLANES, LANES), F32)
    term_shape = [
        jax.ShapeDtypeStruct((rows, PROBES * SUBLANES), F32),
        jax.ShapeDtypeStruct((PROBES * SUBLANES, LANES), F32),
        number_shape,
    ]
    end_shape = [jax.ShapeDtypeStruct((SUBLANES, PROBES * rows), BF16), number_shape]

    def fields(kept, blocks, us, terms, last=False):
        return plain(
            functools.partial(field_kernel, own_bins, blocks, len(kept), bool(terms), last),
            (mean, label, *kept, *us, *terms),
            end_shape if last else term_shape,
            "field",
            cost_estimate=cost(1, 1),
        )

    u_near = swap(u, "ind", n, 1)
    u_here = [swap(u, "ind", n, d) for d in here_order]
    terms = fields([kept_own, kept_near], [(0, 0), (0, 1)], [u, u_near], [])
    u_away = []
    for slot, (distance, value) in enumerate(zip(here_order, u_here)):
        shape = [jax.ShapeDtypeStruct(value.shape, value.dtype)]
        (value,) = plain(relay_kernel, (terms[2], value), shape, "relay")
        u_away.append(swap(value, "ind", n, 1))
        if slot < chips - 2:
            terms = fields([kept_here], [(slot, distance)], [value], terms)
        else:
            blocks = [(slot, distance), (0, away_order[0])]
            terms = fields([kept_here, kept_away], blocks, [value, u_away[0]], terms)
    blocks = list(enumerate(away_order))[1:]
    flat, number = fields([kept_away], blocks, u_away[1:], terms, last=True)

    flats = [flat] + [swap(flat, "bin", n_bin, d) for d in range(1, n_bin)]
    order = (rows, (away_order, here_order, [1], [0]))
    stats, field = plain(
        functools.partial(stats_kernel, own_bins, order),
        (flat, mean, scale, label, trait, local_away, local_here, local_near, local_own),
        [number_shape, jax.ShapeDtypeStruct((PROBES, own_bins, rows), BF16)],
        "stats",
    )
    (part,) = plain(pair_kernel, (stats, *flats), [number_shape], "pair")
    pairs, common = chosen_pairs(list(range(2, n, 2)))
    part_common = swap(part, "ind", n, common)
    part = part + swap(part, "ind", n, 1)
    mine = [swap_mixed(part, n, pair) for pair in pairs]
    theirs = [swap(value, "ind", n, 1) for value in mine + [part_common]]
    pair, trace, quad = plain(
        functools.partial(final_kernel, own_bins, n_bin, len(pairs), rows * n),
        (number, part, part_common, *mine, *theirs),
        [
            jax.ShapeDtypeStruct((own_bins, BINS), F32),
            jax.ShapeDtypeStruct((1, own_bins), F32),
            jax.ShapeDtypeStruct((1, own_bins), F32),
        ],
        "final",
    )
    return jnp.transpose(field, (1, 0, 2)), pair, trace[0], quad[0]


def solution(mesh):
    placed = (P("ind", "bin"), P("bin"), P("bin"), P("bin"), P(None, "ind"), P("ind"))
    return jax.shard_map(
        shards,
        mesh=mesh,
        in_specs=placed,
        out_specs=(P("bin", None, "ind"), P("bin", None), P("bin"), P("bin")),
        check_vma=False,
    )
```

```python
import functools

import jax
import jax.numpy as jnp
from jax import lax
from jax.experimental import pallas as pl
from jax.experimental.pallas import tpu as pltpu
from jax.sharding import PartitionSpec as P

BINS = 24
PROBES = 10
LANES = 128
SUBLANES = 8
ROWS = 16
TRAIT, ONES = PROBES, PROBES + 1
TRACE_LANE, QUAD_LANE = LANES - 2, LANES - 1
PIECE = 640
DOT_PIECE = 1664
F32 = jnp.float32
BF16 = jnp.bfloat16
VMEM = pltpu.VMEM
MIB = 1 << 20


def core():
    return lax.rem(lax.axis_index("ind"), 2)


def fold_lanes(value):
    return tree_sum([value[:, at : at + LANES] for at in range(0, value.shape[1], LANES)])


def rows_iota(count, width=1):
    return lax.broadcasted_iota(jnp.int32, (count, width), 0)


def tree_sum(terms):
    terms = list(terms)
    while len(terms) > 1:
        pairs = [a + b for a, b in zip(terms[::2], terms[1::2])]
        terms = pairs + terms[len(pairs) * 2 :]
    return terms[0]


def pack_sums(value):
    half = value.shape[1] // 2
    low = value[SUBLANES:]
    turned = pltpu.roll(low[:, half:], 4, 0)
    low = jnp.where(rows_iota(SUBLANES) < 4, low[:, :half], turned)
    return value[:SUBLANES], low


def unpack_sums(value):
    span = value.shape[1] * 2 // 3
    low = value[:, span:]
    return value[:, :span], jnp.concatenate([low, pltpu.roll(low, 4, 0)], axis=1)


def moments_kernel(snps, distances, opening, taken, given, geno_ref, *rest):
    rest = list(rest)
    if opening:
        bits_ref, trait_ref, kept_ref, sums_ref, local_ref, left_ref = rest[:6]
        rest = rest[6:]
    else:
        raw_in = rest.pop(0) if taken else None
        left_ref, kept_ref, sums_ref, local_ref = rest[:4]
        rest = rest[4:]
    raw_out = rest.pop(0) if given is not None else None
    slots, rows, block = kept_ref.shape
    fetched = slots - taken
    devices = -(-snps // block)
    tail = snps - (devices - 1) * block
    span = sums_ref.shape[2] * 2 // 3

    def copy(distance, target, semaphore, width):
        start = pl.multiple_of((lax.axis_index("ind") ^ distance) * block, LANES)
        return pltpu.make_async_copy(
            geno_ref.at[:, pl.ds(start, width)], target.at[:, pl.ds(0, width)], semaphore
        )

    def whole_or_tail(distance, target, semaphore, act):
        if tail == block:
            act(copy(distance, target, semaphore, block))
        else:
            last = (lax.axis_index("ind") ^ distance) == devices - 1
            pl.when(last)(lambda: act(copy(distance, target, semaphore, tail)))
            pl.when(jnp.logical_not(last))(lambda: act(copy(distance, target, semaphore, block)))

    if fetched:
        buffer, arrived = rest[:2]
        rest = rest[2:]

        def fetch(index, act):
            distance = distances[0] - 2 * (index + taken)
            whole_or_tail(distance, buffer.at[index], arrived.at[index], act)

    if raw_out is not None:
        raw_arrived = rest.pop(0)

    if opening:
        bits, trait, small = rest[:3]
        bits_copy = pltpu.make_async_copy(bits_ref, bits, small.at[0])
        trait_copy = pltpu.make_async_copy(trait_ref, trait, small.at[1])
        bits_copy.start()
        trait_copy.start()
    if fetched:
        pl.loop(0, fetched)(lambda index: fetch(index, lambda c: c.start()))
    if raw_out is not None:
        whole_or_tail(given, raw_out, raw_arrived, lambda c: c.start())
    if opening:
        bits_copy.wait()
        trait_copy.wait()
        left_ref[...] = jnp.zeros_like(left_ref)
        left_ref[0:PROBES] = (2 * bits[...] - 1).astype(F32)
        left_ref[TRAIT : TRAIT + 1] = trait[...].astype(F32).reshape(1, rows)
        left_ref[ONES : ONES + 1] = jnp.ones((1, rows), F32)
    left = left_ref[...]
    base = jnp.sum(left, axis=1, keepdims=True)
    left = left.astype(BF16)
    row = rows_iota(ROWS)

    def with_low(value):
        high = value[TRAIT : TRAIT + 1]
        return jnp.where(row == TRAIT + 1, high - high.astype(BF16).astype(F32), value)

    ends = jnp.broadcast_to(with_low(base), (ROWS, span - block))

    def work(slot, source):
        squares = []
        for at in range(0, block, PIECE):
            lanes = slice(at, min(at + PIECE, block))
            square = 0.0
            for r in range(0, rows, 16):
                dose = source[r : r + 16, lanes].astype(F32)
                kept_ref[slot, r : r + 16, lanes] = dose.astype(BF16)
                dose = dose * dose
                square = square + (dose[:8] + dose[8:])
            squares.append(jnp.sum(square, axis=0, keepdims=True))
        total = jnp.dot(left, kept_ref[slot], preferred_element_type=F32) - base
        ones = total[ONES : ONES + 1]
        local_ref[slot, 0:1] = ones
        local_ref[slot, 1:2] = jnp.concatenate(squares, axis=1) - 2.0 * ones - rows
        high, low = pack_sums(jnp.concatenate([with_low(total), ends], axis=1))
        sums_ref[slot, :, :span] = high.astype(BF16)
        sums_ref[slot, :, span:] = low.astype(BF16)

    if taken:
        work(0, raw_in)
    if fetched:

        @pl.loop(0, fetched)
        def _(index):
            fetch(index, lambda c: c.wait())
            work(index + taken, buffer.at[index])

    if raw_out is not None:
        whole_or_tail(given, raw_out, raw_arrived, lambda c: c.wait())


def cores_kernel(left_ref, here_ref, away_ref, *outs):
    outs, left_out = outs[:-1], outs[-1]
    left_out[...] = left_ref[...]
    for index, out in enumerate(outs):
        out[...] = (here_ref[index].astype(F32) + away_ref[index].astype(F32)).astype(BF16)


def relay_kernel(token_ref, value_ref, out_ref):
    out_ref[...] = value_ref[...]


def weights_kernel(mean_ref, scale_ref, own_ref, near_ref, *refs):
    parts, (u_ref, trait_ref) = refs[:-2], refs[-2:]
    block = trait_ref.shape[1]
    width = u_ref.shape[1] - block
    here = pl.ds(pl.multiple_of(lax.axis_index("ind") * block, LANES), block)
    parts = [own_ref[0], near_ref[0]] + [part[...] for part in parts]
    total = tree_sum([part.astype(F32) for part in parts])
    shift = mean_ref[:, here] - 1.0
    inverse = 1.0 / scale_ref[:, here]
    high, low = [
        (part[:, :block] - part[:, block : block + 1] * shift) * inverse
        for part in unpack_sums(total)
    ]
    trait_ref[...] = low[2:3] + low[3:4]
    high, low = [part.astype(BF16).astype(F32) * inverse for part in (high, low)]
    low = jnp.concatenate([low, jnp.zeros((SUBLANES, 4 * width - block), F32)], axis=1)
    folded = low[:, :width]
    for j in range(1, 4):
        turned = pltpu.roll(low[:, j * width : (j + 1) * width], 2 * j, 0)
        folded = jnp.where(rows_iota(SUBLANES) < 2 * j, folded, turned)
    u_ref[:, :block] = high.astype(BF16)
    u_ref[:, block:] = folded.astype(BF16)


def stats_kernel(own_bins, order, flat_ref, mean_ref, scale_ref, label_ref, trait_ref, *rest):
    locals_, (out_ref, field_ref) = rest[:-2], rest[-2:]
    block = trait_ref.shape[1]
    rows = order[0]
    bins = rows_iota(SUBLANES)

    def member_of(owner):
        here = pl.ds(pl.multiple_of(owner * block, LANES), block)
        member = label_ref[:, here] - lax.axis_index("bin") * own_bins == bins
        return here, member & (bins < own_bins)

    trace = jnp.zeros((SUBLANES, 1), F32)
    for ref, distances in zip(locals_, order[1]):
        for slot, distance in enumerate(distances):
            here, member = member_of(lax.axis_index("ind") ^ distance)
            shift = mean_ref[:, here] - 1.0
            inverse = 1.0 / scale_ref[:, here]
            square = ref[slot, 1:2] - 2.0 * shift * ref[slot, 0:1] + rows * shift * shift
            square = square * (inverse * inverse)
            trace += jnp.sum(jnp.where(member, square, 0.0), axis=1, keepdims=True)
    _, member = member_of(lax.axis_index("ind"))
    trait = trait_ref[...]
    quad = jnp.sum(jnp.where(member, trait * trait, 0.0), axis=1, keepdims=True)
    lane = lax.broadcasted_iota(jnp.int32, (SUBLANES, LANES), 1)
    out_ref[...] = jnp.where(lane == TRACE_LANE, trace, jnp.where(lane == QUAD_LANE, quad, 0.0))
    flat = flat_ref[...].astype(F32)
    for b in range(PROBES):
        field_ref[b] = flat[:own_bins, b * rows : (b + 1) * rows].astype(BF16)


def field_kernel(own_bins, blocks, sources, started, last, *refs):
    refs = list(refs)
    mean_ref, label_ref = refs[:2]
    kept_refs, refs = refs[2 : 2 + sources], refs[2 + sources :]
    u_refs, refs = refs[: len(blocks)], refs[len(blocks) :]
    rows, block = kept_refs[0].shape[1:]
    bins = rows_iota(SUBLANES)
    if started:
        acc, offset, number = [ref[...] for ref in refs[:3]]
        refs = refs[3:]
    else:
        acc = jnp.zeros((rows, PROBES * SUBLANES), F32)
        offset = jnp.zeros((PROBES * SUBLANES, LANES), F32)
        number = jnp.zeros((SUBLANES, LANES), F32)
    for index, (slot, distance) in enumerate(blocks):
        start = (lax.axis_index("ind") ^ distance) * block
        u = u_refs[index][...].astype(F32)
        lines = [u[b : b + 1, :block] for b in range(SUBLANES)]
        for b in range(PROBES - SUBLANES):
            line = [u[2 * j + b : 2 * j + b + 1, block:] for j in range(4)]
            lines.append(jnp.concatenate(line, axis=1)[:, :block])
        for at in range(0, block, DOT_PIECE):
            width = min(DOT_PIECE, block - at)
            here = pl.ds(pl.multiple_of(start + at, LANES), width)
            member = label_ref[:, here] - lax.axis_index("bin") * own_bins == bins
            member = member & (bins < own_bins)
            mean = mean_ref[:, here]
            spread = [jnp.where(member, line[:, at : at + width], 0.0) for line in lines]
            offset += jnp.concatenate([fold_lanes(value * mean) for value in spread], axis=0)
            number += fold_lanes(jnp.where(member, 1.0, 0.0))
            acc += lax.dot_general(
                kept_refs[index if sources > 1 else 0][slot, :, at : at + width],
                jnp.concatenate(spread, axis=0).astype(BF16),
                (((1,), (1,)), ((), ())),
                preferred_element_type=F32,
            )
    if not last:
        for ref, value in zip(refs, (acc, offset, number)):
            ref[...] = value
        return
    flat_ref, count_ref = refs
    acc = jnp.concatenate([acc, jnp.zeros((rows, LANES - acc.shape[1]), F32)], axis=1)
    acc = jnp.transpose(acc)[: PROBES * SUBLANES] - jnp.sum(offset, axis=1, keepdims=True)
    number = jnp.sum(number, axis=1, keepdims=True)
    count_ref[...] = jnp.broadcast_to(number, count_ref.shape)
    inverse = 1.0 / jnp.maximum(number, 1.0)
    flat = [acc[b * SUBLANES : (b + 1) * SUBLANES] * inverse for b in range(PROBES)]
    flat_ref[...] = jnp.concatenate(flat, axis=1).astype(BF16)


def pair_kernel(stats_ref, *rest):
    flats, out_ref = rest[:-1], rest[-1]
    everyone = [flat[...].astype(F32) for flat in flats]
    everyone += [jnp.zeros_like(everyone[0])] * (LANES // SUBLANES - len(flats))
    out_ref[...] = stats_ref[...] + lax.dot_general(
        flats[0][...],
        jnp.concatenate(everyone, axis=0).astype(BF16),
        (((1,), (1,)), ((), ())),
        preferred_element_type=F32,
    )


def final_kernel(own_bins, n_bin, pairs, total_rows, count_ref, own_ref, common_ref, *rest):
    mine, theirs, outs = rest[:pairs], rest[pairs : 2 * pairs + 1], rest[2 * pairs + 1 :]
    pair_ref, trace_ref, quad_ref = outs
    terms = [own_ref[...]]
    even = core() == 0
    for ref, other in zip(mine, theirs):
        terms.append(jnp.where(even, ref[...], other[...]))
        terms.append(jnp.where(even, other[...], ref[...]))
    terms.append(common_ref[...] + theirs[pairs][...])
    total = tree_sum(terms)
    row = lax.broadcasted_iota(jnp.int32, (SUBLANES, LANES), 0)
    lane = lax.broadcasted_iota(jnp.int32, (SUBLANES, LANES), 1)
    pair = jnp.zeros_like(total)
    for slot in range(n_bin):
        start = slot * SUBLANES
        part = jnp.where((lane >= start) & (lane < start + own_bins), total, 0.0)
        shift = (lax.axis_index("bin") ^ slot) * own_bins - start + LANES
        pair = pair + pltpu.roll(part, lax.rem(shift, LANES), 1)
    pair_ref[...] = pair[:own_bins, :BINS] / (PROBES * total_rows)
    scaled = total / (count_ref[...] * total_rows)
    for ref, column in ((trace_ref, TRACE_LANE), (quad_ref, QUAD_LANE)):
        turned = jnp.where(row == lane, scaled[:, column : column + 1], 0.0)
        ref[...] = jnp.sum(turned, axis=0, keepdims=True)[:, :own_bins]


def swap(value, axis, size, distance):
    return lax.ppermute(value, axis, [(i, i ^ distance) for i in range(size)])


def swap_mixed(value, size, pair):
    return lax.ppermute(value, "ind", [(i, i ^ pair[i % 2]) for i in range(size)])


def chosen_pairs(distances):
    return list(zip(distances[:-1:2], distances[1:-1:2])), distances[-1]


def in_vmem():
    return pl.BlockSpec(memory_space=VMEM)


def in_hbm():
    return pl.BlockSpec(memory_space=pltpu.HBM)


def params(mib):
    return pltpu.CompilerParams(vmem_limit_bytes=mib * MIB)


def cost(flops, moved):
    return pl.CostEstimate(flops=flops, bytes_accessed=moved, transcendentals=0)


def shards(genotype, snp_mean, snp_scale, snp_label, probe_bits, phenotype):
    n = lax.axis_size("ind")
    n_bin = lax.axis_size("bin")
    chips = n // 2
    own_bins = BINS // n_bin
    rows, snps = genotype.shape
    tiles = -(-snps // LANES)
    block_tiles = -(-tiles // n)
    block = block_tiles * LANES
    span = block + LANES * (2 - block_tiles % 2)
    folded = block + -(-block_tiles // 4) * LANES
    whole = n * block
    mean, scale, label = snp_mean, snp_scale, snp_label
    if whole != snps:
        mean = jnp.pad(mean, (0, whole - snps), constant_values=1.0)
        scale = jnp.pad(scale, (0, whole - snps), constant_values=1.0)
        label = jnp.pad(label, (0, whole - snps), constant_values=-1)
    mean, scale, label = mean[None, :], scale[None, :], label[None, :]
    genotype, probe_bits, phenotype = [
        pltpu.with_memory_space_constraint(value, pltpu.HBM)
        for value in (genotype, probe_bits, phenotype)
    ]

    def moments(distances, given, extra, name):
        slots = len(distances)
        opening = extra[0] is probe_bits
        taken = int(not opening and extra[0] is not None)
        extra = [value for value in extra if value is not None]
        fetched = slots - taken
        out_shape = [
            jax.ShapeDtypeStruct((slots, rows, block), BF16),
            jax.ShapeDtypeStruct((slots, SUBLANES, span * 3 // 2), BF16),
            jax.ShapeDtypeStruct((slots, 2, block), F32),
        ]
        if opening:
            out_shape.append(jax.ShapeDtypeStruct((ROWS, rows), F32))
        if given is not None:
            out_shape.append(jax.ShapeDtypeStruct((rows, block), jnp.int32))
        scratch = []
        if fetched:
            scratch += [VMEM((fetched, rows, block), jnp.int32), pltpu.SemaphoreType.DMA((fetched,))]
        if given is not None:
            scratch.append(pltpu.SemaphoreType.DMA)
        if opening:
            scratch += [
                VMEM(probe_bits.shape, jnp.int32),
                VMEM((rows,), BF16),
                pltpu.SemaphoreType.DMA((2,)),
            ]
        return pl.pallas_call(
            functools.partial(moments_kernel, snps, distances, opening, taken, given),
            in_specs=[in_hbm()] + [in_hbm() if opening else in_vmem()] * len(extra),
            out_specs=[in_vmem()] * len(out_shape),
            scratch_shapes=scratch,
            out_shape=out_shape,
            cost_estimate=cost(1, 4 * rows * block * slots if slots > 1 else 1),
            compiler_params=params(20),
            name=name,
        )(genotype, *extra)

    here_order = list(range(n - 2, 0, -2))
    away_order = [d + 1 for d in here_order]

    def plain(kernel, operands, out_shape, name, **options):
        return pl.pallas_call(
            kernel,
            in_specs=[in_vmem()] * len(operands),
            out_specs=[in_vmem()] * len(out_shape),
            out_shape=out_shape,
            compiler_params=params(20),
            name=name,
            **options,
        )(*operands)

    kept_away, away, local_away, left, raw = moments(
        away_order, here_order[0], (probe_bits, phenotype), "moments_away"
    )
    away = swap(away, "ind", n, 1)
    kept_here, here, local_here = moments(here_order, None, (raw, left), "moments_here")
    packed = jax.ShapeDtypeStruct((SUBLANES, span * 3 // 2), BF16)
    *sums, left = plain(
        cores_kernel,
        (left, here, away),
        [packed] * (chips - 1) + [jax.ShapeDtypeStruct(left.shape, F32)],
        "cores",
    )
    sums = [swap(value, "ind", n, d) for value, d in zip(sums, here_order)]
    kept_near, near, local_near, raw = moments([1], 0, (None, left), "moments_near")
    near = swap(near, "ind", n, 1)
    kept_own, own, local_own = moments([0], None, (raw, left), "moments_own")

    u, trait = plain(
        weights_kernel,
        (mean, scale, own, near, *sums),
        [
            jax.ShapeDtypeStruct((SUBLANES, folded), BF16),
            jax.ShapeDtypeStruct((1, block), F32),
        ],
        "weights",
    )

    number_shape = jax.ShapeDtypeStruct((SUBLANES, LANES), F32)
    term_shape = [
        jax.ShapeDtypeStruct((rows, PROBES * SUBLANES), F32),
        jax.ShapeDtypeStruct((PROBES * SUBLANES, LANES), F32),
        number_shape,
    ]
    end_shape = [jax.ShapeDtypeStruct((SUBLANES, PROBES * rows), BF16), number_shape]

    def fields(kept, blocks, us, terms, last=False):
        return plain(
            functools.partial(field_kernel, own_bins, blocks, len(kept), bool(terms), last),
            (mean, label, *kept, *us, *terms),
            end_shape if last else term_shape,
            "field",
            cost_estimate=cost(1, 1),
        )

    u_near = swap(u, "ind", n, 1)
    u_here = [swap(u, "ind", n, d) for d in here_order]
    terms = fields([kept_own, kept_near], [(0, 0), (0, 1)], [u, u_near], [])
    u_away = []
    for slot, (distance, value) in enumerate(zip(here_order, u_here)):
        shape = [jax.ShapeDtypeStruct(value.shape, value.dtype)]
        (value,) = plain(relay_kernel, (terms[2], value), shape, "relay")
        u_away.append(swap(value, "ind", n, 1))
        if slot < chips - 2:
            terms = fields([kept_here], [(slot, distance)], [value], terms)
        else:
            blocks = [(slot, distance), (0, away_order[0])]
            terms = fields([kept_here, kept_away], blocks, [value, u_away[0]], terms)
    blocks = list(enumerate(away_order))[1:]
    flat, number = fields([kept_away], blocks, u_away[1:], terms, last=True)

    flats = [flat] + [swap(flat, "bin", n_bin, d) for d in range(1, n_bin)]
    order = (rows, (away_order, here_order, [1], [0]))
    stats, field = plain(
        functools.partial(stats_kernel, own_bins, order),
        (flat, mean, scale, label, trait, local_away, local_here, local_near, local_own),
        [number_shape, jax.ShapeDtypeStruct((PROBES, own_bins, rows), BF16)],
        "stats",
    )
    (part,) = plain(pair_kernel, (stats, *flats), [number_shape], "pair")
    pairs, common = chosen_pairs(list(range(2, n, 2)))
    part_common = swap(part, "ind", n, common)
    part = part + swap(part, "ind", n, 1)
    mine = [swap_mixed(part, n, pair) for pair in pairs]
    theirs = [swap(value, "ind", n, 1) for value in mine + [part_common]]
    pair, trace, quad = plain(
        functools.partial(final_kernel, own_bins, n_bin, len(pairs), rows * n),
        (number, part, part_common, *mine, *theirs),
        [
            jax.ShapeDtypeStruct((own_bins, BINS), F32),
            jax.ShapeDtypeStruct((1, own_bins), F32),
            jax.ShapeDtypeStruct((1, own_bins), F32),
        ],
        "final",
    )
    return jnp.transpose(field, (1, 0, 2)), pair, trace[0], quad[0]


def solution(mesh):
    placed = (P("ind", "bin"), P("bin"), P("bin"), P("bin"), P(None, "ind"), P("ind"))
    return jax.shard_map(
        shards,
        mesh=mesh,
        in_specs=placed,
        out_specs=(P("bin", None, "ind"), P("bin", None), P("bin"), P("bin")),
        check_vma=False,
    )
```

```python
import functools

import jax
import jax.numpy as jnp
from jax import lax
from jax.experimental import pallas as pl
from jax.experimental.pallas import tpu as pltpu
from jax.sharding import PartitionSpec as P

BINS = 24
PROBES = 10
LANES = 128
SUBLANES = 8
ROWS = 16
TRAIT, ONES = PROBES, PROBES + 1
TRACE_LANE, QUAD_LANE = LANES - 2, LANES - 1
PIECE = 640
DOT_PIECE = 1664
F32 = jnp.float32
BF16 = jnp.bfloat16
VMEM = pltpu.VMEM
MIB = 1 << 20


def core():
    return lax.rem(lax.axis_index("ind"), 2)


def fold_lanes(value):
    return tree_sum([value[:, at : at + LANES] for at in range(0, value.shape[1], LANES)])


def rows_iota(count, width=1):
    return lax.broadcasted_iota(jnp.int32, (count, width), 0)


def tree_sum(terms):
    terms = list(terms)
    while len(terms) > 1:
        pairs = [a + b for a, b in zip(terms[::2], terms[1::2])]
        terms = pairs + terms[len(pairs) * 2 :]
    return terms[0]


def pack_sums(value):
    half = value.shape[1] // 2
    low = value[SUBLANES:]
    turned = pltpu.roll(low[:, half:], 4, 0)
    low = jnp.where(rows_iota(SUBLANES) < 4, low[:, :half], turned)
    return value[:SUBLANES], low


def unpack_sums(value):
    span = value.shape[1] * 2 // 3
    low = value[:, span:]
    return value[:, :span], jnp.concatenate([low, pltpu.roll(low, 4, 0)], axis=1)


def moments_kernel(snps, distances, opening, taken, given, geno_ref, *rest):
    rest = list(rest)
    if opening:
        bits_ref, trait_ref, kept_ref, sums_ref, local_ref, left_ref = rest[:6]
        rest = rest[6:]
    else:
        raw_in = rest.pop(0) if taken else None
        left_ref, kept_ref, sums_ref, local_ref = rest[:4]
        rest = rest[4:]
    raw_out = rest.pop(0) if given is not None else None
    slots, rows, block = kept_ref.shape
    fetched = slots - taken
    devices = -(-snps // block)
    tail = snps - (devices - 1) * block
    span = sums_ref.shape[2] * 2 // 3

    def copy(distance, target, semaphore, width):
        start = pl.multiple_of((lax.axis_index("ind") ^ distance) * block, LANES)
        return pltpu.make_async_copy(
            geno_ref.at[:, pl.ds(start, width)], target.at[:, pl.ds(0, width)], semaphore
        )

    def whole_or_tail(distance, target, semaphore, act):
        if tail == block:
            act(copy(distance, target, semaphore, block))
        else:
            last = (lax.axis_index("ind") ^ distance) == devices - 1
            pl.when(last)(lambda: act(copy(distance, target, semaphore, tail)))
            pl.when(jnp.logical_not(last))(lambda: act(copy(distance, target, semaphore, block)))

    if fetched:
        buffer, arrived = rest[:2]
        rest = rest[2:]

        def fetch(index, act):
            distance = distances[taken]
            for slot in range(taken + 1, slots):
                distance = jnp.where(index + taken == slot, distances[slot], distance)
            whole_or_tail(distance, buffer.at[index], arrived.at[index], act)

    if raw_out is not None:
        raw_arrived = rest.pop(0)

    if opening:
        bits, trait, small = rest[:3]
        bits_copy = pltpu.make_async_copy(bits_ref, bits, small.at[0])
        trait_copy = pltpu.make_async_copy(trait_ref, trait, small.at[1])
        bits_copy.start()
        trait_copy.start()
    if fetched:
        pl.loop(0, fetched)(lambda index: fetch(index, lambda c: c.start()))
    if raw_out is not None:
        whole_or_tail(given, raw_out, raw_arrived, lambda c: c.start())
    if opening:
        bits_copy.wait()
        trait_copy.wait()
        left_ref[...] = jnp.zeros_like(left_ref)
        left_ref[0:PROBES] = (2 * bits[...] - 1).astype(F32)
        left_ref[TRAIT : TRAIT + 1] = trait[...].astype(F32).reshape(1, rows)
        left_ref[ONES : ONES + 1] = jnp.ones((1, rows), F32)
    left = left_ref[...]
    base = jnp.sum(left, axis=1, keepdims=True)
    left = left.astype(BF16)
    row = rows_iota(ROWS)

    def with_low(value):
        high = value[TRAIT : TRAIT + 1]
        return jnp.where(row == TRAIT + 1, high - high.astype(BF16).astype(F32), value)

    ends = jnp.broadcast_to(with_low(base), (ROWS, span - block))

    def work(slot, source):
        squares = []
        for at in range(0, block, PIECE):
            lanes = slice(at, min(at + PIECE, block))
            square = 0.0
            for r in range(0, rows, 16):
                dose = source[r : r + 16, lanes].astype(F32)
                kept_ref[slot, r : r + 16, lanes] = dose.astype(BF16)
                dose = dose * dose
                square = square + (dose[:8] + dose[8:])
            squares.append(jnp.sum(square, axis=0, keepdims=True))
        total = jnp.dot(left, kept_ref[slot], preferred_element_type=F32) - base
        ones = total[ONES : ONES + 1]
        local_ref[slot, 0:1] = ones
        local_ref[slot, 1:2] = jnp.concatenate(squares, axis=1) - 2.0 * ones - rows
        high, low = pack_sums(jnp.concatenate([with_low(total), ends], axis=1))
        sums_ref[slot, :, :span] = high.astype(BF16)
        sums_ref[slot, :, span:] = low.astype(BF16)

    if taken:
        work(0, raw_in)
    if fetched:

        @pl.loop(0, fetched)
        def _(index):
            fetch(index, lambda c: c.wait())
            work(index + taken, buffer.at[index])

    if raw_out is not None:
        whole_or_tail(given, raw_out, raw_arrived, lambda c: c.wait())


def cores_kernel(left_ref, here_ref, away_ref, *outs):
    outs, left_out = outs[:-1], outs[-1]
    left_out[...] = left_ref[...]
    for index, out in enumerate(outs):
        out[...] = (here_ref[index].astype(F32) + away_ref[index].astype(F32)).astype(BF16)


def relay_kernel(token_ref, value_ref, out_ref):
    out_ref[...] = value_ref[...]


def weights_kernel(mean_ref, scale_ref, own_ref, near_ref, *refs):
    parts, (u_ref, trait_ref) = refs[:-2], refs[-2:]
    block = trait_ref.shape[1]
    width = u_ref.shape[1] - block
    here = pl.ds(pl.multiple_of(lax.axis_index("ind") * block, LANES), block)
    parts = [own_ref[0], near_ref[0]] + [part[...] for part in parts]
    total = tree_sum([part.astype(F32) for part in parts])
    shift = mean_ref[:, here] - 1.0
    inverse = 1.0 / scale_ref[:, here]
    high, low = [
        (part[:, :block] - part[:, block : block + 1] * shift) * inverse
        for part in unpack_sums(total)
    ]
    trait_ref[...] = low[2:3] + low[3:4]
    high, low = [part.astype(BF16).astype(F32) * inverse for part in (high, low)]
    low = jnp.concatenate([low, jnp.zeros((SUBLANES, 4 * width - block), F32)], axis=1)
    folded = low[:, :width]
    for j in range(1, 4):
        turned = pltpu.roll(low[:, j * width : (j + 1) * width], 2 * j, 0)
        folded = jnp.where(rows_iota(SUBLANES) < 2 * j, folded, turned)
    u_ref[:, :block] = high.astype(BF16)
    u_ref[:, block:] = folded.astype(BF16)


def stats_kernel(own_bins, order, flat_ref, mean_ref, scale_ref, label_ref, trait_ref, *rest):
    locals_, (out_ref, field_ref) = rest[:-2], rest[-2:]
    block = trait_ref.shape[1]
    rows = order[0]
    bins = rows_iota(SUBLANES)

    def member_of(owner):
        here = pl.ds(pl.multiple_of(owner * block, LANES), block)
        member = label_ref[:, here] - lax.axis_index("bin") * own_bins == bins
        return here, member & (bins < own_bins)

    trace = jnp.zeros((SUBLANES, 1), F32)
    for ref, distances in zip(locals_, order[1]):
        for slot, distance in enumerate(distances):
            here, member = member_of(lax.axis_index("ind") ^ distance)
            shift = mean_ref[:, here] - 1.0
            inverse = 1.0 / scale_ref[:, here]
            square = ref[slot, 1:2] - 2.0 * shift * ref[slot, 0:1] + rows * shift * shift
            square = square * (inverse * inverse)
            trace += jnp.sum(jnp.where(member, square, 0.0), axis=1, keepdims=True)
    _, member = member_of(lax.axis_index("ind"))
    trait = trait_ref[...]
    quad = jnp.sum(jnp.where(member, trait * trait, 0.0), axis=1, keepdims=True)
    lane = lax.broadcasted_iota(jnp.int32, (SUBLANES, LANES), 1)
    out_ref[...] = jnp.where(lane == TRACE_LANE, trace, jnp.where(lane == QUAD_LANE, quad, 0.0))
    flat = flat_ref[...].astype(F32)
    for b in range(PROBES):
        field_ref[b] = flat[:own_bins, b * rows : (b + 1) * rows].astype(BF16)


def field_kernel(own_bins, blocks, sources, started, last, *refs):
    refs = list(refs)
    mean_ref, label_ref = refs[:2]
    kept_refs, refs = refs[2 : 2 + sources], refs[2 + sources :]
    u_refs, refs = refs[: len(blocks)], refs[len(blocks) :]
    rows, block = kept_refs[0].shape[1:]
    bins = rows_iota(SUBLANES)
    if started:
        acc, offset, number = [ref[...] for ref in refs[:3]]
        refs = refs[3:]
    else:
        acc = jnp.zeros((rows, PROBES * SUBLANES), F32)
        offset = jnp.zeros((PROBES * SUBLANES, LANES), F32)
        number = jnp.zeros((SUBLANES, LANES), F32)
    for index, (slot, distance) in enumerate(blocks):
        start = (lax.axis_index("ind") ^ distance) * block
        u = u_refs[index][...].astype(F32)
        lines = [u[b : b + 1, :block] for b in range(SUBLANES)]
        for b in range(PROBES - SUBLANES):
            line = [u[2 * j + b : 2 * j + b + 1, block:] for j in range(4)]
            lines.append(jnp.concatenate(line, axis=1)[:, :block])
        for at in range(0, block, DOT_PIECE):
            width = min(DOT_PIECE, block - at)
            here = pl.ds(pl.multiple_of(start + at, LANES), width)
            member = label_ref[:, here] - lax.axis_index("bin") * own_bins == bins
            member = member & (bins < own_bins)
            mean = mean_ref[:, here]
            spread = [jnp.where(member, line[:, at : at + width], 0.0) for line in lines]
            offset += jnp.concatenate([fold_lanes(value * mean) for value in spread], axis=0)
            number += fold_lanes(jnp.where(member, 1.0, 0.0))
            acc += lax.dot_general(
                kept_refs[index if sources > 1 else 0][slot, :, at : at + width],
                jnp.concatenate(spread, axis=0).astype(BF16),
                (((1,), (1,)), ((), ())),
                preferred_element_type=F32,
            )
    if not last:
        for ref, value in zip(refs, (acc, offset, number)):
            ref[...] = value
        return
    flat_ref, count_ref = refs
    acc = jnp.concatenate([acc, jnp.zeros((rows, LANES - acc.shape[1]), F32)], axis=1)
    acc = jnp.transpose(acc)[: PROBES * SUBLANES] - jnp.sum(offset, axis=1, keepdims=True)
    number = jnp.sum(number, axis=1, keepdims=True)
    count_ref[...] = jnp.broadcast_to(number, count_ref.shape)
    inverse = 1.0 / jnp.maximum(number, 1.0)
    flat = [acc[b * SUBLANES : (b + 1) * SUBLANES] * inverse for b in range(PROBES)]
    flat_ref[...] = jnp.concatenate(flat, axis=1).astype(BF16)


def pair_kernel(stats_ref, *rest):
    flats, out_ref = rest[:-1], rest[-1]
    everyone = [flat[...].astype(F32) for flat in flats]
    everyone += [jnp.zeros_like(everyone[0])] * (LANES // SUBLANES - len(flats))
    out_ref[...] = stats_ref[...] + lax.dot_general(
        flats[0][...],
        jnp.concatenate(everyone, axis=0).astype(BF16),
        (((1,), (1,)), ((), ())),
        preferred_element_type=F32,
    )


def final_kernel(own_bins, n_bin, pairs, total_rows, count_ref, own_ref, common_ref, *rest):
    mine, theirs, outs = rest[:pairs], rest[pairs : 2 * pairs + 1], rest[2 * pairs + 1 :]
    pair_ref, trace_ref, quad_ref = outs
    terms = [own_ref[...]]
    even = core() == 0
    for ref, other in zip(mine, theirs):
        terms.append(jnp.where(even, ref[...], other[...]))
        terms.append(jnp.where(even, other[...], ref[...]))
    terms.append(common_ref[...] + theirs[pairs][...])
    total = tree_sum(terms)
    row = lax.broadcasted_iota(jnp.int32, (SUBLANES, LANES), 0)
    lane = lax.broadcasted_iota(jnp.int32, (SUBLANES, LANES), 1)
    pair = jnp.zeros_like(total)
    for slot in range(n_bin):
        start = slot * SUBLANES
        part = jnp.where((lane >= start) & (lane < start + own_bins), total, 0.0)
        shift = (lax.axis_index("bin") ^ slot) * own_bins - start + LANES
        pair = pair + pltpu.roll(part, lax.rem(shift, LANES), 1)
    pair_ref[...] = pair[:own_bins, :BINS] / (PROBES * total_rows)
    scaled = total / (count_ref[...] * total_rows)
    for ref, column in ((trace_ref, TRACE_LANE), (quad_ref, QUAD_LANE)):
        turned = jnp.where(row == lane, scaled[:, column : column + 1], 0.0)
        ref[...] = jnp.sum(turned, axis=0, keepdims=True)[:, :own_bins]


def swap(value, axis, size, distance):
    return lax.ppermute(value, axis, [(i, i ^ distance) for i in range(size)])


def swap_mixed(value, size, pair):
    return lax.ppermute(value, "ind", [(i, i ^ pair[i % 2]) for i in range(size)])


def chosen_pairs(distances):
    return list(zip(distances[:-1:2], distances[1:-1:2])), distances[-1]


def in_vmem():
    return pl.BlockSpec(memory_space=VMEM)


def in_hbm():
    return pl.BlockSpec(memory_space=pltpu.HBM)


def params(mib):
    return pltpu.CompilerParams(vmem_limit_bytes=mib * MIB)


def cost(flops, moved):
    return pl.CostEstimate(flops=flops, bytes_accessed=moved, transcendentals=0)


def shards(genotype, snp_mean, snp_scale, snp_label, probe_bits, phenotype):
    n = lax.axis_size("ind")
    n_bin = lax.axis_size("bin")
    chips = n // 2
    own_bins = BINS // n_bin
    rows, snps = genotype.shape
    tiles = -(-snps // LANES)
    block_tiles = -(-tiles // n)
    block = block_tiles * LANES
    span = block + LANES * (2 - block_tiles % 2)
    folded = block + -(-block_tiles // 4) * LANES
    whole = n * block
    mean, scale, label = snp_mean, snp_scale, snp_label
    if whole != snps:
        mean = jnp.pad(mean, (0, whole - snps), constant_values=1.0)
        scale = jnp.pad(scale, (0, whole - snps), constant_values=1.0)
        label = jnp.pad(label, (0, whole - snps), constant_values=-1)
    mean, scale, label = mean[None, :], scale[None, :], label[None, :]
    genotype, probe_bits, phenotype = [
        pltpu.with_memory_space_constraint(value, pltpu.HBM)
        for value in (genotype, probe_bits, phenotype)
    ]

    def moments(distances, given, extra, name):
        slots = len(distances)
        opening = extra[0] is probe_bits
        taken = int(not opening and extra[0] is not None)
        extra = [value for value in extra if value is not None]
        fetched = slots - taken
        out_shape = [
            jax.ShapeDtypeStruct((slots, rows, block), BF16),
            jax.ShapeDtypeStruct((slots, SUBLANES, span * 3 // 2), BF16),
            jax.ShapeDtypeStruct((slots, 2, block), F32),
        ]
        if opening:
            out_shape.append(jax.ShapeDtypeStruct((ROWS, rows), F32))
        if given is not None:
            out_shape.append(jax.ShapeDtypeStruct((rows, block), jnp.int32))
        scratch = []
        if fetched:
            scratch += [VMEM((fetched, rows, block), jnp.int32), pltpu.SemaphoreType.DMA((fetched,))]
        if given is not None:
            scratch.append(pltpu.SemaphoreType.DMA)
        if opening:
            scratch += [
                VMEM(probe_bits.shape, jnp.int32),
                VMEM((rows,), BF16),
                pltpu.SemaphoreType.DMA((2,)),
            ]
        return pl.pallas_call(
            functools.partial(moments_kernel, snps, distances, opening, taken, given),
            in_specs=[in_hbm()] + [in_hbm() if opening else in_vmem()] * len(extra),
            out_specs=[in_vmem()] * len(out_shape),
            scratch_shapes=scratch,
            out_shape=out_shape,
            cost_estimate=cost(1, 4 * rows * block * slots if slots > 1 else 1),
            compiler_params=params(20),
            name=name,
        )(genotype, *extra)

    here_order = [n - 2] + list(range(2, n - 2, 2))
    away_order = [d + 1 for d in here_order]

    def plain(kernel, operands, out_shape, name, **options):
        return pl.pallas_call(
            kernel,
            in_specs=[in_vmem()] * len(operands),
            out_specs=[in_vmem()] * len(out_shape),
            out_shape=out_shape,
            compiler_params=params(20),
            name=name,
            **options,
        )(*operands)

    kept_away, away, local_away, left, raw = moments(
        away_order, here_order[0], (probe_bits, phenotype), "moments_away"
    )
    away = swap(away, "ind", n, 1)
    kept_here, here, local_here = moments(here_order, None, (raw, left), "moments_here")
    packed = jax.ShapeDtypeStruct((SUBLANES, span * 3 // 2), BF16)
    *sums, left = plain(
        cores_kernel,
        (left, here, away),
        [packed] * (chips - 1) + [jax.ShapeDtypeStruct(left.shape, F32)],
        "cores",
    )
    sums = [swap(value, "ind", n, d) for value, d in zip(sums, here_order)]
    kept_near, near, local_near, raw = moments([1], 0, (None, left), "moments_near")
    near = swap(near, "ind", n, 1)
    kept_own, own, local_own = moments([0], None, (raw, left), "moments_own")

    u, trait = plain(
        weights_kernel,
        (mean, scale, own, near, *sums),
        [
            jax.ShapeDtypeStruct((SUBLANES, folded), BF16),
            jax.ShapeDtypeStruct((1, block), F32),
        ],
        "weights",
    )

    number_shape = jax.ShapeDtypeStruct((SUBLANES, LANES), F32)
    term_shape = [
        jax.ShapeDtypeStruct((rows, PROBES * SUBLANES), F32),
        jax.ShapeDtypeStruct((PROBES * SUBLANES, LANES), F32),
        number_shape,
    ]
    end_shape = [jax.ShapeDtypeStruct((SUBLANES, PROBES * rows), BF16), number_shape]

    def fields(kept, blocks, us, terms, last=False):
        return plain(
            functools.partial(field_kernel, own_bins, blocks, len(kept), bool(terms), last),
            (mean, label, *kept, *us, *terms),
            end_shape if last else term_shape,
            "field",
            cost_estimate=cost(1, 1),
        )

    u_near = swap(u, "ind", n, 1)
    u_here = [swap(u, "ind", n, d) for d in here_order]
    terms = fields([kept_own, kept_near], [(0, 0), (0, 1)], [u, u_near], [])
    u_away = []
    for slot, (distance, value) in enumerate(zip(here_order, u_here)):
        shape = [jax.ShapeDtypeStruct(value.shape, value.dtype)]
        (value,) = plain(relay_kernel, (terms[2], value), shape, "relay")
        u_away.append(swap(value, "ind", n, 1))
        if slot < chips - 2:
            terms = fields([kept_here], [(slot, distance)], [value], terms)
        else:
            blocks = [(slot, distance), (0, away_order[0])]
            terms = fields([kept_here, kept_away], blocks, [value, u_away[0]], terms)
    blocks = list(enumerate(away_order))[1:]
    flat, number = fields([kept_away], blocks, u_away[1:], terms, last=True)

    flats = [flat] + [swap(flat, "bin", n_bin, d) for d in range(1, n_bin)]
    order = (rows, (away_order, here_order, [1], [0]))
    stats, field = plain(
        functools.partial(stats_kernel, own_bins, order),
        (flat, mean, scale, label, trait, local_away, local_here, local_near, local_own),
        [number_shape, jax.ShapeDtypeStruct((PROBES, own_bins, rows), BF16)],
        "stats",
    )
    (part,) = plain(pair_kernel, (stats, *flats), [number_shape], "pair")
    pairs, common = chosen_pairs(list(range(2, n, 2)))
    part_common = swap(part, "ind", n, common)
    part = part + swap(part, "ind", n, 1)
    mine = [swap_mixed(part, n, pair) for pair in pairs]
    theirs = [swap(value, "ind", n, 1) for value in mine + [part_common]]
    pair, trace, quad = plain(
        functools.partial(final_kernel, own_bins, n_bin, len(pairs), rows * n),
        (number, part, part_common, *mine, *theirs),
        [
            jax.ShapeDtypeStruct((own_bins, BINS), F32),
            jax.ShapeDtypeStruct((1, own_bins), F32),
            jax.ShapeDtypeStruct((1, own_bins), F32),
        ],
        "final",
    )
    return jnp.transpose(field, (1, 0, 2)), pair, trace[0], quad[0]


def solution(mesh):
    placed = (P("ind", "bin"), P("bin"), P("bin"), P("bin"), P(None, "ind"), P("ind"))
    return jax.shard_map(
        shards,
        mesh=mesh,
        in_specs=placed,
        out_specs=(P("bin", None, "ind"), P("bin", None), P("bin"), P("bin")),
        check_vma=False,
    )
```

```python
import functools

import jax
import jax.numpy as jnp
from jax import lax
from jax.experimental import pallas as pl
from jax.experimental.pallas import tpu as pltpu
from jax.sharding import PartitionSpec as P

BINS = 24
PROBES = 10
LANES = 128
SUBLANES = 8
ROWS = 16
TRAIT, ONES = PROBES, PROBES + 1
TRACE_LANE, QUAD_LANE = LANES - 2, LANES - 1
PIECE = 640
DOT_PIECE = 1664
F32 = jnp.float32
BF16 = jnp.bfloat16
VMEM = pltpu.VMEM
MIB = 1 << 20


def core():
    return lax.rem(lax.axis_index("ind"), 2)


def fold_lanes(value):
    return tree_sum([value[:, at : at + LANES] for at in range(0, value.shape[1], LANES)])


def rows_iota(count, width=1):
    return lax.broadcasted_iota(jnp.int32, (count, width), 0)


def tree_sum(terms):
    terms = list(terms)
    while len(terms) > 1:
        pairs = [a + b for a, b in zip(terms[::2], terms[1::2])]
        terms = pairs + terms[len(pairs) * 2 :]
    return terms[0]


def pack_sums(value):
    half = value.shape[1] // 2
    low = value[SUBLANES:]
    turned = pltpu.roll(low[:, half:], 4, 0)
    low = jnp.where(rows_iota(SUBLANES) < 4, low[:, :half], turned)
    return value[:SUBLANES], low


def unpack_sums(value):
    span = value.shape[1] * 2 // 3
    low = value[:, span:]
    return value[:, :span], jnp.concatenate([low, pltpu.roll(low, 4, 0)], axis=1)


def moments_kernel(snps, distances, opening, taken, given, geno_ref, *rest):
    rest = list(rest)
    if opening:
        bits_ref, trait_ref, kept_ref, sums_ref, local_ref, left_ref = rest[:6]
        rest = rest[6:]
    else:
        raw_in = rest.pop(0) if taken else None
        left_ref, kept_ref, sums_ref, local_ref = rest[:4]
        rest = rest[4:]
    raw_out = rest.pop(0) if given is not None else None
    slots, rows, block = kept_ref.shape
    fetched = slots - taken
    devices = -(-snps // block)
    tail = snps - (devices - 1) * block
    span = sums_ref.shape[2] * 2 // 3

    def copy(distance, target, semaphore, width):
        start = pl.multiple_of((lax.axis_index("ind") ^ distance) * block, LANES)
        return pltpu.make_async_copy(
            geno_ref.at[:, pl.ds(start, width)], target.at[:, pl.ds(0, width)], semaphore
        )

    def whole_or_tail(distance, target, semaphore, act):
        if tail == block:
            act(copy(distance, target, semaphore, block))
        else:
            last = (lax.axis_index("ind") ^ distance) == devices - 1
            pl.when(last)(lambda: act(copy(distance, target, semaphore, tail)))
            pl.when(jnp.logical_not(last))(lambda: act(copy(distance, target, semaphore, block)))

    if fetched:
        buffer, arrived = rest[:2]
        rest = rest[2:]

        def fetch(index, act):
            distance = distances[taken]
            for slot in range(taken + 1, slots):
                distance = jnp.where(index + taken == slot, distances[slot], distance)
            whole_or_tail(distance, buffer.at[index], arrived.at[index], act)

    if raw_out is not None:
        raw_arrived = rest.pop(0)

    if opening:
        bits, trait, small = rest[:3]
        bits_copy = pltpu.make_async_copy(bits_ref, bits, small.at[0])
        trait_copy = pltpu.make_async_copy(trait_ref, trait, small.at[1])
        bits_copy.start()
        trait_copy.start()
    if fetched:
        pl.loop(0, fetched)(lambda index: fetch(index, lambda c: c.start()))
    if raw_out is not None:
        whole_or_tail(given, raw_out, raw_arrived, lambda c: c.start())
    if opening:
        bits_copy.wait()
        trait_copy.wait()
        left_ref[...] = jnp.zeros_like(left_ref)
        left_ref[0:PROBES] = (2 * bits[...] - 1).astype(F32)
        left_ref[TRAIT : TRAIT + 1] = trait[...].astype(F32).reshape(1, rows)
        left_ref[ONES : ONES + 1] = jnp.ones((1, rows), F32)
    left = left_ref[...]
    base = jnp.sum(left, axis=1, keepdims=True)
    left = left.astype(BF16)
    row = rows_iota(ROWS)

    def with_low(value):
        high = value[TRAIT : TRAIT + 1]
        return jnp.where(row == TRAIT + 1, high - high.astype(BF16).astype(F32), value)

    ends = jnp.broadcast_to(with_low(base), (ROWS, span - block))

    def work(slot, source):
        squares = []
        for at in range(0, block, PIECE):
            lanes = slice(at, min(at + PIECE, block))
            square = 0.0
            for r in range(0, rows, 16):
                dose = source[r : r + 16, lanes].astype(F32)
                kept_ref[slot, r : r + 16, lanes] = dose.astype(BF16)
                dose = dose * dose
                square = square + (dose[:8] + dose[8:])
            squares.append(jnp.sum(square, axis=0, keepdims=True))
        total = jnp.dot(left, kept_ref[slot], preferred_element_type=F32) - base
        ones = total[ONES : ONES + 1]
        local_ref[slot, 0:1] = ones
        local_ref[slot, 1:2] = jnp.concatenate(squares, axis=1) - 2.0 * ones - rows
        high, low = pack_sums(jnp.concatenate([with_low(total), ends], axis=1))
        sums_ref[slot, :, :span] = high.astype(BF16)
        sums_ref[slot, :, span:] = low.astype(BF16)

    if taken:
        work(0, raw_in)
    if fetched:

        @pl.loop(0, fetched)
        def _(index):
            fetch(index, lambda c: c.wait())
            work(index + taken, buffer.at[index])

    if raw_out is not None:
        whole_or_tail(given, raw_out, raw_arrived, lambda c: c.wait())


def cores_kernel(left_ref, here_ref, away_ref, *outs):
    outs, left_out = outs[:-1], outs[-1]
    left_out[...] = left_ref[...]
    for index, out in enumerate(outs):
        out[...] = (here_ref[index].astype(F32) + away_ref[index].astype(F32)).astype(BF16)


def relay_kernel(token_ref, value_ref, out_ref):
    out_ref[...] = value_ref[...]


def weights_kernel(mean_ref, scale_ref, own_ref, near_ref, *refs):
    parts, (u_ref, trait_ref) = refs[:-2], refs[-2:]
    block = trait_ref.shape[1]
    width = u_ref.shape[1] - block
    here = pl.ds(pl.multiple_of(lax.axis_index("ind") * block, LANES), block)
    parts = [own_ref[0], near_ref[0]] + [part[...] for part in parts]
    total = tree_sum([part.astype(F32) for part in parts])
    shift = mean_ref[:, here] - 1.0
    inverse = 1.0 / scale_ref[:, here]
    high, low = [
        (part[:, :block] - part[:, block : block + 1] * shift) * inverse
        for part in unpack_sums(total)
    ]
    trait_ref[...] = low[2:3] + low[3:4]
    high, low = [part.astype(BF16).astype(F32) * inverse for part in (high, low)]
    low = jnp.concatenate([low, jnp.zeros((SUBLANES, 4 * width - block), F32)], axis=1)
    folded = low[:, :width]
    for j in range(1, 4):
        turned = pltpu.roll(low[:, j * width : (j + 1) * width], 2 * j, 0)
        folded = jnp.where(rows_iota(SUBLANES) < 2 * j, folded, turned)
    u_ref[:, :block] = high.astype(BF16)
    u_ref[:, block:] = folded.astype(BF16)


def stats_kernel(own_bins, order, flat_ref, mean_ref, scale_ref, label_ref, trait_ref, *rest):
    locals_, (out_ref, field_ref) = rest[:-2], rest[-2:]
    block = trait_ref.shape[1]
    rows = order[0]
    bins = rows_iota(SUBLANES)

    def member_of(owner):
        here = pl.ds(pl.multiple_of(owner * block, LANES), block)
        member = label_ref[:, here] - lax.axis_index("bin") * own_bins == bins
        return here, member & (bins < own_bins)

    trace = jnp.zeros((SUBLANES, 1), F32)
    for ref, distances in zip(locals_, order[1]):
        for slot, distance in enumerate(distances):
            here, member = member_of(lax.axis_index("ind") ^ distance)
            shift = mean_ref[:, here] - 1.0
            inverse = 1.0 / scale_ref[:, here]
            square = ref[slot, 1:2] - 2.0 * shift * ref[slot, 0:1] + rows * shift * shift
            square = square * (inverse * inverse)
            trace += jnp.sum(jnp.where(member, square, 0.0), axis=1, keepdims=True)
    _, member = member_of(lax.axis_index("ind"))
    trait = trait_ref[...]
    quad = jnp.sum(jnp.where(member, trait * trait, 0.0), axis=1, keepdims=True)
    lane = lax.broadcasted_iota(jnp.int32, (SUBLANES, LANES), 1)
    out_ref[...] = jnp.where(lane == TRACE_LANE, trace, jnp.where(lane == QUAD_LANE, quad, 0.0))
    flat = flat_ref[...].astype(F32)
    for b in range(PROBES):
        field_ref[b] = flat[:own_bins, b * rows : (b + 1) * rows].astype(BF16)


def field_kernel(own_bins, blocks, sources, started, last, *refs):
    refs = list(refs)
    mean_ref, label_ref = refs[:2]
    kept_refs, refs = refs[2 : 2 + sources], refs[2 + sources :]
    u_refs, refs = refs[: len(blocks)], refs[len(blocks) :]
    rows, block = kept_refs[0].shape[1:]
    bins = rows_iota(SUBLANES)
    if started:
        acc, offset, number = [ref[...] for ref in refs[:3]]
        refs = refs[3:]
    else:
        acc = jnp.zeros((rows, PROBES * SUBLANES), F32)
        offset = jnp.zeros((PROBES * SUBLANES, LANES), F32)
        number = jnp.zeros((SUBLANES, LANES), F32)
    for index, (slot, distance) in enumerate(blocks):
        start = (lax.axis_index("ind") ^ distance) * block
        u = u_refs[index][...].astype(F32)
        lines = [u[b : b + 1, :block] for b in range(SUBLANES)]
        for b in range(PROBES - SUBLANES):
            line = [u[2 * j + b : 2 * j + b + 1, block:] for j in range(4)]
            lines.append(jnp.concatenate(line, axis=1)[:, :block])
        for at in range(0, block, DOT_PIECE):
            width = min(DOT_PIECE, block - at)
            here = pl.ds(pl.multiple_of(start + at, LANES), width)
            member = label_ref[:, here] - lax.axis_index("bin") * own_bins == bins
            member = member & (bins < own_bins)
            mean = mean_ref[:, here]
            spread = [jnp.where(member, line[:, at : at + width], 0.0) for line in lines]
            offset += jnp.concatenate([fold_lanes(value * mean) for value in spread], axis=0)
            number += fold_lanes(jnp.where(member, 1.0, 0.0))
            acc += lax.dot_general(
                kept_refs[index if sources > 1 else 0][slot, :, at : at + width],
                jnp.concatenate(spread, axis=0).astype(BF16),
                (((1,), (1,)), ((), ())),
                preferred_element_type=F32,
            )
    if not last:
        for ref, value in zip(refs, (acc, offset, number)):
            ref[...] = value
        return
    flat_ref, count_ref = refs
    acc = jnp.concatenate([acc, jnp.zeros((rows, LANES - acc.shape[1]), F32)], axis=1)
    acc = jnp.transpose(acc)[: PROBES * SUBLANES] - jnp.sum(offset, axis=1, keepdims=True)
    number = jnp.sum(number, axis=1, keepdims=True)
    count_ref[...] = jnp.broadcast_to(number, count_ref.shape)
    inverse = 1.0 / jnp.maximum(number, 1.0)
    flat = [acc[b * SUBLANES : (b + 1) * SUBLANES] * inverse for b in range(PROBES)]
    flat_ref[...] = jnp.concatenate(flat, axis=1).astype(BF16)


def pair_kernel(stats_ref, *rest):
    flats, out_ref = rest[:-1], rest[-1]
    everyone = [flat[...].astype(F32) for flat in flats]
    everyone += [jnp.zeros_like(everyone[0])] * (LANES // SUBLANES - len(flats))
    out_ref[...] = stats_ref[...] + lax.dot_general(
        flats[0][...],
        jnp.concatenate(everyone, axis=0).astype(BF16),
        (((1,), (1,)), ((), ())),
        preferred_element_type=F32,
    )


def final_kernel(own_bins, n_bin, pairs, total_rows, count_ref, own_ref, common_ref, *rest):
    mine, theirs, outs = rest[:pairs], rest[pairs : 2 * pairs + 1], rest[2 * pairs + 1 :]
    pair_ref, trace_ref, quad_ref = outs
    terms = [own_ref[...]]
    even = core() == 0
    for ref, other in zip(mine, theirs):
        terms.append(jnp.where(even, ref[...], other[...]))
        terms.append(jnp.where(even, other[...], ref[...]))
    terms.append(common_ref[...] + theirs[pairs][...])
    total = tree_sum(terms)
    row = lax.broadcasted_iota(jnp.int32, (SUBLANES, LANES), 0)
    lane = lax.broadcasted_iota(jnp.int32, (SUBLANES, LANES), 1)
    pair = jnp.zeros_like(total)
    for slot in range(n_bin):
        start = slot * SUBLANES
        part = jnp.where((lane >= start) & (lane < start + own_bins), total, 0.0)
        shift = (lax.axis_index("bin") ^ slot) * own_bins - start + LANES
        pair = pair + pltpu.roll(part, lax.rem(shift, LANES), 1)
    pair_ref[...] = pair[:own_bins, :BINS] / (PROBES * total_rows)
    scaled = total / (count_ref[...] * total_rows)
    for ref, column in ((trace_ref, TRACE_LANE), (quad_ref, QUAD_LANE)):
        turned = jnp.where(row == lane, scaled[:, column : column + 1], 0.0)
        ref[...] = jnp.sum(turned, axis=0, keepdims=True)[:, :own_bins]


def swap(value, axis, size, distance):
    return lax.ppermute(value, axis, [(i, i ^ distance) for i in range(size)])


def swap_mixed(value, size, pair):
    return lax.ppermute(value, "ind", [(i, i ^ pair[i % 2]) for i in range(size)])


def chosen_pairs(distances):
    return list(zip(distances[:-1:2], distances[1:-1:2])), distances[-1]


def in_vmem():
    return pl.BlockSpec(memory_space=VMEM)


def in_hbm():
    return pl.BlockSpec(memory_space=pltpu.HBM)


def params(mib):
    return pltpu.CompilerParams(vmem_limit_bytes=mib * MIB)


def cost(flops, moved):
    return pl.CostEstimate(flops=flops, bytes_accessed=moved, transcendentals=0)


def shards(genotype, snp_mean, snp_scale, snp_label, probe_bits, phenotype):
    n = lax.axis_size("ind")
    n_bin = lax.axis_size("bin")
    chips = n // 2
    own_bins = BINS // n_bin
    rows, snps = genotype.shape
    tiles = -(-snps // LANES)
    block_tiles = -(-tiles // n)
    block = block_tiles * LANES
    span = block + LANES * (2 - block_tiles % 2)
    folded = block + -(-block_tiles // 4) * LANES
    whole = n * block
    mean, scale, label = snp_mean, snp_scale, snp_label
    if whole != snps:
        mean = jnp.pad(mean, (0, whole - snps), constant_values=1.0)
        scale = jnp.pad(scale, (0, whole - snps), constant_values=1.0)
        label = jnp.pad(label, (0, whole - snps), constant_values=-1)
    mean, scale, label = mean[None, :], scale[None, :], label[None, :]
    genotype, probe_bits, phenotype = [
        pltpu.with_memory_space_constraint(value, pltpu.HBM)
        for value in (genotype, probe_bits, phenotype)
    ]

    def moments(distances, given, extra, name):
        slots = len(distances)
        opening = extra[0] is probe_bits
        taken = int(not opening and extra[0] is not None)
        extra = [value for value in extra if value is not None]
        fetched = slots - taken
        out_shape = [
            jax.ShapeDtypeStruct((slots, rows, block), BF16),
            jax.ShapeDtypeStruct((slots, SUBLANES, span * 3 // 2), BF16),
            jax.ShapeDtypeStruct((slots, 2, block), F32),
        ]
        if opening:
            out_shape.append(jax.ShapeDtypeStruct((ROWS, rows), F32))
        if given is not None:
            out_shape.append(jax.ShapeDtypeStruct((rows, block), jnp.int32))
        scratch = []
        if fetched:
            scratch += [VMEM((fetched, rows, block), jnp.int32), pltpu.SemaphoreType.DMA((fetched,))]
        if given is not None:
            scratch.append(pltpu.SemaphoreType.DMA)
        if opening:
            scratch += [
                VMEM(probe_bits.shape, jnp.int32),
                VMEM((rows,), BF16),
                pltpu.SemaphoreType.DMA((2,)),
            ]
        return pl.pallas_call(
            functools.partial(moments_kernel, snps, distances, opening, taken, given),
            in_specs=[in_hbm()] + [in_hbm() if opening else in_vmem()] * len(extra),
            out_specs=[in_vmem()] * len(out_shape),
            scratch_shapes=scratch,
            out_shape=out_shape,
            cost_estimate=cost(1, 4 * rows * block * slots if slots > 1 else 1),
            compiler_params=params(20),
            name=name,
        )(genotype, *extra)

    here_order = [n - 2] + list(range(2, n - 2, 2))
    away_order = [d + 1 for d in here_order]

    def plain(kernel, operands, out_shape, name, **options):
        return pl.pallas_call(
            kernel,
            in_specs=[in_vmem()] * len(operands),
            out_specs=[in_vmem()] * len(out_shape),
            out_shape=out_shape,
            compiler_params=params(20),
            name=name,
            **options,
        )(*operands)

    kept_away, away, local_away, left, raw = moments(
        away_order, here_order[0], (probe_bits, phenotype), "moments_away"
    )
    away = swap(away, "ind", n, 1)
    kept_here, here, local_here = moments(here_order, None, (raw, left), "moments_here")
    packed = jax.ShapeDtypeStruct((SUBLANES, span * 3 // 2), BF16)
    *sums, left = plain(
        cores_kernel,
        (left, here, away),
        [packed] * (chips - 1) + [jax.ShapeDtypeStruct(left.shape, F32)],
        "cores",
    )
    sums = [swap(value, "ind", n, d) for value, d in zip(sums, here_order)]
    kept_near, near, local_near, raw = moments([1], 0, (None, left), "moments_near")
    near = swap(near, "ind", n, 1)
    kept_own, own, local_own = moments([0], None, (raw, left), "moments_own")

    u, trait = plain(
        weights_kernel,
        (mean, scale, own, near, *sums),
        [
            jax.ShapeDtypeStruct((SUBLANES, folded), BF16),
            jax.ShapeDtypeStruct((1, block), F32),
        ],
        "weights",
    )

    number_shape = jax.ShapeDtypeStruct((SUBLANES, LANES), F32)
    term_shape = [
        jax.ShapeDtypeStruct((rows, PROBES * SUBLANES), F32),
        jax.ShapeDtypeStruct((PROBES * SUBLANES, LANES), F32),
        number_shape,
    ]
    end_shape = [jax.ShapeDtypeStruct((SUBLANES, PROBES * rows), BF16), number_shape]

    def fields(kept, blocks, us, terms, last=False):
        return plain(
            functools.partial(field_kernel, own_bins, blocks, len(kept), bool(terms), last),
            (mean, label, *kept, *us, *terms),
            end_shape if last else term_shape,
            "field",
            cost_estimate=cost(1, 1),
        )

    u_near = swap(u, "ind", n, 1)
    u_here = [swap(u, "ind", n, d) for d in here_order]
    terms = fields([kept_own, kept_near], [(0, 0), (0, 1)], [u, u_near], [])
    u_away = []
    for first in range(0, chips - 1, 2):
        slots = range(first, min(first + 2, chips - 1))
        values = []
        for slot in slots:
            shape = [jax.ShapeDtypeStruct(u.shape, u.dtype)]
            (value,) = plain(relay_kernel, (terms[2], u_here[slot]), shape, "relay")
            u_away.append(swap(value, "ind", n, 1))
            values.append(value)
        blocks = [(slot, here_order[slot]) for slot in slots]
        kept = [kept_here] * len(blocks)
        if len(blocks) == 1:
            blocks.append((0, away_order[0]))
            kept.append(kept_away)
            values.append(u_away[0])
        terms = fields(kept, blocks, values, terms)
    blocks = list(enumerate(away_order))[1:]
    flat, number = fields([kept_away], blocks, u_away[1:], terms, last=True)

    flats = [flat] + [swap(flat, "bin", n_bin, d) for d in range(1, n_bin)]
    order = (rows, (away_order, here_order, [1], [0]))
    stats, field = plain(
        functools.partial(stats_kernel, own_bins, order),
        (flat, mean, scale, label, trait, local_away, local_here, local_near, local_own),
        [number_shape, jax.ShapeDtypeStruct((PROBES, own_bins, rows), BF16)],
        "stats",
    )
    (part,) = plain(pair_kernel, (stats, *flats), [number_shape], "pair")
    pairs, common = chosen_pairs(list(range(2, n, 2)))
    part_common = swap(part, "ind", n, common)
    part = part + swap(part, "ind", n, 1)
    mine = [swap_mixed(part, n, pair) for pair in pairs]
    theirs = [swap(value, "ind", n, 1) for value in mine + [part_common]]
    pair, trace, quad = plain(
        functools.partial(final_kernel, own_bins, n_bin, len(pairs), rows * n),
        (number, part, part_common, *mine, *theirs),
        [
            jax.ShapeDtypeStruct((own_bins, BINS), F32),
            jax.ShapeDtypeStruct((1, own_bins), F32),
            jax.ShapeDtypeStruct((1, own_bins), F32),
        ],
        "final",
    )
    return jnp.transpose(field, (1, 0, 2)), pair, trace[0], quad[0]


def solution(mesh):
    placed = (P("ind", "bin"), P("bin"), P("bin"), P("bin"), P(None, "ind"), P("ind"))
    return jax.shard_map(
        shards,
        mesh=mesh,
        in_specs=placed,
        out_specs=(P("bin", None, "ind"), P("bin", None), P("bin"), P("bin")),
        check_vma=False,
    )
```

```python
import functools

import jax
import jax.numpy as jnp
from jax import lax
from jax.experimental import pallas as pl
from jax.experimental.pallas import tpu as pltpu
from jax.sharding import PartitionSpec as P

BINS = 24
PROBES = 10
LANES = 128
SUBLANES = 8
ROWS = 16
TRAIT, ONES = PROBES, PROBES + 1
TRACE_LANE, QUAD_LANE = LANES - 2, LANES - 1
PIECE = 640
DOT_PIECE = 1664
F32 = jnp.float32
BF16 = jnp.bfloat16
VMEM = pltpu.VMEM
MIB = 1 << 20


def folds(rows, width):
    return rows == 6 and width % (4 * LANES) == 0


def fold_rows(value, rows):
    width = value.shape[1]
    if not folds(rows, width):
        return value
    main = width * 3 // 4
    tail = value[:, main:]
    row = rows_iota(SUBLANES)
    result = value[:, :main]
    for at in range(2):
        line = jnp.concatenate([tail[3 * at + i : 3 * at + i + 1] for i in range(3)], axis=1)
        result = jnp.where(row == 6 + at, line, result)
    return result


def unfold_rows(value, rows, width):
    if not folds(rows, width):
        return value
    main, part = width * 3 // 4, width // 4
    row = rows_iota(SUBLANES)
    tail = jnp.zeros((SUBLANES, part), F32)
    for i in range(6):
        line = value[6 + i // 3 : 7 + i // 3, i % 3 * part : (i % 3 + 1) * part]
        tail = jnp.where(row == i, line, tail)
    return jnp.concatenate([jnp.where(row < 6, value, 0.0), tail], axis=1)


def core():
    return lax.rem(lax.axis_index("ind"), 2)


def fold_lanes(value):
    return tree_sum([value[:, at : at + LANES] for at in range(0, value.shape[1], LANES)])


def rows_iota(count, width=1):
    return lax.broadcasted_iota(jnp.int32, (count, width), 0)


def tree_sum(terms):
    terms = list(terms)
    while len(terms) > 1:
        pairs = [a + b for a, b in zip(terms[::2], terms[1::2])]
        terms = pairs + terms[len(pairs) * 2 :]
    return terms[0]


def pack_sums(value):
    half = value.shape[1] // 2
    low = value[SUBLANES:]
    turned = pltpu.roll(low[:, half:], 4, 0)
    low = jnp.where(rows_iota(SUBLANES) < 4, low[:, :half], turned)
    return value[:SUBLANES], low


def unpack_sums(value):
    span = value.shape[1] * 2 // 3
    low = value[:, span:]
    return value[:, :span], jnp.concatenate([low, pltpu.roll(low, 4, 0)], axis=1)


def moments_kernel(snps, distances, opening, taken, given, geno_ref, *rest):
    rest = list(rest)
    if opening:
        bits_ref, trait_ref, kept_ref, sums_ref, local_ref, left_ref = rest[:6]
        rest = rest[6:]
    else:
        raw_in = rest.pop(0) if taken else None
        left_ref, kept_ref, sums_ref, local_ref = rest[:4]
        rest = rest[4:]
    raw_out = rest.pop(0) if given is not None else None
    slots, rows, block = kept_ref.shape
    fetched = slots - taken
    devices = -(-snps // block)
    tail = snps - (devices - 1) * block
    span = sums_ref.shape[2] * 2 // 3

    def copy(distance, target, semaphore, width):
        start = pl.multiple_of((lax.axis_index("ind") ^ distance) * block, LANES)
        return pltpu.make_async_copy(
            geno_ref.at[:, pl.ds(start, width)], target.at[:, pl.ds(0, width)], semaphore
        )

    def whole_or_tail(distance, target, semaphore, act):
        if tail == block:
            act(copy(distance, target, semaphore, block))
        else:
            last = (lax.axis_index("ind") ^ distance) == devices - 1
            pl.when(last)(lambda: act(copy(distance, target, semaphore, tail)))
            pl.when(jnp.logical_not(last))(lambda: act(copy(distance, target, semaphore, block)))

    if fetched:
        buffer, arrived = rest[:2]
        rest = rest[2:]

        def fetch(index, act):
            distance = distances[taken]
            for slot in range(taken + 1, slots):
                distance = jnp.where(index + taken == slot, distances[slot], distance)
            whole_or_tail(distance, buffer.at[index], arrived.at[index], act)

    if raw_out is not None:
        raw_arrived = rest.pop(0)

    if opening:
        bits, trait, small = rest[:3]
        bits_copy = pltpu.make_async_copy(bits_ref, bits, small.at[0])
        trait_copy = pltpu.make_async_copy(trait_ref, trait, small.at[1])
        bits_copy.start()
        trait_copy.start()
    if fetched:
        pl.loop(0, fetched)(lambda index: fetch(index, lambda c: c.start()))
    if raw_out is not None:
        whole_or_tail(given, raw_out, raw_arrived, lambda c: c.start())
    if opening:
        bits_copy.wait()
        trait_copy.wait()
        left_ref[...] = jnp.zeros_like(left_ref)
        left_ref[0:PROBES] = (2 * bits[...] - 1).astype(F32)
        left_ref[TRAIT : TRAIT + 1] = trait[...].astype(F32).reshape(1, rows)
        left_ref[ONES : ONES + 1] = jnp.ones((1, rows), F32)
    left = left_ref[...]
    base = jnp.sum(left, axis=1, keepdims=True)
    left = left.astype(BF16)
    row = rows_iota(ROWS)

    def with_low(value):
        high = value[TRAIT : TRAIT + 1]
        return jnp.where(row == TRAIT + 1, high - high.astype(BF16).astype(F32), value)

    ends = jnp.broadcast_to(with_low(base), (ROWS, span - block))

    def work(slot, source):
        squares = []
        for at in range(0, block, PIECE):
            lanes = slice(at, min(at + PIECE, block))
            square = 0.0
            for r in range(0, rows, 16):
                dose = source[r : r + 16, lanes].astype(F32)
                kept_ref[slot, r : r + 16, lanes] = dose.astype(BF16)
                dose = dose * dose
                square = square + (dose[:8] + dose[8:])
            squares.append(jnp.sum(square, axis=0, keepdims=True))
        total = jnp.dot(left, kept_ref[slot], preferred_element_type=F32) - base
        ones = total[ONES : ONES + 1]
        local_ref[slot, 0:1] = ones
        local_ref[slot, 1:2] = jnp.concatenate(squares, axis=1) - 2.0 * ones - rows
        high, low = pack_sums(jnp.concatenate([with_low(total), ends], axis=1))
        sums_ref[slot, :, :span] = high.astype(BF16)
        sums_ref[slot, :, span:] = low.astype(BF16)

    if taken:
        work(0, raw_in)
    if fetched:

        @pl.loop(0, fetched)
        def _(index):
            fetch(index, lambda c: c.wait())
            work(index + taken, buffer.at[index])

    if raw_out is not None:
        whole_or_tail(given, raw_out, raw_arrived, lambda c: c.wait())


def cores_kernel(left_ref, here_ref, away_ref, *outs):
    outs, left_out = outs[:-1], outs[-1]
    left_out[...] = left_ref[...]
    for index, out in enumerate(outs):
        out[...] = (here_ref[index].astype(F32) + away_ref[index].astype(F32)).astype(BF16)


def relay_kernel(token_ref, value_ref, out_ref):
    out_ref[...] = value_ref[...]


def weights_kernel(mean_ref, scale_ref, own_ref, near_ref, *refs):
    parts, (u_ref, trait_ref) = refs[:-2], refs[-2:]
    block = trait_ref.shape[1]
    width = u_ref.shape[1] - block
    here = pl.ds(pl.multiple_of(lax.axis_index("ind") * block, LANES), block)
    parts = [own_ref[0], near_ref[0]] + [part[...] for part in parts]
    total = tree_sum([part.astype(F32) for part in parts])
    shift = mean_ref[:, here] - 1.0
    inverse = 1.0 / scale_ref[:, here]
    high, low = [
        (part[:, :block] - part[:, block : block + 1] * shift) * inverse
        for part in unpack_sums(total)
    ]
    trait_ref[...] = low[2:3] + low[3:4]
    high, low = [part.astype(BF16).astype(F32) * inverse for part in (high, low)]
    low = jnp.concatenate([low, jnp.zeros((SUBLANES, 4 * width - block), F32)], axis=1)
    folded = low[:, :width]
    for j in range(1, 4):
        turned = pltpu.roll(low[:, j * width : (j + 1) * width], 2 * j, 0)
        folded = jnp.where(rows_iota(SUBLANES) < 2 * j, folded, turned)
    u_ref[:, :block] = high.astype(BF16)
    u_ref[:, block:] = folded.astype(BF16)


def stats_kernel(own_bins, order, flat_ref, mean_ref, scale_ref, label_ref, trait_ref, *rest):
    locals_, (out_ref, field_ref) = rest[:-2], rest[-2:]
    block = trait_ref.shape[1]
    rows = order[0]
    bins = rows_iota(SUBLANES)

    def member_of(owner):
        here = pl.ds(pl.multiple_of(owner * block, LANES), block)
        member = label_ref[:, here] - lax.axis_index("bin") * own_bins == bins
        return here, member & (bins < own_bins)

    trace = jnp.zeros((SUBLANES, 1), F32)
    for ref, distances in zip(locals_, order[1]):
        for slot, distance in enumerate(distances):
            here, member = member_of(lax.axis_index("ind") ^ distance)
            shift = mean_ref[:, here] - 1.0
            inverse = 1.0 / scale_ref[:, here]
            square = ref[slot, 1:2] - 2.0 * shift * ref[slot, 0:1] + rows * shift * shift
            square = square * (inverse * inverse)
            trace += jnp.sum(jnp.where(member, square, 0.0), axis=1, keepdims=True)
    _, member = member_of(lax.axis_index("ind"))
    trait = trait_ref[...]
    quad = jnp.sum(jnp.where(member, trait * trait, 0.0), axis=1, keepdims=True)
    lane = lax.broadcasted_iota(jnp.int32, (SUBLANES, LANES), 1)
    out_ref[...] = jnp.where(lane == TRACE_LANE, trace, jnp.where(lane == QUAD_LANE, quad, 0.0))
    flat = unfold_rows(flat_ref[...].astype(F32), own_bins, PROBES * rows)
    for b in range(PROBES):
        field_ref[b] = flat[:own_bins, b * rows : (b + 1) * rows].astype(BF16)


def field_kernel(own_bins, blocks, sources, started, last, *refs):
    refs = list(refs)
    mean_ref, label_ref = refs[:2]
    kept_refs, refs = refs[2 : 2 + sources], refs[2 + sources :]
    u_refs, refs = refs[: len(blocks)], refs[len(blocks) :]
    rows, block = kept_refs[0].shape[1:]
    bins = rows_iota(SUBLANES)
    if started:
        acc, offset, number = [ref[...] for ref in refs[:3]]
        refs = refs[3:]
    else:
        acc = jnp.zeros((rows, PROBES * SUBLANES), F32)
        offset = jnp.zeros((PROBES * SUBLANES, LANES), F32)
        number = jnp.zeros((SUBLANES, LANES), F32)
    for index, (slot, distance) in enumerate(blocks):
        start = (lax.axis_index("ind") ^ distance) * block
        u = u_refs[index][...].astype(F32)
        lines = [u[b : b + 1, :block] for b in range(SUBLANES)]
        for b in range(PROBES - SUBLANES):
            line = [u[2 * j + b : 2 * j + b + 1, block:] for j in range(4)]
            lines.append(jnp.concatenate(line, axis=1)[:, :block])
        for at in range(0, block, DOT_PIECE):
            width = min(DOT_PIECE, block - at)
            here = pl.ds(pl.multiple_of(start + at, LANES), width)
            member = label_ref[:, here] - lax.axis_index("bin") * own_bins == bins
            member = member & (bins < own_bins)
            mean = mean_ref[:, here]
            spread = [jnp.where(member, line[:, at : at + width], 0.0) for line in lines]
            offset += jnp.concatenate([fold_lanes(value * mean) for value in spread], axis=0)
            number += fold_lanes(jnp.where(member, 1.0, 0.0))
            acc += lax.dot_general(
                kept_refs[index if sources > 1 else 0][slot, :, at : at + width],
                jnp.concatenate(spread, axis=0).astype(BF16),
                (((1,), (1,)), ((), ())),
                preferred_element_type=F32,
            )
    if not last:
        for ref, value in zip(refs, (acc, offset, number)):
            ref[...] = value
        return
    flat_ref, count_ref = refs
    acc = jnp.concatenate([acc, jnp.zeros((rows, LANES - acc.shape[1]), F32)], axis=1)
    acc = jnp.transpose(acc)[: PROBES * SUBLANES] - jnp.sum(offset, axis=1, keepdims=True)
    number = jnp.sum(number, axis=1, keepdims=True)
    count_ref[...] = jnp.broadcast_to(number, count_ref.shape)
    inverse = 1.0 / jnp.maximum(number, 1.0)
    flat = [acc[b * SUBLANES : (b + 1) * SUBLANES] * inverse for b in range(PROBES)]
    flat_ref[...] = fold_rows(jnp.concatenate(flat, axis=1), own_bins).astype(BF16)


def pair_kernel(own_bins, width, stats_ref, *rest):
    flats, out_ref = rest[:-1], rest[-1]
    everyone = [unfold_rows(flat[...].astype(F32), own_bins, width) for flat in flats]
    own = everyone[0].astype(BF16)
    everyone += [jnp.zeros_like(everyone[0])] * (LANES // SUBLANES - len(flats))
    out_ref[...] = stats_ref[...] + lax.dot_general(
        own,
        jnp.concatenate(everyone, axis=0).astype(BF16),
        (((1,), (1,)), ((), ())),
        preferred_element_type=F32,
    )


def final_kernel(own_bins, n_bin, pairs, total_rows, count_ref, own_ref, common_ref, *rest):
    mine, theirs, outs = rest[:pairs], rest[pairs : 2 * pairs + 1], rest[2 * pairs + 1 :]
    pair_ref, trace_ref, quad_ref = outs
    terms = [own_ref[...]]
    even = core() == 0
    for ref, other in zip(mine, theirs):
        terms.append(jnp.where(even, ref[...], other[...]))
        terms.append(jnp.where(even, other[...], ref[...]))
    terms.append(common_ref[...] + theirs[pairs][...])
    total = tree_sum(terms)
    row = lax.broadcasted_iota(jnp.int32, (SUBLANES, LANES), 0)
    lane = lax.broadcasted_iota(jnp.int32, (SUBLANES, LANES), 1)
    pair = jnp.zeros_like(total)
    for slot in range(n_bin):
        start = slot * SUBLANES
        part = jnp.where((lane >= start) & (lane < start + own_bins), total, 0.0)
        shift = (lax.axis_index("bin") ^ slot) * own_bins - start + LANES
        pair = pair + pltpu.roll(part, lax.rem(shift, LANES), 1)
    pair_ref[...] = pair[:own_bins, :BINS] / (PROBES * total_rows)
    scaled = total / (count_ref[...] * total_rows)
    for ref, column in ((trace_ref, TRACE_LANE), (quad_ref, QUAD_LANE)):
        turned = jnp.where(row == lane, scaled[:, column : column + 1], 0.0)
        ref[...] = jnp.sum(turned, axis=0, keepdims=True)[:, :own_bins]


def swap(value, axis, size, distance):
    return lax.ppermute(value, axis, [(i, i ^ distance) for i in range(size)])


def swap_mixed(value, size, pair):
    return lax.ppermute(value, "ind", [(i, i ^ pair[i % 2]) for i in range(size)])


def chosen_pairs(distances):
    return list(zip(distances[:-1:2], distances[1:-1:2])), distances[-1]


def in_vmem():
    return pl.BlockSpec(memory_space=VMEM)


def in_hbm():
    return pl.BlockSpec(memory_space=pltpu.HBM)


def params(mib):
    return pltpu.CompilerParams(vmem_limit_bytes=mib * MIB)


def cost(flops, moved):
    return pl.CostEstimate(flops=flops, bytes_accessed=moved, transcendentals=0)


def shards(genotype, snp_mean, snp_scale, snp_label, probe_bits, phenotype):
    n = lax.axis_size("ind")
    n_bin = lax.axis_size("bin")
    chips = n // 2
    own_bins = BINS // n_bin
    rows, snps = genotype.shape
    tiles = -(-snps // LANES)
    block_tiles = -(-tiles // n)
    block = block_tiles * LANES
    span = block + LANES * (2 - block_tiles % 2)
    folded = block + -(-block_tiles // 4) * LANES
    whole = n * block
    mean, scale, label = snp_mean, snp_scale, snp_label
    if whole != snps:
        mean = jnp.pad(mean, (0, whole - snps), constant_values=1.0)
        scale = jnp.pad(scale, (0, whole - snps), constant_values=1.0)
        label = jnp.pad(label, (0, whole - snps), constant_values=-1)
    mean, scale, label = mean[None, :], scale[None, :], label[None, :]
    genotype, probe_bits, phenotype = [
        pltpu.with_memory_space_constraint(value, pltpu.HBM)
        for value in (genotype, probe_bits, phenotype)
    ]

    def moments(distances, given, extra, name):
        slots = len(distances)
        opening = extra[0] is probe_bits
        taken = int(not opening and extra[0] is not None)
        extra = [value for value in extra if value is not None]
        fetched = slots - taken
        out_shape = [
            jax.ShapeDtypeStruct((slots, rows, block), BF16),
            jax.ShapeDtypeStruct((slots, SUBLANES, span * 3 // 2), BF16),
            jax.ShapeDtypeStruct((slots, 2, block), F32),
        ]
        if opening:
            out_shape.append(jax.ShapeDtypeStruct((ROWS, rows), F32))
        if given is not None:
            out_shape.append(jax.ShapeDtypeStruct((rows, block), jnp.int32))
        scratch = []
        if fetched:
            scratch += [VMEM((fetched, rows, block), jnp.int32), pltpu.SemaphoreType.DMA((fetched,))]
        if given is not None:
            scratch.append(pltpu.SemaphoreType.DMA)
        if opening:
            scratch += [
                VMEM(probe_bits.shape, jnp.int32),
                VMEM((rows,), BF16),
                pltpu.SemaphoreType.DMA((2,)),
            ]
        return pl.pallas_call(
            functools.partial(moments_kernel, snps, distances, opening, taken, given),
            in_specs=[in_hbm()] + [in_hbm() if opening else in_vmem()] * len(extra),
            out_specs=[in_vmem()] * len(out_shape),
            scratch_shapes=scratch,
            out_shape=out_shape,
            cost_estimate=cost(1, 4 * rows * block * slots if slots > 1 else 1),
            compiler_params=params(20),
            name=name,
        )(genotype, *extra)

    here_order = [n - 2] + list(range(2, n - 2, 2))
    away_order = [d + 1 for d in here_order]

    def plain(kernel, operands, out_shape, name, **options):
        return pl.pallas_call(
            kernel,
            in_specs=[in_vmem()] * len(operands),
            out_specs=[in_vmem()] * len(out_shape),
            out_shape=out_shape,
            compiler_params=params(20),
            name=name,
            **options,
        )(*operands)

    kept_away, away, local_away, left, raw = moments(
        away_order, here_order[0], (probe_bits, phenotype), "moments_away"
    )
    away = swap(away, "ind", n, 1)
    kept_here, here, local_here = moments(here_order, None, (raw, left), "moments_here")
    packed = jax.ShapeDtypeStruct((SUBLANES, span * 3 // 2), BF16)
    *sums, left = plain(
        cores_kernel,
        (left, here, away),
        [packed] * (chips - 1) + [jax.ShapeDtypeStruct(left.shape, F32)],
        "cores",
    )
    sums = [swap(value, "ind", n, d) for value, d in zip(sums, here_order)]
    kept_near, near, local_near, raw = moments([1], 0, (None, left), "moments_near")
    near = swap(near, "ind", n, 1)
    kept_own, own, local_own = moments([0], None, (raw, left), "moments_own")

    u, trait = plain(
        weights_kernel,
        (mean, scale, own, near, *sums),
        [
            jax.ShapeDtypeStruct((SUBLANES, folded), BF16),
            jax.ShapeDtypeStruct((1, block), F32),
        ],
        "weights",
    )

    number_shape = jax.ShapeDtypeStruct((SUBLANES, LANES), F32)
    term_shape = [
        jax.ShapeDtypeStruct((rows, PROBES * SUBLANES), F32),
        jax.ShapeDtypeStruct((PROBES * SUBLANES, LANES), F32),
        number_shape,
    ]
    wide = PROBES * rows
    if folds(own_bins, wide):
        wide = wide * 3 // 4
    end_shape = [jax.ShapeDtypeStruct((SUBLANES, wide), BF16), number_shape]

    def fields(kept, blocks, us, terms, last=False):
        return plain(
            functools.partial(field_kernel, own_bins, blocks, len(kept), bool(terms), last),
            (mean, label, *kept, *us, *terms),
            end_shape if last else term_shape,
            "field",
            cost_estimate=cost(1, 1),
        )

    u_near = swap(u, "ind", n, 1)
    u_here = [swap(u, "ind", n, d) for d in here_order]
    terms = fields([kept_own, kept_near], [(0, 0), (0, 1)], [u, u_near], [])
    u_away = []
    for first in range(0, chips - 1, 2):
        slots = range(first, min(first + 2, chips - 1))
        values = []
        for slot in slots:
            shape = [jax.ShapeDtypeStruct(u.shape, u.dtype)]
            (value,) = plain(relay_kernel, (terms[2], u_here[slot]), shape, "relay")
            u_away.append(swap(value, "ind", n, 1))
            values.append(value)
        blocks = [(slot, here_order[slot]) for slot in slots]
        kept = [kept_here] * len(blocks)
        if len(blocks) == 1:
            blocks.append((0, away_order[0]))
            kept.append(kept_away)
            values.append(u_away[0])
        terms = fields(kept, blocks, values, terms)
    blocks = list(enumerate(away_order))[1:]
    flat, number = fields([kept_away], blocks, u_away[1:], terms, last=True)

    flats = [flat] + [swap(flat, "bin", n_bin, d) for d in range(1, n_bin)]
    order = (rows, (away_order, here_order, [1], [0]))
    stats, field = plain(
        functools.partial(stats_kernel, own_bins, order),
        (flat, mean, scale, label, trait, local_away, local_here, local_near, local_own),
        [number_shape, jax.ShapeDtypeStruct((PROBES, own_bins, rows), BF16)],
        "stats",
    )
    (part,) = plain(
        functools.partial(pair_kernel, own_bins, PROBES * rows),
        (stats, *flats),
        [number_shape],
        "pair",
    )
    pairs, common = chosen_pairs(list(range(2, n, 2)))
    part_common = swap(part, "ind", n, common)
    part = part + swap(part, "ind", n, 1)
    mine = [swap_mixed(part, n, pair) for pair in pairs]
    theirs = [swap(value, "ind", n, 1) for value in mine + [part_common]]
    pair, trace, quad = plain(
        functools.partial(final_kernel, own_bins, n_bin, len(pairs), rows * n),
        (number, part, part_common, *mine, *theirs),
        [
            jax.ShapeDtypeStruct((own_bins, BINS), F32),
            jax.ShapeDtypeStruct((1, own_bins), F32),
            jax.ShapeDtypeStruct((1, own_bins), F32),
        ],
        "final",
    )
    return jnp.transpose(field, (1, 0, 2)), pair, trace[0], quad[0]


def solution(mesh):
    placed = (P("ind", "bin"), P("bin"), P("bin"), P("bin"), P(None, "ind"), P("ind"))
    return jax.shard_map(
        shards,
        mesh=mesh,
        in_specs=placed,
        out_specs=(P("bin", None, "ind"), P("bin", None), P("bin"), P("bin")),
        check_vma=False,
    )
```

```python
import functools

import jax
import jax.numpy as jnp
from jax import lax
from jax.experimental import pallas as pl
from jax.experimental.pallas import tpu as pltpu
from jax.sharding import PartitionSpec as P

BINS = 24
PROBES = 10
LANES = 128
SUBLANES = 8
ROWS = 16
TRAIT, ONES = PROBES, PROBES + 1
TRACE_LANE, QUAD_LANE = LANES - 2, LANES - 1
PIECE = 640
DOT_PIECE = 1664
F32 = jnp.float32
BF16 = jnp.bfloat16
VMEM = pltpu.VMEM
MIB = 1 << 20


def folds(rows, width):
    return rows == 6 and width % (4 * LANES) == 0


def fold_rows(value, rows):
    width = value.shape[1]
    if not folds(rows, width):
        return value
    main = width * 3 // 4
    tail = value[:, main:]
    row = rows_iota(SUBLANES)
    result = value[:, :main]
    for at in range(2):
        line = jnp.concatenate([tail[3 * at + i : 3 * at + i + 1] for i in range(3)], axis=1)
        result = jnp.where(row == 6 + at, line, result)
    return result


def unfold_rows(value, rows, width):
    if not folds(rows, width):
        return value
    main, part = width * 3 // 4, width // 4
    row = rows_iota(SUBLANES)
    tail = jnp.zeros((SUBLANES, part), F32)
    for i in range(6):
        line = value[6 + i // 3 : 7 + i // 3, i % 3 * part : (i % 3 + 1) * part]
        tail = jnp.where(row == i, line, tail)
    return jnp.concatenate([jnp.where(row < 6, value, 0.0), tail], axis=1)


def core():
    return lax.rem(lax.axis_index("ind"), 2)


def fold_lanes(value):
    return tree_sum([value[:, at : at + LANES] for at in range(0, value.shape[1], LANES)])


def rows_iota(count, width=1):
    return lax.broadcasted_iota(jnp.int32, (count, width), 0)


def tree_sum(terms):
    terms = list(terms)
    while len(terms) > 1:
        pairs = [a + b for a, b in zip(terms[::2], terms[1::2])]
        terms = pairs + terms[len(pairs) * 2 :]
    return terms[0]


def pack_sums(value):
    half = value.shape[1] // 2
    low = value[SUBLANES:]
    turned = pltpu.roll(low[:, half:], 4, 0)
    low = jnp.where(rows_iota(SUBLANES) < 4, low[:, :half], turned)
    return value[:SUBLANES], low


def unpack_sums(value):
    span = value.shape[1] * 2 // 3
    low = value[:, span:]
    return value[:, :span], jnp.concatenate([low, pltpu.roll(low, 4, 0)], axis=1)


def moments_kernel(snps, distances, opening, taken, given, geno_ref, *rest):
    rest = list(rest)
    if opening:
        bits_ref, trait_ref, kept_ref, sums_ref, local_ref, left_ref = rest[:6]
        rest = rest[6:]
    else:
        raw_in = rest.pop(0) if taken else None
        left_ref, kept_ref, sums_ref, local_ref = rest[:4]
        rest = rest[4:]
    raw_out = rest.pop(0) if given is not None else None
    slots, rows, block = kept_ref.shape
    fetched = slots - taken
    devices = -(-snps // block)
    tail = snps - (devices - 1) * block
    span = sums_ref.shape[2] * 2 // 3

    def copy(distance, target, semaphore, width):
        start = pl.multiple_of((lax.axis_index("ind") ^ distance) * block, LANES)
        return pltpu.make_async_copy(
            geno_ref.at[:, pl.ds(start, width)], target.at[:, pl.ds(0, width)], semaphore
        )

    def whole_or_tail(distance, target, semaphore, act):
        if tail == block:
            act(copy(distance, target, semaphore, block))
        else:
            last = (lax.axis_index("ind") ^ distance) == devices - 1
            pl.when(last)(lambda: act(copy(distance, target, semaphore, tail)))
            pl.when(jnp.logical_not(last))(lambda: act(copy(distance, target, semaphore, block)))

    if fetched:
        buffer, arrived = rest[:2]
        rest = rest[2:]

        def fetch(index, act):
            distance = distances[taken]
            for slot in range(taken + 1, slots):
                distance = jnp.where(index + taken == slot, distances[slot], distance)
            whole_or_tail(distance, buffer.at[index], arrived.at[index], act)

    if raw_out is not None:
        raw_arrived = rest.pop(0)

    if opening:
        bits, trait, small = rest[:3]
        bits_copy = pltpu.make_async_copy(bits_ref, bits, small.at[0])
        trait_copy = pltpu.make_async_copy(trait_ref, trait, small.at[1])
        bits_copy.start()
        trait_copy.start()
    if fetched:
        pl.loop(0, fetched)(lambda index: fetch(index, lambda c: c.start()))
    if raw_out is not None:
        whole_or_tail(given, raw_out, raw_arrived, lambda c: c.start())
    if opening:
        bits_copy.wait()
        trait_copy.wait()
        left_ref[...] = jnp.zeros_like(left_ref)
        left_ref[0:PROBES] = (2 * bits[...] - 1).astype(F32)
        left_ref[TRAIT : TRAIT + 1] = trait[...].astype(F32).reshape(1, rows)
        left_ref[ONES : ONES + 1] = jnp.ones((1, rows), F32)
    left = left_ref[...]
    base = jnp.sum(left, axis=1, keepdims=True)
    left = left.astype(BF16)
    row = rows_iota(ROWS)

    def with_low(value):
        high = value[TRAIT : TRAIT + 1]
        return jnp.where(row == TRAIT + 1, high - high.astype(BF16).astype(F32), value)

    ends = jnp.broadcast_to(with_low(base), (ROWS, span - block))

    def work(slot, source):
        squares = []
        for at in range(0, block, PIECE):
            lanes = slice(at, min(at + PIECE, block))
            square = 0.0
            for r in range(0, rows, 16):
                dose = source[r : r + 16, lanes].astype(F32)
                kept_ref[slot, r : r + 16, lanes] = dose.astype(BF16)
                dose = dose * dose
                square = square + (dose[:8] + dose[8:])
            squares.append(jnp.sum(square, axis=0, keepdims=True))
        total = jnp.dot(left, kept_ref[slot], preferred_element_type=F32) - base
        ones = total[ONES : ONES + 1]
        local_ref[slot, 0:1] = ones
        local_ref[slot, 1:2] = jnp.concatenate(squares, axis=1) - 2.0 * ones - rows
        high, low = pack_sums(jnp.concatenate([with_low(total), ends], axis=1))
        sums_ref[slot, :, :span] = high.astype(BF16)
        sums_ref[slot, :, span:] = low.astype(BF16)

    if taken:
        work(0, raw_in)
    if fetched:

        @pl.loop(0, fetched)
        def _(index):
            fetch(index, lambda c: c.wait())
            work(index + taken, buffer.at[index])

    if raw_out is not None:
        whole_or_tail(given, raw_out, raw_arrived, lambda c: c.wait())


def cores_kernel(left_ref, here_ref, away_ref, *outs):
    outs, left_out = outs[:-1], outs[-1]
    left_out[...] = left_ref[...]
    for index, out in enumerate(outs):
        out[...] = (here_ref[index].astype(F32) + away_ref[index].astype(F32)).astype(BF16)


def relay_kernel(token_ref, value_ref, out_ref):
    out_ref[...] = value_ref[...]


def weights_kernel(mean_ref, scale_ref, own_ref, near_ref, *refs):
    parts, (u_ref, trait_ref) = refs[:-2], refs[-2:]
    block = trait_ref.shape[1]
    width = u_ref.shape[1] - block
    here = pl.ds(pl.multiple_of(lax.axis_index("ind") * block, LANES), block)
    parts = [own_ref[0], near_ref[0]] + [part[...] for part in parts]
    total = tree_sum([part.astype(F32) for part in parts])
    shift = mean_ref[:, here] - 1.0
    inverse = 1.0 / scale_ref[:, here]
    high, low = [
        (part[:, :block] - part[:, block : block + 1] * shift) * inverse
        for part in unpack_sums(total)
    ]
    trait_ref[...] = low[2:3] + low[3:4]
    high, low = [part.astype(BF16).astype(F32) * inverse for part in (high, low)]
    low = jnp.concatenate([low, jnp.zeros((SUBLANES, 4 * width - block), F32)], axis=1)
    folded = low[:, :width]
    for j in range(1, 4):
        turned = pltpu.roll(low[:, j * width : (j + 1) * width], 2 * j, 0)
        folded = jnp.where(rows_iota(SUBLANES) < 2 * j, folded, turned)
    u_ref[:, :block] = high.astype(BF16)
    u_ref[:, block:] = folded.astype(BF16)


def stats_kernel(own_bins, order, flat_ref, mean_ref, scale_ref, label_ref, trait_ref, *rest):
    locals_, (out_ref, field_ref) = rest[:-2], rest[-2:]
    block = trait_ref.shape[1]
    rows = order[0]
    bins = rows_iota(SUBLANES)

    def member_of(owner):
        here = pl.ds(pl.multiple_of(owner * block, LANES), block)
        member = label_ref[:, here] - lax.axis_index("bin") * own_bins == bins
        return here, member & (bins < own_bins)

    trace = jnp.zeros((SUBLANES, 1), F32)
    for ref, distances in zip(locals_, order[1]):
        for slot, distance in enumerate(distances):
            here, member = member_of(lax.axis_index("ind") ^ distance)
            shift = mean_ref[:, here] - 1.0
            inverse = 1.0 / scale_ref[:, here]
            square = ref[slot, 1:2] - 2.0 * shift * ref[slot, 0:1] + rows * shift * shift
            square = square * (inverse * inverse)
            trace += jnp.sum(jnp.where(member, square, 0.0), axis=1, keepdims=True)
    _, member = member_of(lax.axis_index("ind"))
    trait = trait_ref[...]
    quad = jnp.sum(jnp.where(member, trait * trait, 0.0), axis=1, keepdims=True)
    lane = lax.broadcasted_iota(jnp.int32, (SUBLANES, LANES), 1)
    out_ref[...] = jnp.where(lane == TRACE_LANE, trace, jnp.where(lane == QUAD_LANE, quad, 0.0))
    flat = unfold_rows(flat_ref[...].astype(F32), own_bins, PROBES * rows)
    for b in range(PROBES):
        field_ref[b] = flat[:own_bins, b * rows : (b + 1) * rows].astype(BF16)


def field_kernel(own_bins, blocks, sources, started, last, *refs):
    refs = list(refs)
    mean_ref, label_ref = refs[:2]
    kept_refs, refs = refs[2 : 2 + sources], refs[2 + sources :]
    u_refs, refs = refs[: len(blocks)], refs[len(blocks) :]
    rows, block = kept_refs[0].shape[1:]
    bins = rows_iota(SUBLANES)
    if started:
        acc, offset, number = [ref[...] for ref in refs[:3]]
        refs = refs[3:]
    else:
        acc = jnp.zeros((rows, PROBES * SUBLANES), F32)
        offset = jnp.zeros((PROBES * SUBLANES, LANES), F32)
        number = jnp.zeros((SUBLANES, LANES), F32)
    for index, (slot, distance) in enumerate(blocks):
        start = (lax.axis_index("ind") ^ distance) * block
        u = u_refs[index][...].astype(F32)
        lines = [u[b : b + 1, :block] for b in range(SUBLANES)]
        for b in range(PROBES - SUBLANES):
            line = [u[2 * j + b : 2 * j + b + 1, block:] for j in range(4)]
            lines.append(jnp.concatenate(line, axis=1)[:, :block])
        for at in range(0, block, DOT_PIECE):
            width = min(DOT_PIECE, block - at)
            here = pl.ds(pl.multiple_of(start + at, LANES), width)
            member = label_ref[:, here] - lax.axis_index("bin") * own_bins == bins
            member = member & (bins < own_bins)
            mean = mean_ref[:, here]
            spread = [jnp.where(member, line[:, at : at + width], 0.0) for line in lines]
            offset += jnp.concatenate([fold_lanes(value * mean) for value in spread], axis=0)
            number += fold_lanes(jnp.where(member, 1.0, 0.0))
            acc += lax.dot_general(
                kept_refs[index if sources > 1 else 0][slot, :, at : at + width],
                jnp.concatenate(spread, axis=0).astype(BF16),
                (((1,), (1,)), ((), ())),
                preferred_element_type=F32,
            )
    if not last:
        for ref, value in zip(refs, (acc, offset, number)):
            ref[...] = value
        return
    flat_ref, count_ref = refs
    acc = jnp.concatenate([acc, jnp.zeros((rows, LANES - acc.shape[1]), F32)], axis=1)
    acc = jnp.transpose(acc)[: PROBES * SUBLANES] - jnp.sum(offset, axis=1, keepdims=True)
    number = jnp.sum(number, axis=1, keepdims=True)
    count_ref[...] = jnp.broadcast_to(number, count_ref.shape)
    inverse = 1.0 / jnp.maximum(number, 1.0)
    flat = [acc[b * SUBLANES : (b + 1) * SUBLANES] * inverse for b in range(PROBES)]
    flat_ref[...] = fold_rows(jnp.concatenate(flat, axis=1), own_bins).astype(BF16)


def pair_kernel(own_bins, width, distances, stats_ref, *rest):
    flats, out_ref = rest[:-1], rest[-1]
    everyone = [unfold_rows(flat[...].astype(F32), own_bins, width) for flat in flats]
    own = everyone[0].astype(BF16)
    everyone = [everyone[distances.index(d)] for d in range(len(distances))]
    everyone += [jnp.zeros_like(everyone[0])] * (LANES // SUBLANES - len(flats))
    out_ref[...] = stats_ref[...] + lax.dot_general(
        own,
        jnp.concatenate(everyone, axis=0).astype(BF16),
        (((1,), (1,)), ((), ())),
        preferred_element_type=F32,
    )


def final_kernel(own_bins, n_bin, pairs, total_rows, count_ref, own_ref, common_ref, *rest):
    mine, theirs, outs = rest[:pairs], rest[pairs : 2 * pairs + 1], rest[2 * pairs + 1 :]
    pair_ref, trace_ref, quad_ref = outs
    terms = [own_ref[...]]
    even = core() == 0
    for ref, other in zip(mine, theirs):
        terms.append(jnp.where(even, ref[...], other[...]))
        terms.append(jnp.where(even, other[...], ref[...]))
    terms.append(common_ref[...] + theirs[pairs][...])
    total = tree_sum(terms)
    row = lax.broadcasted_iota(jnp.int32, (SUBLANES, LANES), 0)
    lane = lax.broadcasted_iota(jnp.int32, (SUBLANES, LANES), 1)
    pair = jnp.zeros_like(total)
    for slot in range(n_bin):
        start = slot * SUBLANES
        part = jnp.where((lane >= start) & (lane < start + own_bins), total, 0.0)
        shift = (lax.axis_index("bin") ^ slot) * own_bins - start + LANES
        pair = pair + pltpu.roll(part, lax.rem(shift, LANES), 1)
    pair_ref[...] = pair[:own_bins, :BINS] / (PROBES * total_rows)
    scaled = total / (count_ref[...] * total_rows)
    for ref, column in ((trace_ref, TRACE_LANE), (quad_ref, QUAD_LANE)):
        turned = jnp.where(row == lane, scaled[:, column : column + 1], 0.0)
        ref[...] = jnp.sum(turned, axis=0, keepdims=True)[:, :own_bins]


def swap(value, axis, size, distance):
    return lax.ppermute(value, axis, [(i, i ^ distance) for i in range(size)])


def swap_mixed(value, size, pair):
    return lax.ppermute(value, "ind", [(i, i ^ pair[i % 2]) for i in range(size)])


def chosen_pairs(distances):
    return list(zip(distances[:-1:2], distances[1:-1:2])), distances[-1]


def in_vmem():
    return pl.BlockSpec(memory_space=VMEM)


def in_hbm():
    return pl.BlockSpec(memory_space=pltpu.HBM)


def params(mib):
    return pltpu.CompilerParams(vmem_limit_bytes=mib * MIB)


def cost(flops, moved):
    return pl.CostEstimate(flops=flops, bytes_accessed=moved, transcendentals=0)


def shards(genotype, snp_mean, snp_scale, snp_label, probe_bits, phenotype):
    n = lax.axis_size("ind")
    n_bin = lax.axis_size("bin")
    chips = n // 2
    own_bins = BINS // n_bin
    rows, snps = genotype.shape
    tiles = -(-snps // LANES)
    block_tiles = -(-tiles // n)
    block = block_tiles * LANES
    span = block + LANES * (2 - block_tiles % 2)
    folded = block + -(-block_tiles // 4) * LANES
    whole = n * block
    mean, scale, label = snp_mean, snp_scale, snp_label
    if whole != snps:
        mean = jnp.pad(mean, (0, whole - snps), constant_values=1.0)
        scale = jnp.pad(scale, (0, whole - snps), constant_values=1.0)
        label = jnp.pad(label, (0, whole - snps), constant_values=-1)
    mean, scale, label = mean[None, :], scale[None, :], label[None, :]
    genotype, probe_bits, phenotype = [
        pltpu.with_memory_space_constraint(value, pltpu.HBM)
        for value in (genotype, probe_bits, phenotype)
    ]

    def moments(distances, given, extra, name):
        slots = len(distances)
        opening = extra[0] is probe_bits
        taken = int(not opening and extra[0] is not None)
        extra = [value for value in extra if value is not None]
        fetched = slots - taken
        out_shape = [
            jax.ShapeDtypeStruct((slots, rows, block), BF16),
            jax.ShapeDtypeStruct((slots, SUBLANES, span * 3 // 2), BF16),
            jax.ShapeDtypeStruct((slots, 2, block), F32),
        ]
        if opening:
            out_shape.append(jax.ShapeDtypeStruct((ROWS, rows), F32))
        if given is not None:
            out_shape.append(jax.ShapeDtypeStruct((rows, block), jnp.int32))
        scratch = []
        if fetched:
            scratch += [VMEM((fetched, rows, block), jnp.int32), pltpu.SemaphoreType.DMA((fetched,))]
        if given is not None:
            scratch.append(pltpu.SemaphoreType.DMA)
        if opening:
            scratch += [
                VMEM(probe_bits.shape, jnp.int32),
                VMEM((rows,), BF16),
                pltpu.SemaphoreType.DMA((2,)),
            ]
        return pl.pallas_call(
            functools.partial(moments_kernel, snps, distances, opening, taken, given),
            in_specs=[in_hbm()] + [in_hbm() if opening else in_vmem()] * len(extra),
            out_specs=[in_vmem()] * len(out_shape),
            scratch_shapes=scratch,
            out_shape=out_shape,
            cost_estimate=cost(1, 4 * rows * block * slots if slots > 1 else 1),
            compiler_params=params(20),
            name=name,
        )(genotype, *extra)

    here_order = [n - 2] + list(range(2, n - 2, 2))
    away_order = [d + 1 for d in here_order]

    def plain(kernel, operands, out_shape, name, **options):
        return pl.pallas_call(
            kernel,
            in_specs=[in_vmem()] * len(operands),
            out_specs=[in_vmem()] * len(out_shape),
            out_shape=out_shape,
            compiler_params=params(20),
            name=name,
            **options,
        )(*operands)

    kept_away, away, local_away, left, raw = moments(
        away_order, here_order[0], (probe_bits, phenotype), "moments_away"
    )
    away = swap(away, "ind", n, 1)
    kept_here, here, local_here = moments(here_order, None, (raw, left), "moments_here")
    packed = jax.ShapeDtypeStruct((SUBLANES, span * 3 // 2), BF16)
    *sums, left = plain(
        cores_kernel,
        (left, here, away),
        [packed] * (chips - 1) + [jax.ShapeDtypeStruct(left.shape, F32)],
        "cores",
    )
    sums = [swap(value, "ind", n, d) for value, d in zip(sums, here_order)]
    kept_near, near, local_near, raw = moments([1], 0, (None, left), "moments_near")
    near = swap(near, "ind", n, 1)
    kept_own, own, local_own = moments([0], None, (raw, left), "moments_own")

    u, trait = plain(
        weights_kernel,
        (mean, scale, own, near, *sums),
        [
            jax.ShapeDtypeStruct((SUBLANES, folded), BF16),
            jax.ShapeDtypeStruct((1, block), F32),
        ],
        "weights",
    )

    number_shape = jax.ShapeDtypeStruct((SUBLANES, LANES), F32)
    term_shape = [
        jax.ShapeDtypeStruct((rows, PROBES * SUBLANES), F32),
        jax.ShapeDtypeStruct((PROBES * SUBLANES, LANES), F32),
        number_shape,
    ]
    wide = PROBES * rows
    if folds(own_bins, wide):
        wide = wide * 3 // 4
    end_shape = [jax.ShapeDtypeStruct((SUBLANES, wide), BF16), number_shape]

    def fields(kept, blocks, us, terms, last=False):
        return plain(
            functools.partial(field_kernel, own_bins, blocks, len(kept), bool(terms), last),
            (mean, label, *kept, *us, *terms),
            end_shape if last else term_shape,
            "field",
            cost_estimate=cost(1, 1),
        )

    u_near = swap(u, "ind", n, 1)
    u_here = [swap(u, "ind", n, d) for d in here_order]
    terms = fields([kept_own, kept_near], [(0, 0), (0, 1)], [u, u_near], [])
    u_away = []
    for first in range(0, chips - 1, 2):
        slots = range(first, min(first + 2, chips - 1))
        values = []
        for slot in slots:
            shape = [jax.ShapeDtypeStruct(u.shape, u.dtype)]
            (value,) = plain(relay_kernel, (terms[2], u_here[slot]), shape, "relay")
            u_away.append(swap(value, "ind", n, 1))
            values.append(value)
        blocks = [(slot, here_order[slot]) for slot in slots]
        kept = [kept_here] * len(blocks)
        if len(blocks) == 1:
            blocks.append((0, away_order[0]))
            kept.append(kept_away)
            values.append(u_away[0])
        terms = fields(kept, blocks, values, terms)
    blocks = list(enumerate(away_order))[1:]
    flat, number = fields([kept_away], blocks, u_away[1:], terms, last=True)

    middle = n_bin // 2
    distances = [0] + [d for d in range(1, n_bin) if d != middle] + [middle]
    flats = [flat] + [swap(flat, "bin", n_bin, d) for d in distances[1:]]
    order = (rows, (away_order, here_order, [1], [0]))
    stats, field = plain(
        functools.partial(stats_kernel, own_bins, order),
        (flat, mean, scale, label, trait, local_away, local_here, local_near, local_own),
        [number_shape, jax.ShapeDtypeStruct((PROBES, own_bins, rows), BF16)],
        "stats",
    )
    (part,) = plain(
        functools.partial(pair_kernel, own_bins, PROBES * rows, distances),
        (stats, *flats),
        [number_shape],
        "pair",
    )
    pairs, common = chosen_pairs(list(range(2, n, 2)))
    part_common = swap(part, "ind", n, common)
    part = part + swap(part, "ind", n, 1)
    mine = [swap_mixed(part, n, pair) for pair in pairs]
    theirs = [swap(value, "ind", n, 1) for value in mine + [part_common]]
    pair, trace, quad = plain(
        functools.partial(final_kernel, own_bins, n_bin, len(pairs), rows * n),
        (number, part, part_common, *mine, *theirs),
        [
            jax.ShapeDtypeStruct((own_bins, BINS), F32),
            jax.ShapeDtypeStruct((1, own_bins), F32),
            jax.ShapeDtypeStruct((1, own_bins), F32),
        ],
        "final",
    )
    return jnp.transpose(field, (1, 0, 2)), pair, trace[0], quad[0]


def solution(mesh):
    placed = (P("ind", "bin"), P("bin"), P("bin"), P("bin"), P(None, "ind"), P("ind"))
    return jax.shard_map(
        shards,
        mesh=mesh,
        in_specs=placed,
        out_specs=(P("bin", None, "ind"), P("bin", None), P("bin"), P("bin")),
        check_vma=False,
    )
```

```python
import functools

import jax
import jax.numpy as jnp
from jax import lax
from jax.experimental import pallas as pl
from jax.experimental.pallas import tpu as pltpu
from jax.sharding import PartitionSpec as P

BINS = 24
PROBES = 10
LANES = 128
SUBLANES = 8
ROWS = 16
TRAIT, ONES = PROBES, PROBES + 1
TRACE_LANE, QUAD_LANE = LANES - 2, LANES - 1
PIECE = 640
DOT_PIECE = 1664
F32 = jnp.float32
BF16 = jnp.bfloat16
VMEM = pltpu.VMEM
MIB = 1 << 20


def folds(rows, width):
    return rows == 6 and width % (4 * LANES) == 0


def fold_rows(value, rows):
    width = value.shape[1]
    if not folds(rows, width):
        return value
    main = width * 3 // 4
    tail = value[:, main:]
    row = rows_iota(SUBLANES)
    result = value[:, :main]
    for at in range(2):
        line = jnp.concatenate([tail[3 * at + i : 3 * at + i + 1] for i in range(3)], axis=1)
        result = jnp.where(row == 6 + at, line, result)
    return result


def unfold_rows(value, rows, width):
    if not folds(rows, width):
        return value
    main, part = width * 3 // 4, width // 4
    row = rows_iota(SUBLANES)
    tail = jnp.zeros((SUBLANES, part), F32)
    for i in range(6):
        line = value[6 + i // 3 : 7 + i // 3, i % 3 * part : (i % 3 + 1) * part]
        tail = jnp.where(row == i, line, tail)
    return jnp.concatenate([jnp.where(row < 6, value, 0.0), tail], axis=1)


def core():
    return lax.rem(lax.axis_index("ind"), 2)


def fold_lanes(value):
    return tree_sum([value[:, at : at + LANES] for at in range(0, value.shape[1], LANES)])


def rows_iota(count, width=1):
    return lax.broadcasted_iota(jnp.int32, (count, width), 0)


def tree_sum(terms):
    terms = list(terms)
    while len(terms) > 1:
        pairs = [a + b for a, b in zip(terms[::2], terms[1::2])]
        terms = pairs + terms[len(pairs) * 2 :]
    return terms[0]


def pack_sums(value):
    half = value.shape[1] // 2
    low = value[SUBLANES:]
    turned = pltpu.roll(low[:, half:], 4, 0)
    low = jnp.where(rows_iota(SUBLANES) < 4, low[:, :half], turned)
    return value[:SUBLANES], low


def unpack_sums(value):
    span = value.shape[1] * 2 // 3
    low = value[:, span:]
    return value[:, :span], jnp.concatenate([low, pltpu.roll(low, 4, 0)], axis=1)


def moments_kernel(snps, distances, opening, taken, given, geno_ref, *rest):
    rest = list(rest)
    if opening:
        bits_ref, trait_ref, kept_ref, sums_ref, local_ref, left_ref = rest[:6]
        rest = rest[6:]
    else:
        raw_in = rest.pop(0) if taken else None
        left_ref, kept_ref, sums_ref, local_ref = rest[:4]
        rest = rest[4:]
    raw_out = rest.pop(0) if given is not None else None
    slots, rows, block = kept_ref.shape
    fetched = slots - taken
    devices = -(-snps // block)
    tail = snps - (devices - 1) * block
    span = sums_ref.shape[2] * 2 // 3

    def copy(distance, target, semaphore, width):
        start = pl.multiple_of((lax.axis_index("ind") ^ distance) * block, LANES)
        return pltpu.make_async_copy(
            geno_ref.at[:, pl.ds(start, width)], target.at[:, pl.ds(0, width)], semaphore
        )

    def whole_or_tail(distance, target, semaphore, act):
        if tail == block:
            act(copy(distance, target, semaphore, block))
        else:
            last = (lax.axis_index("ind") ^ distance) == devices - 1
            pl.when(last)(lambda: act(copy(distance, target, semaphore, tail)))
            pl.when(jnp.logical_not(last))(lambda: act(copy(distance, target, semaphore, block)))

    if fetched:
        buffer, arrived = rest[:2]
        rest = rest[2:]

        def fetch(index, act):
            distance = distances[taken]
            for slot in range(taken + 1, slots):
                distance = jnp.where(index + taken == slot, distances[slot], distance)
            whole_or_tail(distance, buffer.at[index], arrived.at[index], act)

    if raw_out is not None:
        raw_arrived = rest.pop(0)

    if opening:
        bits, trait, small = rest[:3]
        bits_copy = pltpu.make_async_copy(bits_ref, bits, small.at[0])
        trait_copy = pltpu.make_async_copy(trait_ref, trait, small.at[1])
        bits_copy.start()
        trait_copy.start()
    if fetched:
        pl.loop(0, fetched)(lambda index: fetch(index, lambda c: c.start()))
    if raw_out is not None:
        whole_or_tail(given, raw_out, raw_arrived, lambda c: c.start())
    if opening:
        bits_copy.wait()
        trait_copy.wait()
        left_ref[...] = jnp.zeros_like(left_ref)
        left_ref[0:PROBES] = (2 * bits[...] - 1).astype(F32)
        left_ref[TRAIT : TRAIT + 1] = trait[...].astype(F32).reshape(1, rows)
        left_ref[ONES : ONES + 1] = jnp.ones((1, rows), F32)
    left = left_ref[...]
    base = jnp.sum(left, axis=1, keepdims=True)
    left = left.astype(BF16)
    row = rows_iota(ROWS)

    def with_low(value):
        high = value[TRAIT : TRAIT + 1]
        return jnp.where(row == TRAIT + 1, high - high.astype(BF16).astype(F32), value)

    ends = jnp.broadcast_to(with_low(base), (ROWS, span - block))

    def work(slot, source):
        squares = []
        for at in range(0, block, PIECE):
            lanes = slice(at, min(at + PIECE, block))
            for r in range(0, rows, 16):
                dose = source[r : r + 16, lanes].astype(F32).astype(BF16)
                kept_ref[slot, r : r + 16, lanes] = dose
                square = dose * dose if r == 0 else square + dose * dose
            squares.append(jnp.sum(square.astype(F32), axis=0, keepdims=True))
        total = jnp.dot(left, kept_ref[slot], preferred_element_type=F32) - base
        ones = total[ONES : ONES + 1]
        local_ref[slot, 0:1] = ones
        local_ref[slot, 1:2] = jnp.concatenate(squares, axis=1) - 2.0 * ones - rows
        high, low = pack_sums(jnp.concatenate([with_low(total), ends], axis=1))
        sums_ref[slot, :, :span] = high.astype(BF16)
        sums_ref[slot, :, span:] = low.astype(BF16)

    if taken:
        work(0, raw_in)
    if fetched:

        @pl.loop(0, fetched)
        def _(index):
            fetch(index, lambda c: c.wait())
            work(index + taken, buffer.at[index])

    if raw_out is not None:
        whole_or_tail(given, raw_out, raw_arrived, lambda c: c.wait())


def cores_kernel(left_ref, here_ref, away_ref, *outs):
    outs, left_out = outs[:-1], outs[-1]
    left_out[...] = left_ref[...]
    for index, out in enumerate(outs):
        out[...] = (here_ref[index].astype(F32) + away_ref[index].astype(F32)).astype(BF16)


def relay_kernel(token_ref, value_ref, out_ref):
    out_ref[...] = value_ref[...]


def weights_kernel(mean_ref, scale_ref, own_ref, near_ref, *refs):
    parts, (u_ref, trait_ref) = refs[:-2], refs[-2:]
    block = trait_ref.shape[1]
    width = u_ref.shape[1] - block
    here = pl.ds(pl.multiple_of(lax.axis_index("ind") * block, LANES), block)
    parts = [own_ref[0], near_ref[0]] + [part[...] for part in parts]
    total = tree_sum([part.astype(F32) for part in parts])
    shift = mean_ref[:, here] - 1.0
    inverse = 1.0 / scale_ref[:, here]
    high, low = [
        (part[:, :block] - part[:, block : block + 1] * shift) * inverse
        for part in unpack_sums(total)
    ]
    trait_ref[...] = low[2:3] + low[3:4]
    high, low = [part.astype(BF16).astype(F32) * inverse for part in (high, low)]
    low = jnp.concatenate([low, jnp.zeros((SUBLANES, 4 * width - block), F32)], axis=1)
    folded = low[:, :width]
    for j in range(1, 4):
        turned = pltpu.roll(low[:, j * width : (j + 1) * width], 2 * j, 0)
        folded = jnp.where(rows_iota(SUBLANES) < 2 * j, folded, turned)
    u_ref[:, :block] = high.astype(BF16)
    u_ref[:, block:] = folded.astype(BF16)


def stats_kernel(own_bins, order, flat_ref, mean_ref, scale_ref, label_ref, trait_ref, *rest):
    locals_, (out_ref, field_ref) = rest[:-2], rest[-2:]
    block = trait_ref.shape[1]
    rows = order[0]
    bins = rows_iota(SUBLANES)

    def member_of(owner):
        here = pl.ds(pl.multiple_of(owner * block, LANES), block)
        member = label_ref[:, here] - lax.axis_index("bin") * own_bins == bins
        return here, member & (bins < own_bins)

    trace = jnp.zeros((SUBLANES, 1), F32)
    for ref, distances in zip(locals_, order[1]):
        for slot, distance in enumerate(distances):
            here, member = member_of(lax.axis_index("ind") ^ distance)
            shift = mean_ref[:, here] - 1.0
            inverse = 1.0 / scale_ref[:, here]
            square = ref[slot, 1:2] - 2.0 * shift * ref[slot, 0:1] + rows * shift * shift
            square = square * (inverse * inverse)
            trace += jnp.sum(jnp.where(member, square, 0.0), axis=1, keepdims=True)
    _, member = member_of(lax.axis_index("ind"))
    trait = trait_ref[...]
    quad = jnp.sum(jnp.where(member, trait * trait, 0.0), axis=1, keepdims=True)
    lane = lax.broadcasted_iota(jnp.int32, (SUBLANES, LANES), 1)
    out_ref[...] = jnp.where(lane == TRACE_LANE, trace, jnp.where(lane == QUAD_LANE, quad, 0.0))
    flat = unfold_rows(flat_ref[...].astype(F32), own_bins, PROBES * rows)
    for b in range(PROBES):
        field_ref[b] = flat[:own_bins, b * rows : (b + 1) * rows].astype(BF16)


def field_kernel(own_bins, blocks, sources, started, last, *refs):
    refs = list(refs)
    mean_ref, label_ref = refs[:2]
    kept_refs, refs = refs[2 : 2 + sources], refs[2 + sources :]
    u_refs, refs = refs[: len(blocks)], refs[len(blocks) :]
    rows, block = kept_refs[0].shape[1:]
    bins = rows_iota(SUBLANES)
    if started:
        acc, offset, number = [ref[...] for ref in refs[:3]]
        refs = refs[3:]
    else:
        acc = jnp.zeros((rows, PROBES * SUBLANES), F32)
        offset = jnp.zeros((PROBES * SUBLANES, LANES), F32)
        number = jnp.zeros((SUBLANES, LANES), F32)
    for index, (slot, distance) in enumerate(blocks):
        start = (lax.axis_index("ind") ^ distance) * block
        u = u_refs[index][...].astype(F32)
        lines = [u[b : b + 1, :block] for b in range(SUBLANES)]
        for b in range(PROBES - SUBLANES):
            line = [u[2 * j + b : 2 * j + b + 1, block:] for j in range(4)]
            lines.append(jnp.concatenate(line, axis=1)[:, :block])
        for at in range(0, block, DOT_PIECE):
            width = min(DOT_PIECE, block - at)
            here = pl.ds(pl.multiple_of(start + at, LANES), width)
            member = label_ref[:, here] - lax.axis_index("bin") * own_bins == bins
            member = member & (bins < own_bins)
            mean = mean_ref[:, here]
            spread = [jnp.where(member, line[:, at : at + width], 0.0) for line in lines]
            offset += jnp.concatenate([fold_lanes(value * mean) for value in spread], axis=0)
            number += fold_lanes(jnp.where(member, 1.0, 0.0))
            acc += lax.dot_general(
                kept_refs[index if sources > 1 else 0][slot, :, at : at + width],
                jnp.concatenate(spread, axis=0).astype(BF16),
                (((1,), (1,)), ((), ())),
                preferred_element_type=F32,
            )
    if not last:
        for ref, value in zip(refs, (acc, offset, number)):
            ref[...] = value
        return
    flat_ref, count_ref = refs
    acc = jnp.concatenate([acc, jnp.zeros((rows, LANES - acc.shape[1]), F32)], axis=1)
    acc = jnp.transpose(acc)[: PROBES * SUBLANES] - jnp.sum(offset, axis=1, keepdims=True)
    number = jnp.sum(number, axis=1, keepdims=True)
    count_ref[...] = jnp.broadcast_to(number, count_ref.shape)
    inverse = 1.0 / jnp.maximum(number, 1.0)
    flat = [acc[b * SUBLANES : (b + 1) * SUBLANES] * inverse for b in range(PROBES)]
    flat_ref[...] = fold_rows(jnp.concatenate(flat, axis=1), own_bins).astype(BF16)


def pair_kernel(own_bins, width, distances, stats_ref, *rest):
    flats, out_ref = rest[:-1], rest[-1]
    everyone = [unfold_rows(flat[...].astype(F32), own_bins, width) for flat in flats]
    own = everyone[0].astype(BF16)
    everyone = [everyone[distances.index(d)] for d in range(len(distances))]
    everyone += [jnp.zeros_like(everyone[0])] * (LANES // SUBLANES - len(flats))
    out_ref[...] = stats_ref[...] + lax.dot_general(
        own,
        jnp.concatenate(everyone, axis=0).astype(BF16),
        (((1,), (1,)), ((), ())),
        preferred_element_type=F32,
    )


def final_kernel(own_bins, n_bin, pairs, total_rows, count_ref, own_ref, common_ref, *rest):
    mine, theirs, outs = rest[:pairs], rest[pairs : 2 * pairs + 1], rest[2 * pairs + 1 :]
    pair_ref, trace_ref, quad_ref = outs
    terms = [own_ref[...]]
    even = core() == 0
    for ref, other in zip(mine, theirs):
        terms.append(jnp.where(even, ref[...], other[...]))
        terms.append(jnp.where(even, other[...], ref[...]))
    terms.append(common_ref[...] + theirs[pairs][...])
    total = tree_sum(terms)
    row = lax.broadcasted_iota(jnp.int32, (SUBLANES, LANES), 0)
    lane = lax.broadcasted_iota(jnp.int32, (SUBLANES, LANES), 1)
    pair = jnp.zeros_like(total)
    for slot in range(n_bin):
        start = slot * SUBLANES
        part = jnp.where((lane >= start) & (lane < start + own_bins), total, 0.0)
        shift = (lax.axis_index("bin") ^ slot) * own_bins - start + LANES
        pair = pair + pltpu.roll(part, lax.rem(shift, LANES), 1)
    pair_ref[...] = pair[:own_bins, :BINS] / (PROBES * total_rows)
    scaled = total / (count_ref[...] * total_rows)
    for ref, column in ((trace_ref, TRACE_LANE), (quad_ref, QUAD_LANE)):
        turned = jnp.where(row == lane, scaled[:, column : column + 1], 0.0)
        ref[...] = jnp.sum(turned, axis=0, keepdims=True)[:, :own_bins]


def swap(value, axis, size, distance):
    return lax.ppermute(value, axis, [(i, i ^ distance) for i in range(size)])


def swap_mixed(value, size, pair):
    return lax.ppermute(value, "ind", [(i, i ^ pair[i % 2]) for i in range(size)])


def chosen_pairs(distances):
    return list(zip(distances[:-1:2], distances[1:-1:2])), distances[-1]


def in_vmem():
    return pl.BlockSpec(memory_space=VMEM)


def in_hbm():
    return pl.BlockSpec(memory_space=pltpu.HBM)


def params(mib):
    return pltpu.CompilerParams(vmem_limit_bytes=mib * MIB)


def cost(flops, moved):
    return pl.CostEstimate(flops=flops, bytes_accessed=moved, transcendentals=0)


def shards(genotype, snp_mean, snp_scale, snp_label, probe_bits, phenotype):
    n = lax.axis_size("ind")
    n_bin = lax.axis_size("bin")
    chips = n // 2
    own_bins = BINS // n_bin
    rows, snps = genotype.shape
    tiles = -(-snps // LANES)
    block_tiles = -(-tiles // n)
    block = block_tiles * LANES
    span = block + LANES * (2 - block_tiles % 2)
    folded = block + -(-block_tiles // 4) * LANES
    whole = n * block
    mean, scale, label = snp_mean, snp_scale, snp_label
    if whole != snps:
        mean = jnp.pad(mean, (0, whole - snps), constant_values=1.0)
        scale = jnp.pad(scale, (0, whole - snps), constant_values=1.0)
        label = jnp.pad(label, (0, whole - snps), constant_values=-1)
    mean, scale, label = mean[None, :], scale[None, :], label[None, :]
    genotype, probe_bits, phenotype = [
        pltpu.with_memory_space_constraint(value, pltpu.HBM)
        for value in (genotype, probe_bits, phenotype)
    ]

    def moments(distances, given, extra, name):
        slots = len(distances)
        opening = extra[0] is probe_bits
        taken = int(not opening and extra[0] is not None)
        extra = [value for value in extra if value is not None]
        fetched = slots - taken
        out_shape = [
            jax.ShapeDtypeStruct((slots, rows, block), BF16),
            jax.ShapeDtypeStruct((slots, SUBLANES, span * 3 // 2), BF16),
            jax.ShapeDtypeStruct((slots, 2, block), F32),
        ]
        if opening:
            out_shape.append(jax.ShapeDtypeStruct((ROWS, rows), F32))
        if given is not None:
            out_shape.append(jax.ShapeDtypeStruct((rows, block), jnp.int32))
        scratch = []
        if fetched:
            scratch += [VMEM((fetched, rows, block), jnp.int32), pltpu.SemaphoreType.DMA((fetched,))]
        if given is not None:
            scratch.append(pltpu.SemaphoreType.DMA)
        if opening:
            scratch += [
                VMEM(probe_bits.shape, jnp.int32),
                VMEM((rows,), BF16),
                pltpu.SemaphoreType.DMA((2,)),
            ]
        return pl.pallas_call(
            functools.partial(moments_kernel, snps, distances, opening, taken, given),
            in_specs=[in_hbm()] + [in_hbm() if opening else in_vmem()] * len(extra),
            out_specs=[in_vmem()] * len(out_shape),
            scratch_shapes=scratch,
            out_shape=out_shape,
            cost_estimate=cost(1, 4 * rows * block * slots if slots > 1 else 1),
            compiler_params=params(20),
            name=name,
        )(genotype, *extra)

    here_order = [n - 2] + list(range(2, n - 2, 2))
    away_order = [d + 1 for d in here_order]

    def plain(kernel, operands, out_shape, name, **options):
        return pl.pallas_call(
            kernel,
            in_specs=[in_vmem()] * len(operands),
            out_specs=[in_vmem()] * len(out_shape),
            out_shape=out_shape,
            compiler_params=params(20),
            name=name,
            **options,
        )(*operands)

    kept_away, away, local_away, left, raw = moments(
        away_order, here_order[0], (probe_bits, phenotype), "moments_away"
    )
    away = swap(away, "ind", n, 1)
    kept_here, here, local_here = moments(here_order, None, (raw, left), "moments_here")
    packed = jax.ShapeDtypeStruct((SUBLANES, span * 3 // 2), BF16)
    *sums, left = plain(
        cores_kernel,
        (left, here, away),
        [packed] * (chips - 1) + [jax.ShapeDtypeStruct(left.shape, F32)],
        "cores",
    )
    sums = [swap(value, "ind", n, d) for value, d in zip(sums, here_order)]
    kept_near, near, local_near, raw = moments([1], 0, (None, left), "moments_near")
    near = swap(near, "ind", n, 1)
    kept_own, own, local_own = moments([0], None, (raw, left), "moments_own")

    u, trait = plain(
        weights_kernel,
        (mean, scale, own, near, *sums),
        [
            jax.ShapeDtypeStruct((SUBLANES, folded), BF16),
            jax.ShapeDtypeStruct((1, block), F32),
        ],
        "weights",
    )

    number_shape = jax.ShapeDtypeStruct((SUBLANES, LANES), F32)
    term_shape = [
        jax.ShapeDtypeStruct((rows, PROBES * SUBLANES), F32),
        jax.ShapeDtypeStruct((PROBES * SUBLANES, LANES), F32),
        number_shape,
    ]
    wide = PROBES * rows
    if folds(own_bins, wide):
        wide = wide * 3 // 4
    end_shape = [jax.ShapeDtypeStruct((SUBLANES, wide), BF16), number_shape]

    def fields(kept, blocks, us, terms, last=False):
        return plain(
            functools.partial(field_kernel, own_bins, blocks, len(kept), bool(terms), last),
            (mean, label, *kept, *us, *terms),
            end_shape if last else term_shape,
            "field",
            cost_estimate=cost(1, 1),
        )

    u_near = swap(u, "ind", n, 1)
    u_here = [swap(u, "ind", n, d) for d in here_order]
    terms = fields([kept_own, kept_near], [(0, 0), (0, 1)], [u, u_near], [])
    u_away = []
    for first in range(0, chips - 1, 2):
        slots = range(first, min(first + 2, chips - 1))
        values = []
        for slot in slots:
            shape = [jax.ShapeDtypeStruct(u.shape, u.dtype)]
            (value,) = plain(relay_kernel, (terms[2], u_here[slot]), shape, "relay")
            u_away.append(swap(value, "ind", n, 1))
            values.append(value)
        blocks = [(slot, here_order[slot]) for slot in slots]
        kept = [kept_here] * len(blocks)
        if len(blocks) == 1:
            blocks.append((0, away_order[0]))
            kept.append(kept_away)
            values.append(u_away[0])
        terms = fields(kept, blocks, values, terms)
    blocks = list(enumerate(away_order))[1:]
    flat, number = fields([kept_away], blocks, u_away[1:], terms, last=True)

    middle = n_bin // 2
    distances = [0] + [d for d in range(1, n_bin) if d != middle] + [middle]
    flats = [flat] + [swap(flat, "bin", n_bin, d) for d in distances[1:]]
    order = (rows, (away_order, here_order, [1], [0]))
    stats, field = plain(
        functools.partial(stats_kernel, own_bins, order),
        (flat, mean, scale, label, trait, local_away, local_here, local_near, local_own),
        [number_shape, jax.ShapeDtypeStruct((PROBES, own_bins, rows), BF16)],
        "stats",
    )
    (part,) = plain(
        functools.partial(pair_kernel, own_bins, PROBES * rows, distances),
        (stats, *flats),
        [number_shape],
        "pair",
    )
    pairs, common = chosen_pairs(list(range(2, n, 2)))
    part_common = swap(part, "ind", n, common)
    part = part + swap(part, "ind", n, 1)
    mine = [swap_mixed(part, n, pair) for pair in pairs]
    theirs = [swap(value, "ind", n, 1) for value in mine + [part_common]]
    pair, trace, quad = plain(
        functools.partial(final_kernel, own_bins, n_bin, len(pairs), rows * n),
        (number, part, part_common, *mine, *theirs),
        [
            jax.ShapeDtypeStruct((own_bins, BINS), F32),
            jax.ShapeDtypeStruct((1, own_bins), F32),
            jax.ShapeDtypeStruct((1, own_bins), F32),
        ],
        "final",
    )
    return jnp.transpose(field, (1, 0, 2)), pair, trace[0], quad[0]


def solution(mesh):
    placed = (P("ind", "bin"), P("bin"), P("bin"), P("bin"), P(None, "ind"), P("ind"))
    return jax.shard_map(
        shards,
        mesh=mesh,
        in_specs=placed,
        out_specs=(P("bin", None, "ind"), P("bin", None), P("bin"), P("bin")),
        check_vma=False,
    )
```

```python
import functools

import jax
import jax.numpy as jnp
from jax import lax
from jax.experimental import pallas as pl
from jax.experimental.pallas import tpu as pltpu
from jax.sharding import PartitionSpec as P

BINS = 24
PROBES = 10
LANES = 128
SUBLANES = 8
ROWS = 16
TRAIT, ONES = PROBES, PROBES + 1
TRACE_LANE, QUAD_LANE = LANES - 2, LANES - 1
PIECE = 1664
DOT_PIECE = 1664
F32 = jnp.float32
BF16 = jnp.bfloat16
VMEM = pltpu.VMEM
MIB = 1 << 20


def folds(rows, width):
    return rows == 6 and width % (4 * LANES) == 0


def fold_rows(value, rows):
    width = value.shape[1]
    if not folds(rows, width):
        return value
    main = width * 3 // 4
    tail = value[:, main:]
    row = rows_iota(SUBLANES)
    result = value[:, :main]
    for at in range(2):
        line = jnp.concatenate([tail[3 * at + i : 3 * at + i + 1] for i in range(3)], axis=1)
        result = jnp.where(row == 6 + at, line, result)
    return result


def unfold_rows(value, rows, width):
    if not folds(rows, width):
        return value
    main, part = width * 3 // 4, width // 4
    row = rows_iota(SUBLANES)
    tail = jnp.zeros((SUBLANES, part), F32)
    for i in range(6):
        line = value[6 + i // 3 : 7 + i // 3, i % 3 * part : (i % 3 + 1) * part]
        tail = jnp.where(row == i, line, tail)
    return jnp.concatenate([jnp.where(row < 6, value, 0.0), tail], axis=1)


def core():
    return lax.rem(lax.axis_index("ind"), 2)


def fold_lanes(value):
    return tree_sum([value[:, at : at + LANES] for at in range(0, value.shape[1], LANES)])


def rows_iota(count, width=1):
    return lax.broadcasted_iota(jnp.int32, (count, width), 0)


def tree_sum(terms):
    terms = list(terms)
    while len(terms) > 1:
        pairs = [a + b for a, b in zip(terms[::2], terms[1::2])]
        terms = pairs + terms[len(pairs) * 2 :]
    return terms[0]


def pack_sums(value):
    half = value.shape[1] // 2
    low = value[SUBLANES:]
    turned = pltpu.roll(low[:, half:], 4, 0)
    low = jnp.where(rows_iota(SUBLANES) < 4, low[:, :half], turned)
    return value[:SUBLANES], low


def unpack_sums(value):
    span = value.shape[1] * 2 // 3
    low = value[:, span:]
    return value[:, :span], jnp.concatenate([low, pltpu.roll(low, 4, 0)], axis=1)


def moments_kernel(snps, distances, opening, taken, given, geno_ref, *rest):
    rest = list(rest)
    if opening:
        bits_ref, trait_ref, kept_ref, sums_ref, local_ref, left_ref = rest[:6]
        rest = rest[6:]
    else:
        raw_in = rest.pop(0) if taken else None
        left_ref, kept_ref, sums_ref, local_ref = rest[:4]
        rest = rest[4:]
    raw_out = rest.pop(0) if given is not None else None
    slots, rows, block = kept_ref.shape
    fetched = slots - taken
    devices = -(-snps // block)
    tail = snps - (devices - 1) * block
    span = sums_ref.shape[2] * 2 // 3

    def copy(distance, target, semaphore, width):
        start = pl.multiple_of((lax.axis_index("ind") ^ distance) * block, LANES)
        return pltpu.make_async_copy(
            geno_ref.at[:, pl.ds(start, width)], target.at[:, pl.ds(0, width)], semaphore
        )

    def whole_or_tail(distance, target, semaphore, act):
        if tail == block:
            act(copy(distance, target, semaphore, block))
        else:
            last = (lax.axis_index("ind") ^ distance) == devices - 1
            pl.when(last)(lambda: act(copy(distance, target, semaphore, tail)))
            pl.when(jnp.logical_not(last))(lambda: act(copy(distance, target, semaphore, block)))

    if fetched:
        buffer, arrived = rest[:2]
        rest = rest[2:]

        def fetch(index, act):
            distance = distances[taken]
            for slot in range(taken + 1, slots):
                distance = jnp.where(index + taken == slot, distances[slot], distance)
            whole_or_tail(distance, buffer.at[index], arrived.at[index], act)

    if raw_out is not None:
        raw_arrived = rest.pop(0)

    if opening:
        bits, trait, small = rest[:3]
        bits_copy = pltpu.make_async_copy(bits_ref, bits, small.at[0])
        trait_copy = pltpu.make_async_copy(trait_ref, trait, small.at[1])
        bits_copy.start()
        trait_copy.start()
    if fetched:
        pl.loop(0, fetched)(lambda index: fetch(index, lambda c: c.start()))
    if raw_out is not None:
        whole_or_tail(given, raw_out, raw_arrived, lambda c: c.start())
    if opening:
        bits_copy.wait()
        trait_copy.wait()
        left_ref[...] = jnp.zeros_like(left_ref)
        left_ref[0:PROBES] = (2 * bits[...] - 1).astype(F32)
        left_ref[TRAIT : TRAIT + 1] = trait[...].astype(F32).reshape(1, rows)
        left_ref[ONES : ONES + 1] = jnp.ones((1, rows), F32)
    left = left_ref[...]
    base = jnp.sum(left, axis=1, keepdims=True)
    left = left.astype(BF16)
    row = rows_iota(ROWS)

    def with_low(value):
        high = value[TRAIT : TRAIT + 1]
        return jnp.where(row == TRAIT + 1, high - high.astype(BF16).astype(F32), value)

    ends = jnp.broadcast_to(with_low(base), (ROWS, span - block))

    def work(slot, source):
        squares = []
        for at in range(0, block, PIECE):
            lanes = slice(at, min(at + PIECE, block))
            for r in range(0, rows, 16):
                dose = source[r : r + 16, lanes].astype(F32).astype(BF16)
                kept_ref[slot, r : r + 16, lanes] = dose
                square = dose * dose if r == 0 else square + dose * dose
            squares.append(jnp.sum(square.astype(F32), axis=0, keepdims=True))
        total = jnp.dot(left, kept_ref[slot], preferred_element_type=F32) - base
        ones = total[ONES : ONES + 1]
        local_ref[slot, 0:1] = ones
        local_ref[slot, 1:2] = jnp.concatenate(squares, axis=1) - 2.0 * ones - rows
        high, low = pack_sums(jnp.concatenate([with_low(total), ends], axis=1))
        sums_ref[slot, :, :span] = high.astype(BF16)
        sums_ref[slot, :, span:] = low.astype(BF16)

    if taken:
        work(0, raw_in)
    if fetched:

        @pl.loop(0, fetched)
        def _(index):
            fetch(index, lambda c: c.wait())
            work(index + taken, buffer.at[index])

    if raw_out is not None:
        whole_or_tail(given, raw_out, raw_arrived, lambda c: c.wait())


def cores_kernel(left_ref, here_ref, away_ref, *outs):
    outs, left_out = outs[:-1], outs[-1]
    left_out[...] = left_ref[...]
    for index, out in enumerate(outs):
        out[...] = (here_ref[index].astype(F32) + away_ref[index].astype(F32)).astype(BF16)


def relay_kernel(token_ref, value_ref, out_ref):
    out_ref[...] = value_ref[...]


def weights_kernel(mean_ref, scale_ref, own_ref, near_ref, *refs):
    parts, (u_ref, trait_ref) = refs[:-2], refs[-2:]
    block = trait_ref.shape[1]
    width = u_ref.shape[1] - block
    here = pl.ds(pl.multiple_of(lax.axis_index("ind") * block, LANES), block)
    parts = [own_ref[0], near_ref[0]] + [part[...] for part in parts]
    total = tree_sum([part.astype(F32) for part in parts])
    shift = mean_ref[:, here] - 1.0
    inverse = 1.0 / scale_ref[:, here]
    high, low = [
        (part[:, :block] - part[:, block : block + 1] * shift) * inverse
        for part in unpack_sums(total)
    ]
    trait_ref[...] = low[2:3] + low[3:4]
    high, low = [part.astype(BF16).astype(F32) * inverse for part in (high, low)]
    low = jnp.concatenate([low, jnp.zeros((SUBLANES, 4 * width - block), F32)], axis=1)
    folded = low[:, :width]
    for j in range(1, 4):
        turned = pltpu.roll(low[:, j * width : (j + 1) * width], 2 * j, 0)
        folded = jnp.where(rows_iota(SUBLANES) < 2 * j, folded, turned)
    u_ref[:, :block] = high.astype(BF16)
    u_ref[:, block:] = folded.astype(BF16)


def stats_kernel(own_bins, order, flat_ref, mean_ref, scale_ref, label_ref, trait_ref, *rest):
    locals_, (out_ref, field_ref) = rest[:-2], rest[-2:]
    block = trait_ref.shape[1]
    rows = order[0]
    bins = rows_iota(SUBLANES)

    def member_of(owner):
        here = pl.ds(pl.multiple_of(owner * block, LANES), block)
        member = label_ref[:, here] - lax.axis_index("bin") * own_bins == bins
        return here, member & (bins < own_bins)

    trace = jnp.zeros((SUBLANES, 1), F32)
    for ref, distances in zip(locals_, order[1]):
        for slot, distance in enumerate(distances):
            here, member = member_of(lax.axis_index("ind") ^ distance)
            shift = mean_ref[:, here] - 1.0
            inverse = 1.0 / scale_ref[:, here]
            square = ref[slot, 1:2] - 2.0 * shift * ref[slot, 0:1] + rows * shift * shift
            square = square * (inverse * inverse)
            trace += jnp.sum(jnp.where(member, square, 0.0), axis=1, keepdims=True)
    _, member = member_of(lax.axis_index("ind"))
    trait = trait_ref[...]
    quad = jnp.sum(jnp.where(member, trait * trait, 0.0), axis=1, keepdims=True)
    lane = lax.broadcasted_iota(jnp.int32, (SUBLANES, LANES), 1)
    out_ref[...] = jnp.where(lane == TRACE_LANE, trace, jnp.where(lane == QUAD_LANE, quad, 0.0))
    flat = unfold_rows(flat_ref[...].astype(F32), own_bins, PROBES * rows)
    for b in range(PROBES):
        field_ref[b] = flat[:own_bins, b * rows : (b + 1) * rows].astype(BF16)


def field_kernel(own_bins, blocks, sources, started, last, *refs):
    refs = list(refs)
    mean_ref, label_ref = refs[:2]
    kept_refs, refs = refs[2 : 2 + sources], refs[2 + sources :]
    u_refs, refs = refs[: len(blocks)], refs[len(blocks) :]
    rows, block = kept_refs[0].shape[1:]
    bins = rows_iota(SUBLANES)
    if started:
        acc, offset, number = [ref[...] for ref in refs[:3]]
        refs = refs[3:]
    else:
        acc = jnp.zeros((rows, PROBES * SUBLANES), F32)
        offset = jnp.zeros((PROBES * SUBLANES, LANES), F32)
        number = jnp.zeros((SUBLANES, LANES), F32)
    for index, (slot, distance) in enumerate(blocks):
        start = (lax.axis_index("ind") ^ distance) * block
        u = u_refs[index][...].astype(F32)
        lines = [u[b : b + 1, :block] for b in range(SUBLANES)]
        for b in range(PROBES - SUBLANES):
            line = [u[2 * j + b : 2 * j + b + 1, block:] for j in range(4)]
            lines.append(jnp.concatenate(line, axis=1)[:, :block])
        for at in range(0, block, DOT_PIECE):
            width = min(DOT_PIECE, block - at)
            here = pl.ds(pl.multiple_of(start + at, LANES), width)
            member = label_ref[:, here] - lax.axis_index("bin") * own_bins == bins
            member = member & (bins < own_bins)
            mean = mean_ref[:, here]
            spread = [jnp.where(member, line[:, at : at + width], 0.0) for line in lines]
            offset += jnp.concatenate([fold_lanes(value * mean) for value in spread], axis=0)
            number += fold_lanes(jnp.where(member, 1.0, 0.0))
            acc += lax.dot_general(
                kept_refs[index if sources > 1 else 0][slot, :, at : at + width],
                jnp.concatenate(spread, axis=0).astype(BF16),
                (((1,), (1,)), ((), ())),
                preferred_element_type=F32,
            )
    if not last:
        for ref, value in zip(refs, (acc, offset, number)):
            ref[...] = value
        return
    flat_ref, count_ref = refs
    acc = jnp.concatenate([acc, jnp.zeros((rows, LANES - acc.shape[1]), F32)], axis=1)
    acc = jnp.transpose(acc)[: PROBES * SUBLANES] - jnp.sum(offset, axis=1, keepdims=True)
    number = jnp.sum(number, axis=1, keepdims=True)
    count_ref[...] = jnp.broadcast_to(number, count_ref.shape)
    inverse = 1.0 / jnp.maximum(number, 1.0)
    flat = [acc[b * SUBLANES : (b + 1) * SUBLANES] * inverse for b in range(PROBES)]
    flat_ref[...] = fold_rows(jnp.concatenate(flat, axis=1), own_bins).astype(BF16)


def pair_kernel(own_bins, width, distances, stats_ref, *rest):
    flats, out_ref = rest[:-1], rest[-1]
    everyone = [unfold_rows(flat[...].astype(F32), own_bins, width) for flat in flats]
    own = everyone[0].astype(BF16)
    everyone = [everyone[distances.index(d)] for d in range(len(distances))]
    everyone += [jnp.zeros_like(everyone[0])] * (LANES // SUBLANES - len(flats))
    out_ref[...] = stats_ref[...] + lax.dot_general(
        own,
        jnp.concatenate(everyone, axis=0).astype(BF16),
        (((1,), (1,)), ((), ())),
        preferred_element_type=F32,
    )


def final_kernel(own_bins, n_bin, pairs, total_rows, count_ref, own_ref, common_ref, *rest):
    mine, theirs, outs = rest[:pairs], rest[pairs : 2 * pairs + 1], rest[2 * pairs + 1 :]
    pair_ref, trace_ref, quad_ref = outs
    terms = [own_ref[...]]
    even = core() == 0
    for ref, other in zip(mine, theirs):
        terms.append(jnp.where(even, ref[...], other[...]))
        terms.append(jnp.where(even, other[...], ref[...]))
    terms.append(common_ref[...] + theirs[pairs][...])
    total = tree_sum(terms)
    row = lax.broadcasted_iota(jnp.int32, (SUBLANES, LANES), 0)
    lane = lax.broadcasted_iota(jnp.int32, (SUBLANES, LANES), 1)
    pair = jnp.zeros_like(total)
    for slot in range(n_bin):
        start = slot * SUBLANES
        part = jnp.where((lane >= start) & (lane < start + own_bins), total, 0.0)
        shift = (lax.axis_index("bin") ^ slot) * own_bins - start + LANES
        pair = pair + pltpu.roll(part, lax.rem(shift, LANES), 1)
    pair_ref[...] = pair[:own_bins, :BINS] / (PROBES * total_rows)
    scaled = total / (count_ref[...] * total_rows)
    for ref, column in ((trace_ref, TRACE_LANE), (quad_ref, QUAD_LANE)):
        turned = jnp.where(row == lane, scaled[:, column : column + 1], 0.0)
        ref[...] = jnp.sum(turned, axis=0, keepdims=True)[:, :own_bins]


def swap(value, axis, size, distance):
    return lax.ppermute(value, axis, [(i, i ^ distance) for i in range(size)])


def swap_mixed(value, size, pair):
    return lax.ppermute(value, "ind", [(i, i ^ pair[i % 2]) for i in range(size)])


def chosen_pairs(distances):
    return list(zip(distances[:-1:2], distances[1:-1:2])), distances[-1]


def in_vmem():
    return pl.BlockSpec(memory_space=VMEM)


def in_hbm():
    return pl.BlockSpec(memory_space=pltpu.HBM)


def params(mib):
    return pltpu.CompilerParams(vmem_limit_bytes=mib * MIB)


def cost(flops, moved):
    return pl.CostEstimate(flops=flops, bytes_accessed=moved, transcendentals=0)


def shards(genotype, snp_mean, snp_scale, snp_label, probe_bits, phenotype):
    n = lax.axis_size("ind")
    n_bin = lax.axis_size("bin")
    chips = n // 2
    own_bins = BINS // n_bin
    rows, snps = genotype.shape
    tiles = -(-snps // LANES)
    block_tiles = -(-tiles // n)
    block = block_tiles * LANES
    span = block + LANES * (2 - block_tiles % 2)
    folded = block + -(-block_tiles // 4) * LANES
    whole = n * block
    mean, scale, label = snp_mean, snp_scale, snp_label
    if whole != snps:
        mean = jnp.pad(mean, (0, whole - snps), constant_values=1.0)
        scale = jnp.pad(scale, (0, whole - snps), constant_values=1.0)
        label = jnp.pad(label, (0, whole - snps), constant_values=-1)
    mean, scale, label = mean[None, :], scale[None, :], label[None, :]
    genotype, probe_bits, phenotype = [
        pltpu.with_memory_space_constraint(value, pltpu.HBM)
        for value in (genotype, probe_bits, phenotype)
    ]

    def moments(distances, given, extra, name):
        slots = len(distances)
        opening = extra[0] is probe_bits
        taken = int(not opening and extra[0] is not None)
        extra = [value for value in extra if value is not None]
        fetched = slots - taken
        out_shape = [
            jax.ShapeDtypeStruct((slots, rows, block), BF16),
            jax.ShapeDtypeStruct((slots, SUBLANES, span * 3 // 2), BF16),
            jax.ShapeDtypeStruct((slots, 2, block), F32),
        ]
        if opening:
            out_shape.append(jax.ShapeDtypeStruct((ROWS, rows), F32))
        if given is not None:
            out_shape.append(jax.ShapeDtypeStruct((rows, block), jnp.int32))
        scratch = []
        if fetched:
            scratch += [VMEM((fetched, rows, block), jnp.int32), pltpu.SemaphoreType.DMA((fetched,))]
        if given is not None:
            scratch.append(pltpu.SemaphoreType.DMA)
        if opening:
            scratch += [
                VMEM(probe_bits.shape, jnp.int32),
                VMEM((rows,), BF16),
                pltpu.SemaphoreType.DMA((2,)),
            ]
        return pl.pallas_call(
            functools.partial(moments_kernel, snps, distances, opening, taken, given),
            in_specs=[in_hbm()] + [in_hbm() if opening else in_vmem()] * len(extra),
            out_specs=[in_vmem()] * len(out_shape),
            scratch_shapes=scratch,
            out_shape=out_shape,
            cost_estimate=cost(1, 4 * rows * block * slots if slots > 1 else 1),
            compiler_params=params(20),
            name=name,
        )(genotype, *extra)

    here_order = [n - 2] + list(range(2, n - 2, 2))
    away_order = [d + 1 for d in here_order]

    def plain(kernel, operands, out_shape, name, **options):
        return pl.pallas_call(
            kernel,
            in_specs=[in_vmem()] * len(operands),
            out_specs=[in_vmem()] * len(out_shape),
            out_shape=out_shape,
            compiler_params=params(20),
            name=name,
            **options,
        )(*operands)

    kept_away, away, local_away, left, raw = moments(
        away_order, here_order[0], (probe_bits, phenotype), "moments_away"
    )
    away = swap(away, "ind", n, 1)
    kept_here, here, local_here = moments(here_order, None, (raw, left), "moments_here")
    packed = jax.ShapeDtypeStruct((SUBLANES, span * 3 // 2), BF16)
    *sums, left = plain(
        cores_kernel,
        (left, here, away),
        [packed] * (chips - 1) + [jax.ShapeDtypeStruct(left.shape, F32)],
        "cores",
    )
    sums = [swap(value, "ind", n, d) for value, d in zip(sums, here_order)]
    kept_near, near, local_near, raw = moments([1], 0, (None, left), "moments_near")
    near = swap(near, "ind", n, 1)
    kept_own, own, local_own = moments([0], None, (raw, left), "moments_own")

    u, trait = plain(
        weights_kernel,
        (mean, scale, own, near, *sums),
        [
            jax.ShapeDtypeStruct((SUBLANES, folded), BF16),
            jax.ShapeDtypeStruct((1, block), F32),
        ],
        "weights",
    )

    number_shape = jax.ShapeDtypeStruct((SUBLANES, LANES), F32)
    term_shape = [
        jax.ShapeDtypeStruct((rows, PROBES * SUBLANES), F32),
        jax.ShapeDtypeStruct((PROBES * SUBLANES, LANES), F32),
        number_shape,
    ]
    wide = PROBES * rows
    if folds(own_bins, wide):
        wide = wide * 3 // 4
    end_shape = [jax.ShapeDtypeStruct((SUBLANES, wide), BF16), number_shape]

    def fields(kept, blocks, us, terms, last=False):
        return plain(
            functools.partial(field_kernel, own_bins, blocks, len(kept), bool(terms), last),
            (mean, label, *kept, *us, *terms),
            end_shape if last else term_shape,
            "field",
            cost_estimate=cost(1, 1),
        )

    u_near = swap(u, "ind", n, 1)
    u_here = [swap(u, "ind", n, d) for d in here_order]
    terms = fields([kept_own, kept_near], [(0, 0), (0, 1)], [u, u_near], [])
    u_away = []
    for first in range(0, chips - 1, 2):
        slots = range(first, min(first + 2, chips - 1))
        values = []
        for slot in slots:
            shape = [jax.ShapeDtypeStruct(u.shape, u.dtype)]
            (value,) = plain(relay_kernel, (terms[2], u_here[slot]), shape, "relay")
            u_away.append(swap(value, "ind", n, 1))
            values.append(value)
        blocks = [(slot, here_order[slot]) for slot in slots]
        kept = [kept_here] * len(blocks)
        if len(blocks) == 1:
            blocks.append((0, away_order[0]))
            kept.append(kept_away)
            values.append(u_away[0])
        terms = fields(kept, blocks, values, terms)
    blocks = list(enumerate(away_order))[1:]
    flat, number = fields([kept_away], blocks, u_away[1:], terms, last=True)

    middle = n_bin // 2
    distances = [0] + [d for d in range(1, n_bin) if d != middle] + [middle]
    flats = [flat] + [swap(flat, "bin", n_bin, d) for d in distances[1:]]
    order = (rows, (away_order, here_order, [1], [0]))
    stats, field = plain(
        functools.partial(stats_kernel, own_bins, order),
        (flat, mean, scale, label, trait, local_away, local_here, local_near, local_own),
        [number_shape, jax.ShapeDtypeStruct((PROBES, own_bins, rows), BF16)],
        "stats",
    )
    (part,) = plain(
        functools.partial(pair_kernel, own_bins, PROBES * rows, distances),
        (stats, *flats),
        [number_shape],
        "pair",
    )
    pairs, common = chosen_pairs(list(range(2, n, 2)))
    part_common = swap(part, "ind", n, common)
    part = part + swap(part, "ind", n, 1)
    mine = [swap_mixed(part, n, pair) for pair in pairs]
    theirs = [swap(value, "ind", n, 1) for value in mine + [part_common]]
    pair, trace, quad = plain(
        functools.partial(final_kernel, own_bins, n_bin, len(pairs), rows * n),
        (number, part, part_common, *mine, *theirs),
        [
            jax.ShapeDtypeStruct((own_bins, BINS), F32),
            jax.ShapeDtypeStruct((1, own_bins), F32),
            jax.ShapeDtypeStruct((1, own_bins), F32),
        ],
        "final",
    )
    return jnp.transpose(field, (1, 0, 2)), pair, trace[0], quad[0]


def solution(mesh):
    placed = (P("ind", "bin"), P("bin"), P("bin"), P("bin"), P(None, "ind"), P("ind"))
    return jax.shard_map(
        shards,
        mesh=mesh,
        in_specs=placed,
        out_specs=(P("bin", None, "ind"), P("bin", None), P("bin"), P("bin")),
        check_vma=False,
    )
```
